32 devices in a mesh: dir: 2 (over x), dp: 16 (over z, y, core).
Axes of the slice: x: 2, y: 2, z: 4, core: 2. Of those that a mesh axis runs over, the one named last changes fastest.
Arguments:
- resid_in: bfloat16 [2, 4096, 768], P(None, 'dp'), may hold values from -6 to 6
- grad_out: bfloat16 [2, 4096, 768], P(None, 'dp'), may hold values from -6 to 6
- seq_spans: int32 [2, 32], P(None, 'dp'), may hold values from 0 to 2, as said below
- in_gain: bfloat16 [2, 768], P(None, 'dp'), may hold values from 0.099609375 to 1.8984375
- w_gate_in: bfloat16 [2, 768, 1536], P(None, 'dp'), may hold values from -0.21875 to 0.21875
- w_conv_in: bfloat16 [2, 768, 1792], P(None, 'dp'), may hold values from -0.21875 to 0.21875
- w_step: bfloat16 [2, 768, 48], P(None, 'dp'), may hold values from -0.21875 to 0.21875
- conv_weight: bfloat16 [2, 4, 1792], P(None, None, 'dp'), may hold values from -3 to 3
- conv_bias: bfloat16 [2, 1792], P(None, 'dp'), may hold values from -3 to 3
- step_bias: float32 [2, 48], replicated, may hold values from -6 to -1
- decay_log: float32 [2, 24], replicated, may hold values from -1 to 1.5
- skip_gain: float32 [2, 24], replicated, may hold values from 0.5 to 1.5
- out_gain: bfloat16 [2, 1536], P(None, 'dp'), may hold values from 0.099609375 to 1.8984375
- w_out: bfloat16 [2, 1536, 768], P(None, 'dp'), may hold values from -0.15625 to 0.15625
Outputs:
- resid_out: bfloat16 [2, 4096, 768], P(None, 'dp')
- grad_in: float32 [2, 4096, 768], P(None, 'dp')
- grad_in_gain: float32 [2, 768], P(None, 'dp')
- grad_gate_in: float32 [2, 768, 1536], P(None, 'dp')
- grad_conv_in: float32 [2, 768, 1792], P(None, 'dp')
- grad_step: float32 [2, 768, 48], P(None, 'dp')
- grad_conv_weight: float32 [2, 4, 1792], P(None, None, 'dp')
- grad_conv_bias: float32 [2, 1792], P(None, 'dp')
- grad_step_bias: float32 [2, 48], replicated
- grad_decay_log: float32 [2, 24], replicated
- grad_skip_gain: float32 [2, 24], replicated
- grad_out_gain: float32 [2, 1536], P(None, 'dp')
- grad_w_out: float32 [2, 1536, 768], P(None, 'dp')
The draws below stay inside these ranges and needn't reach their ends.
Inputs may be any that keep to these rules, and one draw needn't show every extreme that they name: `seq_spans`: A run's 2 entries are 0, 1 or 2, nonzero ones first, summing to 1 or more and 2 at most; in each micro-batch some run holds one sequence of 2 blocks.
All inputs are finite; a program needn't handle non-finite values.
Results may differ from the reference program's by a relative error of at most 0.012.
Values may be sent and summed in bfloat16 or wider, within the bound.
A program may use at most 384 MiB of HBM per device.

```python
import jax
import jax.numpy as jnp
import numpy as np
from jax import lax

D = 768
H = 24
P_SIZE = 64
N = 64
K = 4
BLOCK = 128
LAYERS = 2
MB = 2
SLOTS = 2
TOK_DEV = 256
E = 1536
CONVW = 1792
NBLOCK = 2
TOKENS = 4096
N_DP = 16


def draw_seq_spans(key, part):
    key = jax.random.fold_in(key, 11)
    key_rows, key_full = jax.random.split(key)
    patterns = jnp.array(np.array([[2, 0], [1, 1], [1, 0]], dtype=np.int32))
    picks = jax.random.randint(key_rows, (MB, N_DP), 0, 3)
    chosen = jax.random.randint(key_full, (MB,), 0, N_DP)
    picks = jnp.where(jnp.arange(N_DP)[None, :] == chosen[:, None], 0, picks)
    lengths = patterns[picks] * (NBLOCK // 2)
    return lengths.reshape(MB, N_DP * SLOTS).astype(jnp.int32)


def shard_levels(rng, dims, cuts, least, high):
    gain = 1.0
    for position, shards_of in cuts:
        draws = jax.random.uniform(jax.random.fold_in(jax.random.fold_in(rng, 6), position), (shards_of,), jnp.float32, least / len(cuts), high / len(cuts))
        gain = gain * jnp.repeat(jnp.exp(draws), dims[position] // shards_of).reshape((-1,) + (1,) * (len(dims) - 1 - position))
    return gain


def bell_draw(stream_key, extent, deviation, most, pieces=(), held_as=jnp.bfloat16):
    values = jax.random.normal(stream_key, extent, jnp.float32) * deviation
    if len(pieces) > 0:
        values = shard_levels(stream_key, extent, pieces, -0.22, 0.18) * values
    return jnp.clip(values, min=-most, max=most).astype(held_as)


def setup_inputs(seed: int = 0) -> dict:
    seeds = jax.random.split(jax.random.key(seed), 15)
    resid_in = bell_draw(seeds[0], (MB, TOKENS, D), 1.0, 6.0, ((1, 16),))
    grad_out = bell_draw(seeds[1], (MB, TOKENS, D), 1.0, 6.0, ((1, 16),))
    seq_spans = draw_seq_spans(jax.random.fold_in(seeds[14], 71), 0)
    in_gain = jnp.clip(1.0 + 0.18 * jax.random.normal(seeds[3], (LAYERS, D), jnp.float32), 0.099609375, 1.8984375).astype(jnp.bfloat16)
    w_gate_in = bell_draw(seeds[4], (LAYERS, D, E), D ** -0.5, 0.21875, ((1, 16),))
    w_conv_in = bell_draw(seeds[5], (LAYERS, D, CONVW), D ** -0.5, 0.21875, ((1, 16),))
    w_step = bell_draw(seeds[6], (LAYERS, D, 2 * H), D ** -0.5, 0.21875, ((1, 16),))
    conv_weight = bell_draw(seeds[7], (LAYERS, K, CONVW), K ** -0.5, 3.0, ((2, 16),))
    conv_bias = bell_draw(seeds[8], (LAYERS, CONVW), 0.5, 3.0, ((1, 16),))
    step_bias = jnp.clip(jax.random.uniform(seeds[9], (LAYERS, 2 * H), jnp.float32, -6.0, -1.0), -6.0, -1.0)
    decay_log = jnp.clip(jax.random.uniform(seeds[10], (LAYERS, H), jnp.float32, -1.0, 1.5), -1.0, 1.5)
    skip_gain = jnp.clip(jax.random.uniform(seeds[11], (LAYERS, H), jnp.float32, 0.5, 1.5), 0.5, 1.5)
    out_gain = jnp.clip(1.0 + 0.18 * jax.random.normal(seeds[12], (LAYERS, E), jnp.float32), 0.099609375, 1.8984375).astype(jnp.bfloat16)
    w_out = bell_draw(seeds[13], (LAYERS, E, D), E ** -0.5, 0.15625, ((1, 16),))
    return dict(resid_in=resid_in, grad_out=grad_out, seq_spans=seq_spans, in_gain=in_gain, w_gate_in=w_gate_in, w_conv_in=w_conv_in, w_step=w_step, conv_weight=conv_weight, conv_bias=conv_bias, step_bias=step_bias, decay_log=decay_log, skip_gain=skip_gain, out_gain=out_gain, w_out=w_out)


@jax.custom_vjp
def low(v):
    return lax.optimization_barrier(v.astype(jnp.bfloat16)).astype(jnp.float32)

@jax.custom_vjp
def low_back(v):
    return v

def low_keep(v):
    return (low(v), None)

def low_pass(kept, grad):
    return (grad,)

def back_keep(v):
    return (v, None)

def back_low(kept, grad):
    return (low(grad),)
low.defvjp(low_keep, low_pass)
low_back.defvjp(back_keep, back_low)

def exact_dot(left_in, right_in):
    return jnp.dot(left_in, right_in, precision=lax.Precision.HIGHEST, preferred_element_type=jnp.float32)

def seq_markers(lengths, nblocks):
    lengths = lengths.astype(jnp.int32)
    ends_cum = jnp.cumsum(lengths).astype(jnp.int32)
    begins = (ends_cum - lengths).astype(jnp.int32)
    filled = ends_cum[-1]
    block_ids = jnp.arange(nblocks, dtype=jnp.int32)
    block_open = jnp.any((begins[None, :] == block_ids[:, None]) & (lengths[None, :] > 0), axis=1) | (block_ids >= filled)
    block_close = jnp.concatenate([block_open[1:], jnp.ones((1,), bool)])
    offset = jnp.arange(BLOCK, dtype=jnp.int32)
    tok_first = (block_open[:, None] & (offset[None, :] == 0)).reshape(-1)
    tok_last = (block_close[:, None] & (offset[None, :] == BLOCK - 1)).reshape(-1)
    tok_live = jnp.repeat(block_ids < filled, BLOCK)
    open_tok = jnp.repeat(block_open, BLOCK)
    return tuple((flag.astype(jnp.float32) for flag in (block_open, block_close, tok_first, tok_last, tok_live, open_tok)))

def in_norm(residual, gain_vec):
    return residual * lax.rsqrt(lax.optimization_barrier(jnp.mean(residual * residual, axis=-1, keepdims=True)) + 1e-05) * gain_vec[None, :]

def conv_act(conv_in, conv_taps, conv_shift, markers):
    open_tok = markers[5]
    offset = jnp.arange(conv_in.shape[0], dtype=jnp.int32) % BLOCK
    summed = conv_shift[None, :] + conv_taps[0][None, :] * conv_in
    for lag_step in range(1, K):
        lagged = jnp.concatenate([jnp.zeros((lag_step, conv_in.shape[1]), conv_in.dtype), conv_in[:-lag_step]], 0)
        lag_keep = 1.0 - open_tok * (offset < lag_step).astype(open_tok.dtype)
        summed = summed + conv_taps[lag_step][None, :] * lagged * lag_keep[:, None]
    return jax.nn.silu(summed)

def block_scan(values_in, b_proj, c_proj, step_size, log_decay, block_open):
    nblocks = block_open.shape[0]
    heads_q = values_in.reshape(nblocks, BLOCK, H, P_SIZE)
    keys_q = b_proj.reshape(nblocks, BLOCK, N)
    query_q = c_proj.reshape(nblocks, BLOCK, N)
    steps_q = step_size.reshape(nblocks, BLOCK, H).transpose(0, 2, 1)
    cumulative = jnp.cumsum(log_decay.reshape(nblocks, BLOCK, H).transpose(0, 2, 1), axis=2)
    log_gap = cumulative[:, :, :, None] - cumulative[:, :, None, :]
    causal = jnp.arange(BLOCK, dtype=jnp.int32)[:, None] >= jnp.arange(BLOCK, dtype=jnp.int32)[None, :]
    decays = jnp.where(causal[None, None], jnp.exp(jnp.minimum(log_gap, 0.0)), 0.0)
    scores = jnp.einsum('cin,cjn->cij', query_q, keys_q, precision=lax.Precision.HIGHEST)
    mixing = decays * scores[:, None, :, :] * steps_q[:, :, None, :]
    within = jnp.einsum('chij,cjhp->cihp', mixing, heads_q, precision=lax.Precision.HIGHEST)
    to_end = jnp.exp(cumulative[:, :, -1:] - cumulative) * steps_q
    weighted = heads_q * to_end.transpose(0, 2, 1)[..., None]
    states = jnp.einsum('cjhp,cjn->chpn', weighted, keys_q, precision=lax.Precision.HIGHEST)
    through = jnp.exp(cumulative[:, :, -1])
    keeping = (1.0 - block_open).astype(states.dtype)

    def advance(carried, element):
        state_here, decay_here, keep_here = element
        entering = carried * keep_here
        return (entering * decay_here[:, None, None] + state_here, entering)
    _, entering = lax.scan(advance, jnp.zeros((H, P_SIZE, N), states.dtype), (states, through.astype(states.dtype), keeping))
    carried_in = jnp.einsum('cin,chpn->cihp', query_q, entering, precision=lax.Precision.HIGHEST)
    carried_in = carried_in * jnp.exp(cumulative).transpose(0, 2, 1)[..., None]
    return (within + carried_in).reshape(nblocks * BLOCK, H * P_SIZE)

def scan_dir(values_in, b_proj, c_proj, step_raw, bias_half, decay_log, block_open, tok_first):
    step_size = jax.nn.softplus(step_raw + bias_half[None, :])
    log_decay = -step_size * jnp.exp(decay_log)[None, :]
    scanned = block_scan(values_in, b_proj, c_proj, step_size, log_decay, block_open)
    shifted = jnp.concatenate([jnp.zeros((1, scanned.shape[1]), scanned.dtype), scanned[:-1]], 0)
    return shifted * (1.0 - tok_first)[:, None]

def direction(conv_out, step_raw, bias_all, decay_log, markers, which_way):
    block_open, block_close, tok_first, tok_last = markers[:4]
    inner_width = H * P_SIZE
    offset_col = inner_width + 2 * N * which_way
    values_in = conv_out[:, :inner_width]
    b_proj = conv_out[:, offset_col:offset_col + N]
    c_proj = conv_out[:, offset_col + N:offset_col + 2 * N]
    step_half = step_raw[:, H * which_way:H * which_way + H]
    bias_half = bias_all[H * which_way:H * which_way + H]
    if which_way == 0:
        return scan_dir(values_in, b_proj, c_proj, step_half, bias_half, decay_log, block_open, tok_first)
    reversed_out = scan_dir(jnp.flip(values_in, 0), jnp.flip(b_proj, 0), jnp.flip(c_proj, 0), jnp.flip(step_half, 0), bias_half, decay_log, jnp.flip(block_close, 0), jnp.flip(tok_last, 0))
    return jnp.flip(reversed_out, 0)

def post_mix(summed_y, conv_out, skip_vec, gate_pre, gain_vec):
    values_in = conv_out[:, :H * P_SIZE]
    mixed = summed_y + (values_in.reshape(-1, H, P_SIZE) * skip_vec[None, :, None]).reshape(-1, H * P_SIZE)
    gated = mixed * jax.nn.silu(gate_pre)
    scale = lax.rsqrt(lax.optimization_barrier(jnp.mean(gated * gated, axis=-1, keepdims=True)) + 1e-05)
    return gated * scale * gain_vec[None, :]

def layer_stack(params, residual, markers):
    in_gain, w_gate_in, w_conv_in, w_step, conv_weight, conv_bias, step_bias, decay_log, skip_gain, out_gain, w_out = params
    tok_live = markers[4]
    for layer_idx in range(LAYERS):
        normed = low(in_norm(residual, in_gain[layer_idx]))
        gate_pre = low_back(exact_dot(normed, w_gate_in[layer_idx]))
        conv_in = low_back(exact_dot(normed, w_conv_in[layer_idx]))
        step_raw = low_back(exact_dot(normed, w_step[layer_idx]))
        conv_out = conv_act(conv_in, conv_weight[layer_idx], conv_bias[layer_idx], markers)
        forward_y = direction(conv_out, step_raw, step_bias[layer_idx], decay_log[layer_idx], markers, 0)
        backward_y = direction(conv_out, step_raw, step_bias[layer_idx], decay_log[layer_idx], markers, 1)
        normed_out = low(post_mix(forward_y + backward_y, conv_out, skip_gain[layer_idx], gate_pre, out_gain[layer_idx]))
        branch = low_back(exact_dot(normed_out, w_out[layer_idx]))
        residual = residual + tok_live[:, None] * branch
    return residual

def reference(resid_in, grad_out, seq_spans, in_gain, w_gate_in, w_conv_in, w_step, conv_weight, conv_bias, step_bias, decay_log, skip_gain, out_gain, w_out):
    params = tuple((weight.astype(jnp.float32) for weight in (in_gain, w_gate_in, w_conv_in, w_step, conv_weight, conv_bias, step_bias, decay_log, skip_gain, out_gain, w_out)))
    inputs = resid_in.reshape(MB * N_DP, TOK_DEV, D).astype(jnp.float32)
    cotangents = grad_out.reshape(MB * N_DP, TOK_DEV, D).astype(jnp.float32)
    lengths_all = seq_spans.reshape(MB * N_DP, SLOTS).astype(jnp.int32)

    def one_run(totals, element):
        run_in, run_cot, run_lengths = element
        markers = seq_markers(run_lengths, NBLOCK)
        result, pullback = jax.vjp(lambda prm, res: layer_stack(prm, res, markers), params, run_in)
        grad_params, grad_res = pullback(run_cot)
        totals = jax.tree.map(lambda earlier, current: earlier + current.astype(earlier.dtype), totals, grad_params)
        return (totals, (result.astype(jnp.bfloat16), grad_res.astype(run_in.dtype)))
    zeros_all = jax.tree.map(jnp.zeros_like, params)
    totals, (results, grads_res) = lax.scan(one_run, zeros_all, (inputs, cotangents, lengths_all))
    resid_out = results.reshape(MB, TOKENS, D)
    grad_in = grads_res.reshape(MB, TOKENS, D)
    return (resid_out, grad_in, totals[0], totals[1], totals[2], totals[3], totals[4], totals[5], totals[6], totals[7], totals[8], totals[9], totals[10])
```

```python
import functools
import jax
import jax.numpy as jnp
from jax import lax
from jax.experimental import pallas as pl
from jax.experimental.pallas import tpu as pltpu
from jax.sharding import PartitionSpec as P

BLK = 128
HD = 64
F32 = jnp.float32
BF16 = jnp.bfloat16
HIGH = lax.Precision.HIGHEST
LANES = 128


def mm(a, b):
    return lax.dot_general(a, b, (((1,), (0,)), ((), ())), preferred_element_type=F32)


def mm_nt(a, b):
    return lax.dot_general(a, b, (((1,), (1,)), ((), ())), preferred_element_type=F32)


def mm_tn(a, b):
    return lax.dot_general(a, b, (((0,), (0,)), ((), ())), preferred_element_type=F32)


def mm_exact(a, b):
    return lax.dot_general(
        a, b, (((1,), (0,)), ((), ())), precision=HIGH, preferred_element_type=F32
    )


def iota(shape, dim):
    return lax.broadcasted_iota(jnp.int32, shape, dim)


def square_masks():
    row, col = iota((BLK, BLK), 0), iota((BLK, BLK), 1)
    return row, col


def lag_keep(keep1, lag, rows=2 * BLK):
    at = iota((rows, 1), 0)
    first = (at >= lag).astype(F32)
    edge = ((at >= BLK) & (at < BLK + lag)).astype(F32)
    return first - edge * (1.0 - keep1)


def silu(v):
    return v * jax.nn.sigmoid(v)


class Sizes:
    def __init__(self, width, inner, convw, heads):
        self.D, self.E, self.CW, self.H = width, inner, convw, heads
        self.NP = inner + convw + LANES
        self.STEP = inner + convw
        self.T = 2 * BLK


def spread_matrix(sz, base):
    row = iota((LANES, sz.E), 0)
    col = iota((LANES, sz.E), 1)
    return (row % 64 == col // HD + base).astype(BF16)


def spread(values, matrix):
    high = values.astype(BF16).astype(F32)
    low = values - high
    lane = iota(values.shape, 1)
    packed = jnp.where(lane < 64, high, pltpu.roll(low, 64, 1)).astype(BF16)
    return mm(packed, matrix)


def conv_phase(sz, cin_of, taps, bias, keep1, out_ref, slope_ref):
    keeps = [None] + [lag_keep(keep1, k) for k in range(1, 4)]

    def chunk(n, _):
        at = pl.ds(pl.multiple_of(n * LANES, LANES), LANES)
        cin = cin_of(n)
        z = bias[:, at] + taps[0:1, at] * cin
        for k in range(1, 4):
            z = z + taps[k : k + 1, at] * (pltpu.roll(cin, k, 0) * keeps[k])
        sig = jax.nn.sigmoid(z)
        act = z * sig
        out_ref[:, at] = act
        if slope_ref is not None:
            slope_ref[:, at] = sig + act * (1.0 - sig)
        return 0

    lax.fori_loop(0, sz.CW // LANES, chunk, 0)


def step_phase(sz, raw, sbias, decay):
    z = raw + sbias
    dt = jnp.maximum(z, 0.0) + jnp.log1p(jnp.exp(-jnp.abs(z)))
    a = -dt * decay
    row, col = square_masks()
    lower = (row >= col).astype(F32)
    upper = (row <= col).astype(F32)
    lane = iota((BLK, LANES), 1)
    sums = []
    for b in range(2):
        part = a[b * BLK : (b + 1) * BLK]
        down, up = mm_exact(lower, part), mm_exact(upper, part)
        sums.append(jnp.where(lane < sz.H, down, up))
    return z, dt, a, sums


def b_and_c(sz, conv_ref):
    lane = iota((sz.T, LANES), 1)
    out = []
    for way in range(2):
        pair = conv_ref[:, sz.E + way * LANES : sz.E + (way + 1) * LANES]
        bp = jnp.where(lane < 64, pair, 0.0)
        cp = jnp.where(lane < 64, pltpu.roll(pair, 64, 1), 0.0)
        cp = pltpu.roll(cp, 1 if way == 0 else sz.T - 1, 0)
        out.append((bp.astype(BF16), cp.astype(BF16)))
    return out


def blk(v, b):
    return v[b * BLK : (b + 1) * BLK]


def carry_weights(sz, dt, sums):
    end0 = jnp.exp(sums[0][BLK - 1 : BLK, :] - sums[0])
    end1 = jnp.exp(sums[1][0:1, :] - sums[1])
    lane = iota((BLK, LANES), 1)
    fwd = jnp.where(lane < sz.H, end0, 0.0)
    rev = jnp.where((lane >= sz.H) & (lane < 2 * sz.H), end1, 0.0)
    return fwd, rev


def forward_scan(sz, conv_ref, y_ref, colb, rowt, bc, dt, a, sums, keep1, spreads):
    row, col = square_masks()
    low = row > col
    (bf, cf), (bb, cb) = bc
    excl = [sums[b] - blk(a, b) for b in range(2)]
    scores = []
    for b in range(2):
        sf = mm_nt(blk(cf, b), blk(bf, b))
        sb = mm_nt(blk(cb, b), blk(bb, b))
        scores.append(jnp.where(low, sf, jnp.where(row < col, sb, 0.0)))
        rowt[0, b] = sums[b].T
        rowt[1, b] = blk(dt, b).T
        for h in range(sz.H):
            ef = jnp.broadcast_to(excl[b][:, h : h + 1], (BLK, BLK))
            eb = jnp.broadcast_to(excl[b][:, sz.H + h : sz.H + h + 1], (BLK, BLK))
            colb[0, h, b * BLK : (b + 1) * BLK] = jnp.where(low, ef, eb)
    left = iota((BLK, LANES), 1) < HD

    def pair(p, _):
        at = pl.ds(pl.multiple_of(p * LANES, LANES), LANES)
        for b in range(2):
            rows = slice(b * BLK, (b + 1) * BLK)
            x = conv_ref[rows, at].astype(BF16)
            ys = []
            for hh in range(2):
                h = 2 * p + hh
                sum_row = jnp.where(low, rowt[0, b, pl.ds(h, 1)], rowt[0, b, pl.ds(sz.H + h, 1)])
                dt_row = jnp.where(low, rowt[1, b, pl.ds(h, 1)], rowt[1, b, pl.ds(sz.H + h, 1)])
                decay = jnp.exp(jnp.minimum(colb[0, h, rows] - sum_row, 0.0))
                mix = decay * scores[b] * dt_row
                ys.append(mm(mix.astype(BF16), x))
            y_ref[rows, at] = jnp.where(left, ys[0], ys[1])
        return 0

    lax.fori_loop(0, sz.H // 2, pair, 0)
    states = carry_states(sz, conv_ref, bc, dt, sums, keep1, spreads)
    y_ref[BLK:, :] += mm(blk(cf, 1), states[0]) * spread(jnp.exp(excl[1]), spreads[0])
    y_ref[:BLK, :] += mm(blk(cb, 0), states[1]) * spread(jnp.exp(excl[0]), spreads[1])


def carry_states(sz, conv_ref, bc, dt, sums, keep1, spreads):
    (bf, _), (bb, _) = bc
    fwd, rev = carry_weights(sz, dt, sums)
    xf = conv_ref[:BLK, : sz.E] * spread(fwd * blk(dt, 0), spreads[0])
    xb = conv_ref[BLK:, : sz.E] * spread(rev * blk(dt, 1), spreads[1])
    sf = mm_tn(blk(bf, 0), xf.astype(BF16)) * keep1
    sb = mm_tn(blk(bb, 1), xb.astype(BF16)) * keep1
    return sf.astype(BF16), sb.astype(BF16)


ROWS = 16


def row_loop(sz, body, init):
    def step(n, carry):
        return body(pl.ds(pl.multiple_of(n * ROWS, ROWS), ROWS), n, carry)

    return lax.fori_loop(0, sz.T // ROWS, step, init)


def live_rows(n, live1):
    later = (n >= BLK // ROWS).astype(F32)
    return 1.0 + later * (live1 - 1.0)


def norm_in(sz, u_ref, gain, normed_ref):
    def body(at, n, _):
        u = u_ref[at, :].astype(F32)
        r = lax.rsqrt(jnp.mean(u * u, axis=-1, keepdims=True) + 1e-05)
        normed_ref[at, :] = (u * r * gain[...]).astype(BF16)
        return 0

    row_loop(sz, body, 0)


def project(sz, normed_ref, win_ref, proj_ref, cols=None):
    width = sz.NP // 9
    normed = normed_ref[...]
    for n in range(9):
        proj_ref[:, n * width : (n + 1) * width] = mm(normed, win_ref[:, n * width : (n + 1) * width])


def gate_mix(sz, at, y_ref, conv_ref, proj_ref, skipw):
    x = conv_ref[at, : sz.E]
    gate = proj_ref[at, : sz.E]
    mixed = y_ref[at, :] + x * skipw[...]
    sig = jax.nn.sigmoid(gate)
    act = gate * sig
    gated = mixed * act
    scale = lax.rsqrt(jnp.mean(gated * gated, axis=-1, keepdims=True) + 1e-05)
    return x, gate, mixed, sig, act, gated, scale


def post_mix(sz, y_ref, conv_ref, proj_ref, skipw, gain, nout_ref):
    def body(at, n, _):
        _, _, _, _, _, gated, scale = gate_mix(sz, at, y_ref, conv_ref, proj_ref, skipw)
        nout_ref[at, :] = (gated * scale * gain[...]).astype(BF16)
        return 0

    row_loop(sz, body, 0)


def forward_layer(sz, p, flags, u_ref, win_ref, wout_ref, proj_ref, y_ref, unext_ref, conv_ref,
                  normed_ref, nout_ref, colb, rowt, slope_ref=None, hook=lambda n: None):
    keep1, live1 = flags[0], flags[1]
    norm_in(sz, u_ref, p["gain_in"], normed_ref)
    hook(0)
    project(sz, normed_ref, win_ref, proj_ref)
    hook(1)
    cin_of = lambda n: proj_ref[:, pl.ds(pl.multiple_of(sz.E + n * LANES, LANES), LANES)]
    conv_phase(sz, cin_of, p["taps"], p["cbias"], keep1, conv_ref, slope_ref)
    hook(2)
    _, dt, a, sums = step_phase(sz, proj_ref[:, sz.STEP :], p["sbias"][...], p["decay"][...])
    spreads = (spread_matrix(sz, 0), spread_matrix(sz, sz.H))
    bc = b_and_c(sz, conv_ref)
    forward_scan(sz, conv_ref, y_ref, colb, rowt, bc, dt, a, sums, keep1, spreads)
    hook(3)
    post_mix(sz, y_ref, conv_ref, proj_ref, p["skipw"], p["gain_out"], nout_ref)
    hook(4)
    branch = mm(nout_ref[...], wout_ref[...])
    unext_ref[:BLK, :] = u_ref[:BLK, :].astype(F32) + branch[:BLK]
    unext_ref[BLK:, :] = u_ref[BLK:, :].astype(F32) + live1 * branch[BLK:]


def fold8(v):
    out = v[0:8]
    for n in range(1, v.shape[0] // 8):
        out = out + v[n * 8 : (n + 1) * 8]
    return out


def colsum(v):
    return jnp.sum(v, axis=0, keepdims=True)


def backward_scan(sz, conv_ref, gy_ref, gx_ref, gbc_ref, colb, rowt, accs, z, dt, a, sums, keep1,
                  spreads, decay, hook):
    row, col = square_masks()
    low = row < col
    bc = b_and_c(sz, conv_ref)
    (bf, cf), (bb, cb) = bc
    excl = [sums[b] - blk(a, b) for b in range(2)]
    scores = []
    for b in range(2):
        sf = mm_nt(blk(bf, b), blk(cf, b))
        sb = mm_nt(blk(bb, b), blk(cb, b))
        scores.append(jnp.where(low, sf, jnp.where(row > col, sb, 0.0)))
        rowt[0, b] = excl[b].T
        here = slice(b * BLK, (b + 1) * BLK)
        for h in range(sz.H):
            for n, v in ((0, sums[b]), (1, blk(dt, b))):
                vf = jnp.broadcast_to(v[:, h : h + 1], (BLK, BLK))
                vb = jnp.broadcast_to(v[:, sz.H + h : sz.H + h + 1], (BLK, BLK))
                colb[n, h, here] = jnp.where(low, vf, vb)
    gscore, rho_ref, kappa_ref = accs
    gscore[...] = jnp.zeros_like(gscore)
    kappa_ref[...] = jnp.zeros_like(kappa_ref)
    rho_ref[...] = jnp.zeros_like(rho_ref)
    lane = iota((BLK, LANES), 1)
    left = lane < HD

    def pair(p, _):
        at = pl.ds(pl.multiple_of(p * LANES, LANES), LANES)
        for b in range(2):
            rows = slice(b * BLK, (b + 1) * BLK)
            x = conv_ref[rows, at]
            gy = gy_ref[rows, at]
            x_two = jnp.concatenate([jnp.where(left, x, 0.0), jnp.where(left, 0.0, x)], axis=0)
            w_two = mm_nt(x_two.astype(BF16), gy)
            gxs = []
            gs = gscore[rows]
            kap = kappa_ref[rows]
            for hh in range(2):
                h = 2 * p + hh
                ex_row = jnp.where(low, rowt[0, b, pl.ds(h, 1)], rowt[0, b, pl.ds(sz.H + h, 1)])
                decay_m = jnp.exp(jnp.minimum(ex_row - colb[0, h, rows], 0.0))
                dtc = colb[1, h, rows]
                w = w_two[hh * BLK : (hh + 1) * BLK]
                es = decay_m * scores[b]
                gxs.append(mm((es * dtc).astype(BF16), gy))
                gs = gs + decay_m * w * dtc
                r = es * w
                q = r * dtc
                rl = jnp.where(low, r, 0.0)
                kap = jnp.where(lane == h, jnp.sum(rl, axis=1, keepdims=True), kap)
                kap = jnp.where(lane == sz.H + h, jnp.sum(r - rl, axis=1, keepdims=True), kap)
                ql = jnp.where(low, q, 0.0)
                rho_ref[b, pl.ds(h, 1)] = colsum(ql)
                rho_ref[b, pl.ds(sz.H + h, 1)] = colsum(q - ql)
            gscore[rows] = gs
            kappa_ref[rows] = kap
            gx_ref[rows, at] += jnp.where(left, gxs[0], gxs[1])
        hook(p)
        return 0

    lax.fori_loop(0, sz.H // 2, pair, 0)

    states = carry_states(sz, conv_ref, bc, dt, sums, keep1, spreads)
    ends = carry_weights(sz, dt, sums)
    values, enters = [], []
    gbs, gcs = [], []
    for way in range(2):
        src, dst = (0, 1) if way == 0 else (1, 0)
        bw, cw = bc[way]
        rows_s = slice(src * BLK, (src + 1) * BLK)
        rows_d = slice(dst * BLK, (dst + 1) * BLK)
        gcar = gy_ref[rows_d, :].astype(F32) * spread(jnp.exp(excl[dst]), spreads[way])
        gcar_low = gcar.astype(BF16)
        inner = mm(blk(cw, dst), states[way])
        enters.append(mm_nt((gcar * inner).astype(BF16), spreads[way]))
        gstate = (mm_tn(blk(cw, dst), gcar_low) * keep1).astype(BF16)
        gc_d = mm_nt(gcar_low, states[way])
        weight = spread(ends[way] * blk(dt, src), spreads[way])
        x = conv_ref[rows_s, : sz.E]
        gb_s = mm_nt((x * weight).astype(BF16), gstate)
        bg = mm(blk(bw, src), gstate)
        gx_ref[rows_s, :] += weight * bg
        values.append(mm_nt((x * bg).astype(BF16), spreads[way]))
        gb, gc = [None, None], [None, None]
        for b in range(2):
            g = gscore[b * BLK : (b + 1) * BLK]
            g = jnp.where(low if way == 0 else row > col, g, 0.0).astype(BF16)
            gb[b] = mm(g, blk(cw, b))
            gc[b] = mm_tn(g, blk(bw, b))
        gb[src] = gb[src] + gb_s
        gc[dst] = gc[dst] + gc_d
        gc_all = jnp.concatenate(gc, axis=0)
        at = iota((sz.T, 1), 0)
        if way == 0:
            gc_all = jnp.where(at == sz.T - 1, 0.0, pltpu.roll(gc_all, sz.T - 1, 0))
        else:
            gc_all = jnp.where(at == 0, 0.0, pltpu.roll(gc_all, 1, 0))
        gb_all = jnp.concatenate(gb, axis=0)
        wide_lane = iota((sz.T, LANES), 1)
        gbc_ref[:, way * LANES : (way + 1) * LANES] = jnp.where(
            wide_lane < 64, gb_all, pltpu.roll(gc_all, 64, 1)
        )

    strict_low = (row > col).astype(F32)
    strict_up = (row < col).astype(F32)
    is_f = lane < sz.H
    is_b = (lane >= sz.H) & (lane < 2 * sz.H)
    gsteps, gdecay = [], None
    for b in range(2):
        kr = kappa_ref[b * BLK : (b + 1) * BLK]
        kap = kr * blk(dt, b)
        rho = rho_ref[b].T
        if b == 1:
            rho = rho + jnp.where(is_f, enters[0], 0.0)
            zr = jnp.where(is_b, values[1], 0.0) * ends[1]
        else:
            rho = rho + jnp.where(is_b, enters[1], 0.0)
            zr = jnp.where(is_f, values[0], 0.0) * ends[0]
        zed = zr * blk(dt, b)
        diff = rho - kap
        both = jnp.concatenate([diff, zed], axis=1)
        up, down = mm_exact(strict_up, both), mm_exact(strict_low, both)
        ga = jnp.where(
            is_f, up[:, :LANES] + down[:, LANES:], down[:, :LANES] + up[:, LANES:]
        ) - kap
        ga = jnp.where(is_f | is_b, ga, 0.0)
        gdt = jnp.where(is_f | is_b, kr + zr, 0.0) - ga * decay
        gsteps.append(gdt * jax.nn.sigmoid(blk(z, b)))
        part = colsum(ga * blk(a, b))
        gdecay = part if gdecay is None else gdecay + part
    return jnp.concatenate(gsteps, axis=0), gdecay


def backward_layer(sz, p, flags, g_ref, u_ref, win_ref, wout_ref, proj_ref, y_ref, gu_ref,
                   gwin_ref, gwout_ref, small_ref, head_ref, s, hook=lambda n: None,
                   recompute=True):
    keep1, live1 = flags[0], flags[1]
    conv_ref, slope_ref = s["conv"], s["slope"]
    D, E, CW = sz.D, sz.E, sz.CW
    if recompute:
        cin_of = lambda n: proj_ref[:, pl.ds(pl.multiple_of(E + n * LANES, LANES), LANES)]
        conv_phase(sz, cin_of, p["taps"], p["cbias"], keep1, conv_ref, slope_ref)
        norm_in(sz, u_ref, p["gain_in"], s["normed"])
    hook(0)

    def mask_g(at, n, _):
        s["gb"][at, :] = (g_ref[at, :].astype(F32) * live_rows(n, live1)).astype(BF16)
        return 0

    row_loop(sz, mask_g, 0)
    s["gx"][...] = mm_nt(s["gb"][...], wout_ref[...])
    hook(1)
    s["acc"][...] = jnp.zeros_like(s["acc"])

    def post_back(at, n, _):
        x, gate, mixed, sig, act, gated, scale = gate_mix(sz, at, y_ref, conv_ref, proj_ref, p["skipw"])
        hat = gated * scale
        gn = s["gx"][at, :]
        s["acc"][0] += fold8(gn * hat)
        s["nout"][at, :] = (hat * p["gain_out"][...]).astype(BF16)
        gh = gn * p["gain_out"][...]
        gg = scale * (gh - hat * jnp.mean(gh * hat, axis=-1, keepdims=True))
        gm = gg * act
        s["gproj"][at, :E] = (gg * mixed * (sig + act * (1.0 - sig))).astype(BF16)
        s["gy"][at, :] = gm.astype(BF16)
        s["gx"][at, :] = gm * p["skipw"][...]
        s["acc"][1] += fold8(gm * x)
        return 0

    row_loop(sz, post_back, 0)
    hook(2)
    small_ref[6:7, :E] = colsum(s["acc"][0])
    gwout_ref[...] = mm_tn(s["nout"][...], s["gb"][...]).astype(BF16)
    hook(3)
    spreads = (spread_matrix(sz, 0), spread_matrix(sz, sz.H))
    z, dt, a, sums = step_phase(sz, proj_ref[:, sz.STEP :], p["sbias"][...], p["decay"][...])
    gsteps, gdecay = backward_scan(
        sz, conv_ref, s["gy"], s["gx"], s["gbc"], s["colb"], s["rowt"],
        (s["gscore"], s["rho"], s["kappa"]), z, dt, a, sums, keep1, spreads, p["decay"][...],
        lambda n: None,
    )
    hook(4)
    s["gproj"][:, sz.STEP :] = gsteps.astype(BF16)
    skip_sum = s["acc"][1]
    first = skip_sum.astype(BF16)
    rest = (skip_sum - first.astype(F32)).astype(BF16)
    gskip = colsum(mm_nt(first, spreads[0]) + mm_nt(rest, spreads[0]))
    head_ref[...] = jnp.zeros_like(head_ref)
    head_ref[0:1, :] = colsum(gsteps)
    head_ref[1:2, :] = gdecay
    head_ref[2:3, :] = gskip

    keeps = [None] + [lag_keep(keep1, k) for k in range(1, 4)]

    def conv_chunk(n, gout):
        at = pl.ds(pl.multiple_of(n * LANES, LANES), LANES)
        wide = pl.ds(pl.multiple_of(E + n * LANES, LANES), LANES)
        cin = proj_ref[:, wide]
        gz = gout * slope_ref[:, at]
        taps = p["taps"]
        gc = taps[0:1, at] * gz
        small_ref[1:2, at] = colsum(gz * cin)
        for k in range(1, 4):
            gk = gz * keeps[k]
            small_ref[1 + k : 2 + k, at] = colsum(gk * pltpu.roll(cin, k, 0))
            gc = gc + taps[k : k + 1, at] * pltpu.roll(gk, sz.T - k, 0)
        small_ref[5:6, at] = colsum(gz)
        s["gproj"][:, wide] = gc.astype(BF16)

    def x_chunk(n, _):
        conv_chunk(n, s["gx"][:, pl.ds(pl.multiple_of(n * LANES, LANES), LANES)])
        return 0

    lax.fori_loop(0, E // LANES, x_chunk, 0)
    for n in range((CW - E) // LANES):
        conv_chunk(E // LANES + n, s["gbc"][:, n * LANES : (n + 1) * LANES])
    hook(5)
    width = sz.NP // 9
    normed = s["normed"][...]
    total = None
    for n in range(9):
        cols = slice(n * width, (n + 1) * width)
        gp = s["gproj"][:, cols]
        gwin_ref[:, cols] = mm_tn(normed, gp).astype(BF16)
        part = mm_nt(gp, win_ref[:, cols])
        total = part if total is None else total + part
    s["gn"][...] = total
    hook(6)
    s["acc"][0] = jnp.zeros_like(s["acc"][0])

    def in_back(at, n, _):
        u = u_ref[at, :].astype(F32)
        r = lax.rsqrt(jnp.mean(u * u, axis=-1, keepdims=True) + 1e-05)
        hat = u * r
        gn = s["gn"][at, :]
        s["acc"][0, :, :D] += fold8(gn * hat)
        gh = gn * p["gain_in"][...]
        gu = r * (gh - hat * jnp.mean(gh * hat, axis=-1, keepdims=True))
        gu_ref[at, :] = g_ref[at, :].astype(F32) + gu
        return 0

    row_loop(sz, in_back, 0)
    small_ref[0:1, :D] = colsum(s["acc"][0, :, :D])
    hook(7)


def backward_scratch(sz):
    T, E, CW, D, H = sz.T, sz.E, sz.CW, sz.D, sz.H
    return dict(
        conv=pltpu.VMEM((T, CW), F32),
        slope=pltpu.VMEM((T, CW), F32),
        normed=pltpu.VMEM((T, D), BF16),
        gb=pltpu.VMEM((T, D), BF16),
        gx=pltpu.VMEM((T, E), F32),
        gy=pltpu.VMEM((T, E), BF16),
        nout=pltpu.VMEM((T, E), BF16),
        gproj=pltpu.VMEM((T, sz.NP), BF16),
        gbc=pltpu.VMEM((T, 2 * LANES), F32),
        gn=pltpu.VMEM((T, D), F32),
        acc=pltpu.VMEM((2, 8, E), F32),
        colb=pltpu.VMEM((2, H, T, BLK), F32),
        rowt=pltpu.VMEM((2, 2, LANES, BLK), F32),
        gscore=pltpu.VMEM((T, BLK), F32),
        rho=pltpu.VMEM((2, LANES, BLK), F32),
        kappa=pltpu.VMEM((T, LANES), F32),
    )


PARAMS = ("gain_in", "taps", "cbias", "sbias", "decay", "skipw", "gain_out")


VM = pl.BlockSpec(memory_space=pltpu.VMEM)
SM = pl.BlockSpec(memory_space=pltpu.SMEM)
ROOM = 62 << 20


def fwd_kernel(sz, flags, u, win, wout, *rest):
    p = dict(zip(PARAMS, rest[:7]))
    proj, y, unext = rest[7:10]
    conv, normed, nout, colb, rowt = rest[10:]
    forward_layer(sz, p, flags, u, win, wout, proj, y, unext, conv, normed, nout, colb, rowt)


def forward_scratch(sz):
    return [
        pltpu.VMEM((sz.T, sz.CW), F32),
        pltpu.VMEM((sz.T, sz.D), BF16),
        pltpu.VMEM((sz.T, sz.E), BF16),
        pltpu.VMEM((1, sz.H, sz.T, BLK), F32),
        pltpu.VMEM((2, 2, LANES, BLK), F32),
    ]


def fwd_call(sz, flags, u, win, wout, params):
    return pl.pallas_call(
        functools.partial(fwd_kernel, sz),
        out_shape=[
            jax.ShapeDtypeStruct((sz.T, sz.NP), F32),
            jax.ShapeDtypeStruct((sz.T, sz.E), F32),
            jax.ShapeDtypeStruct((sz.T, sz.D), F32),
        ],
        in_specs=[SM] + [VM] * 10,
        out_specs=[VM] * 3,
        scratch_shapes=forward_scratch(sz),
        compiler_params=pltpu.CompilerParams(vmem_limit_bytes=ROOM),
    )(flags, u, win, wout, *params)


def bwd_kernel(sz, names, flags, g, u, win, wout, proj, y, *rest):
    p = dict(zip(PARAMS, rest[:7]))
    gu, gwin, gwout, small, head = rest[7:12]
    s = dict(zip(names, rest[12:]))
    backward_layer(sz, p, flags, g, u, win, wout, proj, y, gu, gwin, gwout, small, head, s)


def grad_shapes(sz):
    return [
        jax.ShapeDtypeStruct((sz.T, sz.D), F32),
        jax.ShapeDtypeStruct((sz.D, sz.NP), BF16),
        jax.ShapeDtypeStruct((sz.E, sz.D), BF16),
        jax.ShapeDtypeStruct((8, sz.CW), F32),
        jax.ShapeDtypeStruct((8, LANES), F32),
    ]


def bwd_call(sz, flags, g, u, win, wout, proj, y, params):
    s = backward_scratch(sz)
    return pl.pallas_call(
        functools.partial(bwd_kernel, sz, tuple(s)),
        out_shape=grad_shapes(sz),
        in_specs=[SM] + [VM] * 13,
        out_specs=[VM] * 5,
        scratch_shapes=list(s.values()),
        compiler_params=pltpu.CompilerParams(vmem_limit_bytes=ROOM),
    )(flags, g, u, win, wout, proj, y, *params)


def run_flags(lengths):
    ends = jnp.cumsum(lengths)
    begins = ends - lengths
    opens = jnp.any((begins == 1) & (lengths > 0)) | (ends[-1] <= 1)
    return jnp.stack([1.0 - opens.astype(F32), (ends[-1] > 1).astype(F32)])


def pad_lanes(v, width=LANES):
    return jnp.pad(v, [(0, 0)] * (v.ndim - 1) + [(0, width - v.shape[-1])])


def small_pack(in_gain, conv_weight, conv_bias, out_gain):
    layers, taps = conv_weight.shape[:2]
    rows = [
        pad_lanes(in_gain),
        pad_lanes(conv_weight.reshape(layers * taps, -1)),
        pad_lanes(conv_bias),
        pad_lanes(out_gain),
    ]
    packed = jnp.concatenate(rows, axis=0)
    return jnp.pad(packed, ((0, -packed.shape[0] % 16), (0, 0)))


def small_unpack(gathered, layers, taps, sizes):
    gathered = gathered.astype(F32)

    def rows(first, count, n):
        part = gathered[:, first : first + count, :n]
        return part.transpose(1, 0, 2).reshape(count, -1)

    n_in, n_conv, n_out = sizes
    gain_in = rows(0, layers, n_in)
    taps_all = rows(layers, layers * taps, n_conv).reshape(layers, taps, -1)
    bias = rows(layers * (1 + taps), layers, n_conv)
    gain_out = rows(layers * (2 + taps), layers, n_out)
    return gain_in, taps_all, bias, gain_out


def shards(resid_in, grad_out, seq_spans, in_gain, w_gate_in, w_conv_in, w_step, conv_weight,
           conv_bias, step_bias, decay_log, skip_gain, out_gain, w_out):
    layers, taps = conv_weight.shape[:2]
    ndp = lax.axis_size("dp")
    me_dir, me = lax.axis_index("dir"), lax.axis_index("dp")
    width, inner, convw = resid_in.shape[2], w_gate_in.shape[2], w_conv_in.shape[2]
    heads = skip_gain.shape[1]
    sz = Sizes(width, inner, convw, heads)
    pick = lambda v: lax.dynamic_index_in_dim(v, me_dir, 0, keepdims=False)
    u0, g1 = pick(resid_in), pick(grad_out)
    flags = run_flags(pick(seq_spans))

    win_shard = jnp.concatenate([w_gate_in, w_conv_in, pad_lanes(w_step)], axis=2)
    packed = small_pack(in_gain, conv_weight, conv_bias, out_gain)
    sizes = (in_gain.shape[1], conv_weight.shape[2], out_gain.shape[1])
    gain_in, taps_all, bias, gain_out = small_unpack(
        lax.all_gather(packed, "dp"), layers, taps, sizes
    )
    win = [lax.all_gather(win_shard[l], "dp", axis=0, tiled=True) for l in range(layers)]
    wout = [lax.all_gather(w_out[l], "dp", axis=0, tiled=True) for l in range(layers)]
    decay = jnp.exp(decay_log)
    decay = pad_lanes(jnp.concatenate([decay, decay], axis=1))
    sbias = pad_lanes(step_bias)
    skipw = jnp.repeat(skip_gain, inner // heads, axis=1)
    params = [
        [gain_in[l][None], taps_all[l], bias[l][None], sbias[l][None], decay[l][None],
         skipw[l][None], gain_out[l][None]]
        for l in range(layers)
    ]

    u, saved = u0, []
    for l in range(layers):
        proj, y, unext = fwd_call(sz, flags, u, win[l], wout[l], params[l])
        saved.append((u, proj, y))
        u = unext
    resid = lax.all_gather(u.astype(BF16), "dir")

    g = g1
    grads = [None] * layers
    for l in reversed(range(layers)):
        u, proj, y = saved[l]
        g, gwin, gwout, small, head = bwd_call(
            sz, flags, g, u, win[l], wout[l], proj, y, params[l]
        )
        gwin = lax.psum_scatter(gwin, "dp", scatter_dimension=0, tiled=True)
        gwout = lax.psum_scatter(gwout, "dp", scatter_dimension=0, tiled=True)
        grads[l] = (gwin, gwout, small, head)
    grad_in = lax.all_gather(g, "dir")
    gwin = lax.psum(jnp.stack([v[0] for v in grads]).astype(F32), "dir")
    gwout = lax.psum(jnp.stack([v[1] for v in grads]).astype(F32), "dir")
    small, head = lax.psum(
        (jnp.stack([v[2] for v in grads]), jnp.stack([v[3] for v in grads])), ("dir", "dp")
    )

    def own(v, n):
        return lax.dynamic_slice_in_dim(v, me * n, n, axis=v.ndim - 1)

    return (
        resid,
        grad_in,
        own(small[:, 0, :width], sizes[0]),
        gwin[:, :, :inner],
        gwin[:, :, inner : inner + convw],
        gwin[:, :, inner + convw : inner + convw + 2 * heads],
        own(small[:, 1 : 1 + taps], sizes[1]),
        own(small[:, 5], sizes[1]),
        head[:, 0, : 2 * heads],
        head[:, 1, :heads] + head[:, 1, heads : 2 * heads],
        head[:, 2, :heads],
        own(small[:, 6, :inner], sizes[2]),
        gwout,
    )


def solution(mesh):
    rows, cols, last = P(None, "dp", None), P(None, "dp"), P(None, None, "dp")
    placed = (rows, rows, cols, cols, rows, rows, rows, last, cols, P(), P(), P(), cols, rows)
    out = (rows, rows, cols, rows, rows, rows, last, cols, P(), P(), P(), cols, rows)
    return jax.shard_map(shards, mesh=mesh, in_specs=placed, out_specs=out, check_vma=False)
```

```python
import functools
import jax
import jax.numpy as jnp
from jax import lax
from jax.experimental import pallas as pl
from jax.experimental.pallas import tpu as pltpu
from jax.sharding import PartitionSpec as P

BLK = 128
HD = 64
F32 = jnp.float32
BF16 = jnp.bfloat16
HIGH = lax.Precision.HIGHEST
LANES = 128


def mm(a, b):
    return lax.dot_general(a, b, (((1,), (0,)), ((), ())), preferred_element_type=F32)


def mm_nt(a, b):
    return lax.dot_general(a, b, (((1,), (1,)), ((), ())), preferred_element_type=F32)


def mm_tn(a, b):
    return lax.dot_general(a, b, (((0,), (0,)), ((), ())), preferred_element_type=F32)


def mm_exact(a, b):
    return lax.dot_general(
        a, b, (((1,), (0,)), ((), ())), precision=HIGH, preferred_element_type=F32
    )


def iota(shape, dim):
    return lax.broadcasted_iota(jnp.int32, shape, dim)


def square_masks():
    row, col = iota((BLK, BLK), 0), iota((BLK, BLK), 1)
    return row, col


def lag_keep(keep1, lag, rows=2 * BLK):
    at = iota((rows, 1), 0)
    first = (at >= lag).astype(F32)
    edge = ((at >= BLK) & (at < BLK + lag)).astype(F32)
    return first - edge * (1.0 - keep1)


def silu(v):
    return v * jax.nn.sigmoid(v)


class Sizes:
    def __init__(self, width, inner, convw, heads):
        self.D, self.E, self.CW, self.H = width, inner, convw, heads
        self.NP = inner + convw + LANES
        self.STEP = inner + convw
        self.T = 2 * BLK


def spread_matrix(sz, base):
    row = iota((LANES, sz.E), 0)
    col = iota((LANES, sz.E), 1)
    return (row % 64 == col // HD + base).astype(BF16)


def spread(values, matrix):
    high = values.astype(BF16).astype(F32)
    low = values - high
    lane = iota(values.shape, 1)
    packed = jnp.where(lane < 64, high, pltpu.roll(low, 64, 1)).astype(BF16)
    return mm(packed, matrix)


def conv_phase(sz, cin_of, taps, bias, keep1, out_ref, slope_ref):
    keeps = [None] + [lag_keep(keep1, k) for k in range(1, 4)]

    def chunk(n, _):
        at = pl.ds(pl.multiple_of(n * LANES, LANES), LANES)
        cin = cin_of(n)
        z = bias[:, at] + taps[0:1, at] * cin
        for k in range(1, 4):
            z = z + taps[k : k + 1, at] * (pltpu.roll(cin, k, 0) * keeps[k])
        sig = jax.nn.sigmoid(z)
        act = z * sig
        out_ref[:, at] = act
        if slope_ref is not None:
            slope_ref[:, at] = sig + act * (1.0 - sig)
        return 0

    lax.fori_loop(0, sz.CW // LANES, chunk, 0)


def step_phase(sz, raw, sbias, decay):
    z = raw + sbias
    dt = jnp.maximum(z, 0.0) + jnp.log1p(jnp.exp(-jnp.abs(z)))
    a = -dt * decay
    row, col = square_masks()
    lower = (row >= col).astype(F32)
    upper = (row <= col).astype(F32)
    lane = iota((BLK, LANES), 1)
    sums = []
    for b in range(2):
        part = a[b * BLK : (b + 1) * BLK]
        down, up = mm_exact(lower, part), mm_exact(upper, part)
        sums.append(jnp.where(lane < sz.H, down, up))
    return z, dt, a, sums


def b_and_c(sz, conv_ref):
    lane = iota((sz.T, LANES), 1)
    out = []
    for way in range(2):
        pair = conv_ref[:, sz.E + way * LANES : sz.E + (way + 1) * LANES]
        bp = jnp.where(lane < 64, pair, 0.0)
        cp = jnp.where(lane < 64, pltpu.roll(pair, 64, 1), 0.0)
        cp = pltpu.roll(cp, 1 if way == 0 else sz.T - 1, 0)
        out.append((bp.astype(BF16), cp.astype(BF16)))
    return out


def blk(v, b):
    return v[b * BLK : (b + 1) * BLK]


def carry_weights(sz, dt, sums):
    end0 = jnp.exp(sums[0][BLK - 1 : BLK, :] - sums[0])
    end1 = jnp.exp(sums[1][0:1, :] - sums[1])
    lane = iota((BLK, LANES), 1)
    fwd = jnp.where(lane < sz.H, end0, 0.0)
    rev = jnp.where((lane >= sz.H) & (lane < 2 * sz.H), end1, 0.0)
    return fwd, rev


def forward_scan(sz, conv_ref, y_ref, colb, rowt, bc, dt, a, sums, keep1, spreads):
    row, col = square_masks()
    low = row > col
    (bf, cf), (bb, cb) = bc
    excl = [sums[b] - blk(a, b) for b in range(2)]
    scores = []
    for b in range(2):
        sf = mm_nt(blk(cf, b), blk(bf, b))
        sb = mm_nt(blk(cb, b), blk(bb, b))
        scores.append(jnp.where(low, sf, jnp.where(row < col, sb, 0.0)))
        rowt[0, b] = sums[b].T
        rowt[1, b] = blk(dt, b).T
        for h in range(sz.H):
            ef = jnp.broadcast_to(excl[b][:, h : h + 1], (BLK, BLK))
            eb = jnp.broadcast_to(excl[b][:, sz.H + h : sz.H + h + 1], (BLK, BLK))
            colb[0, h, b * BLK : (b + 1) * BLK] = jnp.where(low, ef, eb)
    left = iota((BLK, LANES), 1) < HD

    def pair(p, _):
        at = pl.ds(pl.multiple_of(p * LANES, LANES), LANES)
        for b in range(2):
            rows = slice(b * BLK, (b + 1) * BLK)
            x = conv_ref[rows, at].astype(BF16)
            ys = []
            for hh in range(2):
                h = 2 * p + hh
                sum_row = jnp.where(low, rowt[0, b, pl.ds(h, 1)], rowt[0, b, pl.ds(sz.H + h, 1)])
                dt_row = jnp.where(low, rowt[1, b, pl.ds(h, 1)], rowt[1, b, pl.ds(sz.H + h, 1)])
                decay = jnp.exp(jnp.minimum(colb[0, h, rows] - sum_row, 0.0))
                mix = decay * scores[b] * dt_row
                ys.append(mm(mix.astype(BF16), x))
            y_ref[rows, at] = jnp.where(left, ys[0], ys[1])
        return 0

    lax.fori_loop(0, sz.H // 2, pair, 0)
    states = carry_states(sz, conv_ref, bc, dt, sums, keep1, spreads)
    y_ref[BLK:, :] += mm(blk(cf, 1), states[0]) * spread(jnp.exp(excl[1]), spreads[0])
    y_ref[:BLK, :] += mm(blk(cb, 0), states[1]) * spread(jnp.exp(excl[0]), spreads[1])


def carry_states(sz, conv_ref, bc, dt, sums, keep1, spreads):
    (bf, _), (bb, _) = bc
    fwd, rev = carry_weights(sz, dt, sums)
    xf = conv_ref[:BLK, : sz.E] * spread(fwd * blk(dt, 0), spreads[0])
    xb = conv_ref[BLK:, : sz.E] * spread(rev * blk(dt, 1), spreads[1])
    sf = mm_tn(blk(bf, 0), xf.astype(BF16)) * keep1
    sb = mm_tn(blk(bb, 1), xb.astype(BF16)) * keep1
    return sf.astype(BF16), sb.astype(BF16)


ROWS = 16


def row_loop(sz, body, init):
    def step(n, carry):
        return body(pl.ds(pl.multiple_of(n * ROWS, ROWS), ROWS), n, carry)

    return lax.fori_loop(0, sz.T // ROWS, step, init)


def live_rows(n, live1):
    later = (n >= BLK // ROWS).astype(F32)
    return 1.0 + later * (live1 - 1.0)


def norm_in(sz, u_ref, gain, normed_ref):
    def body(at, n, _):
        u = u_ref[at, :].astype(F32)
        r = lax.rsqrt(jnp.mean(u * u, axis=-1, keepdims=True) + 1e-05)
        normed_ref[at, :] = (u * r * gain[...]).astype(BF16)
        return 0

    row_loop(sz, body, 0)


def project(sz, normed_ref, win_ref, proj_ref, cols=None):
    width = sz.NP // 9
    normed = normed_ref[...]
    for n in range(9):
        proj_ref[:, n * width : (n + 1) * width] = mm(normed, win_ref[:, n * width : (n + 1) * width])


def gate_mix(sz, at, y_ref, conv_ref, proj_ref, skipw):
    x = conv_ref[at, : sz.E]
    gate = proj_ref[at, : sz.E]
    mixed = y_ref[at, :] + x * skipw[...]
    sig = jax.nn.sigmoid(gate)
    act = gate * sig
    gated = mixed * act
    scale = lax.rsqrt(jnp.mean(gated * gated, axis=-1, keepdims=True) + 1e-05)
    return x, gate, mixed, sig, act, gated, scale


def post_mix(sz, y_ref, conv_ref, proj_ref, skipw, gain, nout_ref):
    def body(at, n, _):
        _, _, _, _, _, gated, scale = gate_mix(sz, at, y_ref, conv_ref, proj_ref, skipw)
        nout_ref[at, :] = (gated * scale * gain[...]).astype(BF16)
        return 0

    row_loop(sz, body, 0)


def forward_layer(sz, p, flags, u_ref, win_ref, wout_ref, proj_ref, y_ref, unext_ref, conv_ref,
                  normed_ref, nout_ref, colb, rowt, slope_ref=None, hook=lambda n: None):
    keep1, live1 = flags[0], flags[1]
    norm_in(sz, u_ref, p["gain_in"], normed_ref)
    hook(0)
    project(sz, normed_ref, win_ref, proj_ref)
    hook(1)
    cin_of = lambda n: proj_ref[:, pl.ds(pl.multiple_of(sz.E + n * LANES, LANES), LANES)]
    conv_phase(sz, cin_of, p["taps"], p["cbias"], keep1, conv_ref, slope_ref)
    hook(2)
    _, dt, a, sums = step_phase(sz, proj_ref[:, sz.STEP :], p["sbias"][...], p["decay"][...])
    spreads = (spread_matrix(sz, 0), spread_matrix(sz, sz.H))
    bc = b_and_c(sz, conv_ref)
    forward_scan(sz, conv_ref, y_ref, colb, rowt, bc, dt, a, sums, keep1, spreads)
    hook(3)
    post_mix(sz, y_ref, conv_ref, proj_ref, p["skipw"], p["gain_out"], nout_ref)
    hook(4)
    branch = mm(nout_ref[...], wout_ref[...])
    unext_ref[:BLK, :] = u_ref[:BLK, :].astype(F32) + branch[:BLK]
    unext_ref[BLK:, :] = u_ref[BLK:, :].astype(F32) + live1 * branch[BLK:]


def fold8(v):
    out = v[0:8]
    for n in range(1, v.shape[0] // 8):
        out = out + v[n * 8 : (n + 1) * 8]
    return out


def colsum(v):
    return jnp.sum(v, axis=0, keepdims=True)


def backward_scan(sz, conv_ref, gy_ref, gx_ref, gbc_ref, colb, rowt, accs, z, dt, a, sums, keep1,
                  spreads, decay, hook):
    row, col = square_masks()
    low = row < col
    bc = b_and_c(sz, conv_ref)
    (bf, cf), (bb, cb) = bc
    excl = [sums[b] - blk(a, b) for b in range(2)]
    scores = []
    for b in range(2):
        sf = mm_nt(blk(bf, b), blk(cf, b))
        sb = mm_nt(blk(bb, b), blk(cb, b))
        scores.append(jnp.where(low, sf, jnp.where(row > col, sb, 0.0)))
        rowt[0, b] = excl[b].T
        here = slice(b * BLK, (b + 1) * BLK)
        for h in range(sz.H):
            for n, v in ((0, sums[b]), (1, blk(dt, b))):
                vf = jnp.broadcast_to(v[:, h : h + 1], (BLK, BLK))
                vb = jnp.broadcast_to(v[:, sz.H + h : sz.H + h + 1], (BLK, BLK))
                colb[n, h, here] = jnp.where(low, vf, vb)
    gscore, rho_ref, kappa_ref = accs
    gscore[...] = jnp.zeros_like(gscore)
    kappa_ref[...] = jnp.zeros_like(kappa_ref)
    rho_ref[...] = jnp.zeros_like(rho_ref)
    lane = iota((BLK, LANES), 1)
    left = lane < HD

    def pair(p, _):
        at = pl.ds(pl.multiple_of(p * LANES, LANES), LANES)
        for b in range(2):
            rows = slice(b * BLK, (b + 1) * BLK)
            x = conv_ref[rows, at]
            gy = gy_ref[rows, at]
            x_two = jnp.concatenate([jnp.where(left, x, 0.0), jnp.where(left, 0.0, x)], axis=0)
            w_two = mm_nt(x_two.astype(BF16), gy)
            gxs = []
            gs = gscore[rows]
            kap = kappa_ref[rows]
            for hh in range(2):
                h = 2 * p + hh
                ex_row = jnp.where(low, rowt[0, b, pl.ds(h, 1)], rowt[0, b, pl.ds(sz.H + h, 1)])
                decay_m = jnp.exp(jnp.minimum(ex_row - colb[0, h, rows], 0.0))
                dtc = colb[1, h, rows]
                w = w_two[hh * BLK : (hh + 1) * BLK]
                es = decay_m * scores[b]
                gxs.append(mm((es * dtc).astype(BF16), gy))
                gs = gs + decay_m * w * dtc
                r = es * w
                q = r * dtc
                rl = jnp.where(low, r, 0.0)
                kap = jnp.where(lane == h, jnp.sum(rl, axis=1, keepdims=True), kap)
                kap = jnp.where(lane == sz.H + h, jnp.sum(r - rl, axis=1, keepdims=True), kap)
                ql = jnp.where(low, q, 0.0)
                rho_ref[b, pl.ds(h, 1)] = colsum(ql)
                rho_ref[b, pl.ds(sz.H + h, 1)] = colsum(q - ql)
            gscore[rows] = gs
            kappa_ref[rows] = kap
            gx_ref[rows, at] += jnp.where(left, gxs[0], gxs[1])
        hook(p)
        return 0

    lax.fori_loop(0, sz.H // 2, pair, 0)

    states = carry_states(sz, conv_ref, bc, dt, sums, keep1, spreads)
    ends = carry_weights(sz, dt, sums)
    values, enters = [], []
    gbs, gcs = [], []
    for way in range(2):
        src, dst = (0, 1) if way == 0 else (1, 0)
        bw, cw = bc[way]
        rows_s = slice(src * BLK, (src + 1) * BLK)
        rows_d = slice(dst * BLK, (dst + 1) * BLK)
        gcar = gy_ref[rows_d, :].astype(F32) * spread(jnp.exp(excl[dst]), spreads[way])
        gcar_low = gcar.astype(BF16)
        inner = mm(blk(cw, dst), states[way])
        enters.append(mm_nt((gcar * inner).astype(BF16), spreads[way]))
        gstate = (mm_tn(blk(cw, dst), gcar_low) * keep1).astype(BF16)
        gc_d = mm_nt(gcar_low, states[way])
        weight = spread(ends[way] * blk(dt, src), spreads[way])
        x = conv_ref[rows_s, : sz.E]
        gb_s = mm_nt((x * weight).astype(BF16), gstate)
        bg = mm(blk(bw, src), gstate)
        gx_ref[rows_s, :] += weight * bg
        values.append(mm_nt((x * bg).astype(BF16), spreads[way]))
        gb, gc = [None, None], [None, None]
        for b in range(2):
            g = gscore[b * BLK : (b + 1) * BLK]
            g = jnp.where(low if way == 0 else row > col, g, 0.0).astype(BF16)
            gb[b] = mm(g, blk(cw, b))
            gc[b] = mm_tn(g, blk(bw, b))
        gb[src] = gb[src] + gb_s
        gc[dst] = gc[dst] + gc_d
        gc_all = jnp.concatenate(gc, axis=0)
        at = iota((sz.T, 1), 0)
        if way == 0:
            gc_all = jnp.where(at == sz.T - 1, 0.0, pltpu.roll(gc_all, sz.T - 1, 0))
        else:
            gc_all = jnp.where(at == 0, 0.0, pltpu.roll(gc_all, 1, 0))
        gb_all = jnp.concatenate(gb, axis=0)
        wide_lane = iota((sz.T, LANES), 1)
        gbc_ref[:, way * LANES : (way + 1) * LANES] = jnp.where(
            wide_lane < 64, gb_all, pltpu.roll(gc_all, 64, 1)
        )

    strict_low = (row > col).astype(F32)
    strict_up = (row < col).astype(F32)
    is_f = lane < sz.H
    is_b = (lane >= sz.H) & (lane < 2 * sz.H)
    gsteps, gdecay = [], None
    for b in range(2):
        kr = kappa_ref[b * BLK : (b + 1) * BLK]
        kap = kr * blk(dt, b)
        rho = rho_ref[b].T
        if b == 1:
            rho = rho + jnp.where(is_f, enters[0], 0.0)
            zr = jnp.where(is_b, values[1], 0.0) * ends[1]
        else:
            rho = rho + jnp.where(is_b, enters[1], 0.0)
            zr = jnp.where(is_f, values[0], 0.0) * ends[0]
        zed = zr * blk(dt, b)
        diff = rho - kap
        both = jnp.concatenate([diff, zed], axis=1)
        up, down = mm_exact(strict_up, both), mm_exact(strict_low, both)
        ga = jnp.where(
            is_f, up[:, :LANES] + down[:, LANES:], down[:, :LANES] + up[:, LANES:]
        ) - kap
        ga = jnp.where(is_f | is_b, ga, 0.0)
        gdt = jnp.where(is_f | is_b, kr + zr, 0.0) - ga * decay
        gsteps.append(gdt * jax.nn.sigmoid(blk(z, b)))
        part = colsum(ga * blk(a, b))
        gdecay = part if gdecay is None else gdecay + part
    return jnp.concatenate(gsteps, axis=0), gdecay


def backward_layer(sz, p, flags, g_ref, u_ref, win_ref, wout_ref, proj_ref, y_ref, gu_ref,
                   gwin_ref, gwout_ref, small_ref, head_ref, s, hook=lambda n: None,
                   recompute=True):
    keep1, live1 = flags[0], flags[1]
    conv_ref, slope_ref = s["conv"], s["slope"]
    D, E, CW = sz.D, sz.E, sz.CW
    if recompute:
        cin_of = lambda n: proj_ref[:, pl.ds(pl.multiple_of(E + n * LANES, LANES), LANES)]
        conv_phase(sz, cin_of, p["taps"], p["cbias"], keep1, conv_ref, slope_ref)
        norm_in(sz, u_ref, p["gain_in"], s["normed"])
    hook(0)

    def mask_g(at, n, _):
        s["gb"][at, :] = (g_ref[at, :].astype(F32) * live_rows(n, live1)).astype(BF16)
        return 0

    row_loop(sz, mask_g, 0)
    s["gx"][...] = mm_nt(s["gb"][...], wout_ref[...])
    hook(1)
    s["acc"][...] = jnp.zeros_like(s["acc"])

    def post_back(at, n, _):
        x, gate, mixed, sig, act, gated, scale = gate_mix(sz, at, y_ref, conv_ref, proj_ref, p["skipw"])
        hat = gated * scale
        gn = s["gx"][at, :]
        s["acc"][0] += fold8(gn * hat)
        s["nout"][at, :] = (hat * p["gain_out"][...]).astype(BF16)
        gh = gn * p["gain_out"][...]
        gg = scale * (gh - hat * jnp.mean(gh * hat, axis=-1, keepdims=True))
        gm = gg * act
        s["gproj"][at, :E] = (gg * mixed * (sig + act * (1.0 - sig))).astype(BF16)
        s["gy"][at, :] = gm.astype(BF16)
        s["gx"][at, :] = gm * p["skipw"][...]
        s["acc"][1] += fold8(gm * x)
        return 0

    row_loop(sz, post_back, 0)
    hook(2)
    small_ref[6:7, :E] = colsum(s["acc"][0])
    gwout_ref[...] = mm_tn(s["nout"][...], s["gb"][...]).astype(BF16)
    hook(3)
    spreads = (spread_matrix(sz, 0), spread_matrix(sz, sz.H))
    z, dt, a, sums = step_phase(sz, proj_ref[:, sz.STEP :], p["sbias"][...], p["decay"][...])
    gsteps, gdecay = backward_scan(
        sz, conv_ref, s["gy"], s["gx"], s["gbc"], s["colb"], s["rowt"],
        (s["gscore"], s["rho"], s["kappa"]), z, dt, a, sums, keep1, spreads, p["decay"][...],
        lambda n: None,
    )
    hook(4)
    s["gproj"][:, sz.STEP :] = gsteps.astype(BF16)
    skip_sum = s["acc"][1]
    first = skip_sum.astype(BF16)
    rest = (skip_sum - first.astype(F32)).astype(BF16)
    gskip = colsum(mm_nt(first, spreads[0]) + mm_nt(rest, spreads[0]))
    head_ref[...] = jnp.zeros_like(head_ref)
    head_ref[0:1, :] = colsum(gsteps)
    head_ref[1:2, :] = gdecay
    head_ref[2:3, :] = gskip

    keeps = [None] + [lag_keep(keep1, k) for k in range(1, 4)]

    def conv_chunk(n, gout):
        at = pl.ds(pl.multiple_of(n * LANES, LANES), LANES)
        wide = pl.ds(pl.multiple_of(E + n * LANES, LANES), LANES)
        cin = proj_ref[:, wide]
        gz = gout * slope_ref[:, at]
        taps = p["taps"]
        gc = taps[0:1, at] * gz
        small_ref[1:2, at] = colsum(gz * cin)
        for k in range(1, 4):
            gk = gz * keeps[k]
            small_ref[1 + k : 2 + k, at] = colsum(gk * pltpu.roll(cin, k, 0))
            gc = gc + taps[k : k + 1, at] * pltpu.roll(gk, sz.T - k, 0)
        small_ref[5:6, at] = colsum(gz)
        s["gproj"][:, wide] = gc.astype(BF16)

    def x_chunk(n, _):
        conv_chunk(n, s["gx"][:, pl.ds(pl.multiple_of(n * LANES, LANES), LANES)])
        return 0

    lax.fori_loop(0, E // LANES, x_chunk, 0)
    for n in range((CW - E) // LANES):
        conv_chunk(E // LANES + n, s["gbc"][:, n * LANES : (n + 1) * LANES])
    hook(5)
    width = sz.NP // 9
    normed = s["normed"][...]
    total = None
    for n in range(9):
        cols = slice(n * width, (n + 1) * width)
        gp = s["gproj"][:, cols]
        gwin_ref[:, cols] = mm_tn(normed, gp).astype(BF16)
        part = mm_nt(gp, win_ref[:, cols])
        total = part if total is None else total + part
    s["gn"][...] = total
    hook(6)
    s["acc"][0] = jnp.zeros_like(s["acc"][0])

    def in_back(at, n, _):
        u = u_ref[at, :].astype(F32)
        r = lax.rsqrt(jnp.mean(u * u, axis=-1, keepdims=True) + 1e-05)
        hat = u * r
        gn = s["gn"][at, :]
        s["acc"][0, :, :D] += fold8(gn * hat)
        gh = gn * p["gain_in"][...]
        gu = r * (gh - hat * jnp.mean(gh * hat, axis=-1, keepdims=True))
        gu_ref[at, :] = g_ref[at, :].astype(F32) + gu
        return 0

    row_loop(sz, in_back, 0)
    small_ref[0:1, :D] = colsum(s["acc"][0, :, :D])
    hook(7)


def backward_scratch(sz):
    T, E, CW, D, H = sz.T, sz.E, sz.CW, sz.D, sz.H
    return dict(
        conv=pltpu.VMEM((T, CW), F32),
        slope=pltpu.VMEM((T, CW), F32),
        normed=pltpu.VMEM((T, D), BF16),
        gb=pltpu.VMEM((T, D), BF16),
        gx=pltpu.VMEM((T, E), F32),
        gy=pltpu.VMEM((T, E), BF16),
        nout=pltpu.VMEM((T, E), BF16),
        gproj=pltpu.VMEM((T, sz.NP), BF16),
        gbc=pltpu.VMEM((T, 2 * LANES), F32),
        gn=pltpu.VMEM((T, D), F32),
        acc=pltpu.VMEM((2, 8, E), F32),
        colb=pltpu.VMEM((2, H, T, BLK), F32),
        rowt=pltpu.VMEM((2, 2, LANES, BLK), F32),
        gscore=pltpu.VMEM((T, BLK), F32),
        rho=pltpu.VMEM((2, LANES, BLK), F32),
        kappa=pltpu.VMEM((T, LANES), F32),
    )


PARAMS = ("gain_in", "taps", "cbias", "sbias", "decay", "skipw", "gain_out")


MESH = pl.DeviceIdType.MESH


def remote(src, dst, ssem, rsem, device):
    return pltpu.make_async_remote_copy(
        src, dst, ssem, rsem, device_id=device, device_id_type=MESH
    )


class Ring:
    def __init__(self, ndp, both_ways=True):
        nc = ndp // 2
        self.nc, self.ndp = nc, ndp
        self.plus = nc // 2 if both_ways else nc - 1
        self.minus = nc - 1 - self.plus
        self.d, self.me = lax.axis_index("dir"), lax.axis_index("dp")
        p, self.c = self.me // 2, self.me % 2
        odd = p % 2
        self.pos = (1 - odd) * (p // 2) + odd * (nc - 1 - p // 2)
        self.turn = 1 - 2 * self.c
        self.nxt = (self.d, 2 * self.chip(1) + self.c)
        self.prv = (self.d, 2 * self.chip(-1) + self.c)
        self.sib = (self.d, 2 * p + 1 - self.c)
        self.mate = (1 - self.d, self.me)

    def chip(self, ahead):
        nc = self.nc
        pos = (self.pos + ahead * self.turn + nc) % nc
        half = pos // (nc // 2)
        return (1 - half) * 2 * pos + half * (2 * (nc - 1 - pos) + 1)

    def flip(self, bit):
        return (self.d, self.me + (1 - 2 * ((self.me // bit) % 2)) * bit)

    def flips(self):
        return [self.flip(1 << n) for n in range(self.ndp.bit_length() - 1)]

    def barrier(self, more=()):
        bar = pltpu.get_barrier_semaphore()
        greeted = (self.nxt, self.prv, self.sib, self.mate) + tuple(more)
        for device in greeted:
            pl.semaphore_signal(bar, inc=1, device_id=device, device_id_type=MESH)
        pl.semaphore_wait(bar, len(greeted))

    def hops(self):
        out = []
        for s in range(1, self.plus + 1):
            out.append((1, s))
            if s <= self.minus:
                out.append((-1, s))
        return out

    def index(self, sign, hop):
        return hop if sign > 0 else self.plus + hop


def cols(start, width):
    if isinstance(start, int):
        return pl.ds(start, width)
    return pl.ds(pl.multiple_of(start, LANES), width)


def rows_at(slot, count):
    return pl.ds(pl.multiple_of(slot * count, 16), count)


class Gather:
    def __init__(self, ring, groups, parts, sems):
        self.r, self.g, self.parts = ring, groups, parts
        self.arrive, self.beside, self.along, self.aside, self.across = sems[:5]
        self.local = sems[5]

    @staticmethod
    def scratch(ndp, groups):
        return [pltpu.SemaphoreType.DMA((3 * groups, ndp // 2))] * 5 + [
            pltpu.SemaphoreType.DMA((groups,))
        ]

    def view(self, g, ref, slot, k):
        rows = self.g[g][0].shape[0]
        w, w2 = self.parts[g]
        at = cols(2 * w, w2) if k == 1 else cols((self.r.d if k == 0 else 1 - self.r.d) * w, w)
        return ref.at[:, at] if slot is None else ref.at[rows_at(slot, rows), at]

    def copies(self, g, k, sign, hop):
        r, (src, dst) = self.r, self.g[g]
        m, n = 3 * g + k, (0 if hop == 0 else r.index(sign, hop))
        here = self.view(g, dst, 2 * r.chip(-sign * hop) + r.c, k)
        frm = self.view(g, src, None, k) if hop == 0 else here
        out = []
        if k < 2:
            for way, limit, device in ((1, r.plus, r.nxt), (-1, r.minus, r.prv)):
                if (hop == 0 or way == sign) and hop < limit:
                    to = r.index(way, hop + 1)
                    out.append(remote(frm, here, self.along.at[m, to], self.arrive.at[m, to], device))
        if k == 0 and hop > 0:
            out.append(
                remote(frm, here, self.across.at[m, n], self.arrive.at[m + 2, n], r.mate)
            )
        out.append(remote(frm, here, self.aside.at[m, n], self.beside.at[m, n], r.sib))
        return here, out

    def own(self, g):
        src, dst = self.g[g]
        return pltpu.make_async_copy(
            src, dst.at[rows_at(self.r.me, src.shape[0])], self.local.at[g]
        )

    def event(self, g, k, sign, hop):
        here, out = self.copies(g, k, sign, hop)
        if hop > 0:
            m, n = 3 * g + k, self.r.index(sign, hop)
            remote(here, here, self.along.at[m, n], self.arrive.at[m, n], self.r.nxt).wait_recv()
        for copy in out:
            copy.start()

    def kinds(self, g):
        return (0, 1, 2) if self.parts[g][0] else (1,)

    def begin(self, groups):
        for g in groups:
            for k in self.kinds(g):
                self.event(g, k, 1, 0)
            self.own(g).start()

    def schedule(self, groups):
        order, late = [], []
        for sign, hop in self.r.hops():
            now = [(self.event, (g, k, sign, hop)) for g in groups for k in self.kinds(g) if k < 2]
            order += now + late
            late = [(self.event, (g, 2, sign, hop)) for g in groups if 2 in self.kinds(g)]
        return order + late

    def finish(self, groups):
        r = self.r
        for g in groups:
            src, dst = self.g[g]
            for k in self.kinds(g):
                for sign, hop in [(1, 0)] + r.hops():
                    m, n = 3 * g + k, (0 if hop == 0 else r.index(sign, hop))
                    there = self.view(g, dst, 2 * r.chip(sign * hop) + 1 - r.c, k)
                    remote(
                        there, there, self.aside.at[m, n], self.beside.at[m, n], r.sib
                    ).wait_recv()
            self.own(g).wait()

    def drain(self, groups):
        for g in groups:
            for k in self.kinds(g):
                for sign, hop in [(1, 0)] + self.r.hops():
                    for copy in self.copies(g, k, sign, hop)[1]:
                        copy.wait_send()


class Scatter:
    def __init__(self, ring, groups, parts, bufs, sems):
        self.r, self.g, self.parts, self.bufs = ring, groups, parts, bufs
        (self.s_sib, self.r_sib, self.s_mate, self.r_mate, self.s_ring, self.r_ring,
         self.s_end, self.r_end) = sems

    @staticmethod
    def scratch(ndp, shapes, parts):
        nc = ndp // 2
        bufs = []
        for (rows, width), (w, w2) in zip(shapes, parts):
            bufs += [
                pltpu.VMEM((nc, rows, width), BF16),
                pltpu.VMEM((nc, rows, w), BF16),
                pltpu.VMEM((nc + 1, rows, w + w2), BF16),
                pltpu.VMEM((2, rows, w + w2), BF16),
            ]
        n = len(shapes)
        sems = [pltpu.SemaphoreType.DMA((n, nc))] * 4 + [
            pltpu.SemaphoreType.DMA((2 * n, nc + 1))
        ] * 2 + [pltpu.SemaphoreType.DMA((n,))] * 2
        return bufs, sems

    def buf(self, g):
        return self.bufs[4 * g : 4 * g + 4]

    def span(self, g, k):
        w, w2 = self.parts[g]
        if k == 1:
            return cols(2 * w, w2)
        return cols((self.r.d if k == 0 else 1 - self.r.d) * w, w)

    def packed(self, g, k):
        w, w2 = self.parts[g]
        return pl.ds(0, w) if k == 0 else pl.ds(w, w2)

    def order(self):
        r, out = self.r, []
        for s in range(r.plus):
            out.append(r.plus - s)
            if s < r.minus:
                out.append(-(r.minus - s))
        return out + [0]

    def number(self, ahead):
        return ahead % self.r.nc

    def sib_copy(self, g, ahead):
        r, own, n = self.r, self.g[g], self.number(ahead)
        sib = self.buf(g)[0]
        rows = sib.shape[1]
        src = own.at[rows_at(2 * r.chip(-ahead) + 1 - r.c, rows)]
        return remote(src, sib.at[n], self.s_sib.at[g, n], self.r_sib.at[g, n], r.sib)

    def mate_copy(self, g, ahead):
        r, n = self.r, self.number(ahead)
        sib, mate = self.buf(g)[:2]
        src = sib.at[n, :, self.span(g, 2)]
        return remote(src, mate.at[n], self.s_mate.at[g, n], self.r_mate.at[g, n], r.mate)

    def ring_copy(self, g, k, sign, step):
        r = self.r
        run = self.buf(g)[2]
        frm = run.at[self.slot(sign, step), :, self.packed(g, k)]
        to = run.at[self.slot(sign, step + 1), :, self.packed(g, k)]
        n = self.slot(sign, step + 1)
        device = r.nxt if sign > 0 else r.prv
        return remote(
            frm, to, self.s_ring.at[2 * g + k, n], self.r_ring.at[2 * g + k, n], device
        )

    def slot(self, sign, step):
        return step if sign > 0 else self.r.plus + 1 + step

    def begin(self, groups):
        for g in groups:
            for ahead in self.order():
                self.sib_copy(g, ahead).start()

    def hand_over(self, g, ahead):
        r, own, n = self.r, self.g[g], self.number(ahead)
        sib = self.buf(g)[0]
        rows = sib.shape[1]
        self.sib_copy(g, ahead).wait_recv()
        first = (2 * r.chip(ahead) + r.c) * rows
        at = self.span(g, 2)

        def part(n16, _):
            inner = pl.ds(pl.multiple_of(n16 * 16, 16), 16)
            outer = pl.ds(pl.multiple_of(first + n16 * 16, 16), 16)
            sib[n, inner, at] = (own[outer, at].astype(F32) + sib[n, inner, at].astype(F32)).astype(BF16)
            return 0

        lax.fori_loop(0, rows // 16, part, 0)
        self.mate_copy(g, ahead).start()

    def step(self, g, k, sign, step):
        r, own = self.r, self.g[g]
        sib, mate, run, end = self.buf(g)
        rows = sib.shape[1]
        last = r.plus if sign > 0 else r.minus
        ahead = sign * (last - step)
        n = self.number(ahead)
        if k == 0:
            self.mate_copy(g, ahead).wait_recv()
        if step > 0:
            self.ring_copy(g, k, sign, step - 1).wait_recv()
        first = (2 * r.chip(ahead) + r.c) * rows
        at, mine = self.span(g, k), self.packed(g, k)
        here = self.slot(sign, step)

        def part(n16, _):
            inner = pl.ds(pl.multiple_of(n16 * 16, 16), 16)
            outer = pl.ds(pl.multiple_of(first + n16 * 16, 16), 16)
            total = own[outer, at].astype(F32) + sib[n, inner, at].astype(F32)
            if k == 0:
                total = total + mate[n, inner, :].astype(F32)
            if step > 0:
                total = total + run[here, inner, mine].astype(F32)
            run[here, inner, mine] = total.astype(BF16)
            return 0

        lax.fori_loop(0, rows // 16, part, 0)
        self.ring_copy(g, k, sign, step).start()

    def own_sum(self, g):
        r, own = self.r, self.g[g]
        sib, mate, run, end = self.buf(g)
        rows = sib.shape[1]
        self.mate_copy(g, 0).wait_recv()
        for k in range(2):
            self.ring_copy(g, k, 1, r.plus - 1).wait_recv()
            self.ring_copy(g, k, -1, r.minus - 1).wait_recv()
        first = (2 * r.chip(0) + r.c) * rows

        def part(n16, _):
            inner = pl.ds(pl.multiple_of(n16 * 16, 16), 16)
            outer = pl.ds(pl.multiple_of(first + n16 * 16, 16), 16)
            for k in range(2):
                at, mine = self.span(g, k), self.packed(g, k)
                total = own[outer, at].astype(F32) + sib[0, inner, at].astype(F32)
                if k == 0:
                    total = total + mate[0, inner, :].astype(F32)
                total = total + run[self.slot(1, r.plus), inner, mine].astype(F32)
                total = total + run[self.slot(-1, r.minus), inner, mine].astype(F32)
                end[0, inner, mine] = total.astype(BF16)
            return 0

        lax.fori_loop(0, rows // 16, part, 0)
        self.end_copy(g).start()

    def end_copy(self, g):
        end = self.buf(g)[3]
        return remote(end.at[0], end.at[1], self.s_end.at[g], self.r_end.at[g], self.r.mate)

    def result(self, g, out):
        end = self.buf(g)[3]
        rows = end.shape[1]
        self.end_copy(g).wait_recv()

        def part(n16, _):
            inner = pl.ds(pl.multiple_of(n16 * 16, 16), 16)
            mine0, mine1 = self.packed(g, 0), self.packed(g, 1)
            out[inner, self.span(g, 0)] = end[0, inner, mine0].astype(F32)
            out[inner, self.span(g, 2)] = end[1, inner, mine0].astype(F32)
            out[inner, self.span(g, 1)] = end[0, inner, mine1].astype(F32) + end[1, inner, mine1].astype(F32)
            return 0

        lax.fori_loop(0, rows // 16, part, 0)

    def schedule(self, groups):
        r, calls = self.r, []
        over = [[(self.hand_over, (g, ahead)) for g in groups] for ahead in self.order()]

        def hand(count):
            for _ in range(min(count, len(over))):
                calls.extend(over.pop(0))

        hand(4)
        for s in range(r.plus):
            for sign in (1, -1) if s < r.minus else (1,):
                calls.extend((self.step, (g, k, sign, s)) for g in groups for k in (1, 0))
            hand(2)
        hand(len(over))
        calls.extend((self.own_sum, (g,)) for g in groups)
        return calls

    def drain(self, groups):
        r = self.r
        for g in groups:
            for ahead in self.order():
                self.sib_copy(g, ahead).wait_send()
                self.mate_copy(g, ahead).wait_send()
            for k in range(2):
                for s in range(r.plus):
                    self.ring_copy(g, k, 1, s).wait_send()
                for s in range(r.minus):
                    self.ring_copy(g, k, -1, s).wait_send()
            self.end_copy(g).wait_send()


class AllSum:
    @staticmethod
    def scratch(ndp, shape):
        n = ndp.bit_length()
        return [pltpu.VMEM((n,) + shape, F32), pltpu.SemaphoreType.DMA((n,)), pltpu.SemaphoreType.DMA((n,))]

    def __init__(self, ring, acc, bufs):
        self.acc, (self.buf, self.s, self.r) = acc, bufs
        self.partners = [ring.mate] + ring.flips()

    def copy(self, n):
        return remote(self.acc, self.buf.at[n], self.s.at[n], self.r.at[n], self.partners[n])

    def start(self, n):
        self.copy(n).start()

    def end(self, n):
        self.copy(n).wait()
        self.acc[...] += self.buf[n]

    def schedule(self):
        calls = [(self.start, (0,))]
        for n in range(len(self.partners)):
            calls.append((self.end, (n,)))
            if n + 1 < len(self.partners):
                calls.append((self.start, (n + 1,)))
        return calls


VM = pl.BlockSpec(memory_space=pltpu.VMEM)
SM = pl.BlockSpec(memory_space=pltpu.SMEM)
ANY = pl.BlockSpec(memory_space=pl.ANY)
ROOM = 62 << 20
TABLE_ROWS = 16


def table_params(sz, tab):
    return dict(
        gain_in=tab.at[0:1, : sz.D],
        taps=tab.at[1:5],
        cbias=tab.at[5:6],
        gain_out=tab.at[6:7, : sz.E],
        sbias=tab.at[7:8, :LANES],
        decay=tab.at[8:9, :LANES],
        skipw=tab.at[9:10, : sz.E],
    )


def run_flags(spans, d):
    begin, opens = jnp.int32(0), jnp.int32(0)
    for s in range(spans.shape[1]):
        length = spans[d, s]
        starts = jnp.where(begin == 1, 1, 0) * jnp.where(length > 0, 1, 0)
        opens = jnp.maximum(opens, starts)
        begin = begin + length
    live = jnp.where(begin > 1, 1.0, 0.0).astype(F32)
    opened = jnp.maximum(opens.astype(F32), 1.0 - live)
    return 1.0 - opened, live


class Plan:
    def __init__(self, layers, taps, ndp, sz, n_in, n_conv, n_out):
        self.L, self.K, self.ndp, self.sz = layers, taps, ndp, sz
        self.n_in, self.n_conv, self.n_out = n_in, n_conv, n_out
        tiles_in, tiles_out = sz.NP // LANES, sz.D // LANES
        third_in, third_out = tiles_in // 3 * LANES, tiles_out // 3 * LANES
        self.ag_in = (third_in, sz.NP - 2 * third_in)
        self.ag_out = (third_out, sz.D - 2 * third_out)
        part_in, part_out = tiles_in * 2 // 9 * LANES, tiles_out // 6 * LANES
        self.rs_in = (part_in, sz.NP - 2 * part_in)
        self.rs_out = (part_out, sz.D - 2 * part_out)


def stage_own(pl_, ins, stage, smallf, small, sems):
    sz = pl_.sz
    w_gate, w_conv, w_step, in_gain, conv_weight, conv_bias, out_gain = ins
    copies = []
    for l in range(pl_.L):
        copies.append(
            pltpu.make_async_copy(w_gate.at[l], stage.at[l, :, pl.ds(0, sz.E)], sems.at[2 * l])
        )
        copies.append(
            pltpu.make_async_copy(
                w_conv.at[l], stage.at[l, :, pl.ds(sz.E, sz.CW)], sems.at[2 * l + 1]
            )
        )
    for copy in copies:
        copy.start()
    smallf[...] = jnp.zeros_like(smallf)
    L, K = pl_.L, pl_.K
    smallf[0:L, : pl_.n_in] = in_gain[...].astype(F32)
    for l in range(L):
        smallf[L + l * K : L + (l + 1) * K, : pl_.n_conv] = conv_weight[l].astype(F32)
    smallf[L + L * K : 2 * L + L * K, : pl_.n_conv] = conv_bias[...].astype(F32)
    smallf[2 * L + L * K : 3 * L + L * K, : pl_.n_out] = out_gain[...].astype(F32)
    small[...] = smallf[...].astype(BF16)
    for l in range(L):
        stage[l, :, sz.STEP :] = jnp.zeros((stage.shape[1], LANES), BF16)
        stage[l, :, sz.STEP : sz.STEP + 2 * sz.H] = w_step[l]
    for copy in copies:
        copy.wait()


def fill_table(pl_, table, gathered, step_bias, decay_log, skip_gain):
    sz, L, K = pl_.sz, pl_.L, pl_.K
    table[...] = jnp.zeros_like(table)
    rows = gathered.shape[0] // pl_.ndp
    for q in range(pl_.ndp):
        part = gathered[q * rows : (q + 1) * rows, :].astype(F32)
        for l in range(L):
            table[l, 0:1, q * pl_.n_in : (q + 1) * pl_.n_in] = part[l : l + 1, : pl_.n_in]
            conv = slice(q * pl_.n_conv, (q + 1) * pl_.n_conv)
            table[l, 1 : 1 + K, conv] = part[L + l * K : L + (l + 1) * K, : pl_.n_conv]
            at = L + L * K + l
            table[l, 5:6, conv] = part[at : at + 1, : pl_.n_conv]
            out = slice(q * pl_.n_out, (q + 1) * pl_.n_out)
            table[l, 6:7, out] = part[at + L : at + L + 1, : pl_.n_out]
    head_of = iota((sz.H, sz.E), 1) // HD
    one_hot = (iota((sz.H, sz.E), 0) == head_of).astype(F32)
    wide = mm_exact(skip_gain[...], one_hot)
    decay = jnp.exp(decay_log[...])
    for l in range(L):
        table[l, 7:8, : 2 * sz.H] = step_bias[l : l + 1, :]
        table[l, 8:9, : sz.H] = decay[l : l + 1]
        table[l, 8:9, sz.H : 2 * sz.H] = decay[l : l + 1]
        table[l, 9:10, : sz.E] = wide[l : l + 1]


def gather_kernel(pl_, *refs):
    L = pl_.L
    (w_gate, w_conv, w_step, in_gain, conv_weight, conv_bias, out_gain, w_out,
     step_bias, decay_log, skip_gain) = refs[:11]
    fulls = refs[11 : 11 + 2 * L]
    table = refs[11 + 2 * L]
    stage, smallf, small, gathered, own_sems = refs[12 + 2 * L : 17 + 2 * L]
    sems = refs[17 + 2 * L :]
    ring = Ring(pl_.ndp)
    ring.barrier()
    stage_own(pl_, (w_gate, w_conv, w_step, in_gain, conv_weight, conv_bias, out_gain),
              stage, smallf, small, own_sems)
    groups, parts = [(small, gathered)], [(0, LANES)]
    for l in range(L):
        groups += [(stage.at[l], fulls[2 * l]), (w_out.at[l], fulls[2 * l + 1])]
        parts += [pl_.ag_in, pl_.ag_out]
    gather = Gather(ring, groups, parts, sems)
    everything = range(len(groups))
    gather.begin(everything)
    for call, args in gather.schedule(everything):
        call(*args)
    gather.finish([0])
    fill_table(pl_, table, gathered, step_bias, decay_log, skip_gain)
    gather.finish(everything[1:])
    gather.drain(everything)


def gather_call(pl_, w_gate, w_conv, w_step, in_gain, conv_weight, conv_bias, out_gain, w_out,
                step_bias, decay_log, skip_gain):
    sz, L = pl_.sz, pl_.L
    full = [jax.ShapeDtypeStruct((sz.D, sz.NP), BF16), jax.ShapeDtypeStruct((sz.E, sz.D), BF16)] * L
    return pl.pallas_call(
        functools.partial(gather_kernel, pl_),
        out_shape=full + [jax.ShapeDtypeStruct((L, TABLE_ROWS, sz.CW), F32)],
        in_specs=[ANY, ANY] + [VM] * 5 + [ANY] + [VM] * 3,
        out_specs=[ANY] * (2 * L) + [VM],
        scratch_shapes=[
            pltpu.VMEM((L, w_gate.shape[1], sz.NP), BF16),
            pltpu.VMEM((16, LANES), F32),
            pltpu.VMEM((16, LANES), BF16),
            pltpu.VMEM((16 * pl_.ndp, LANES), BF16),
            pltpu.SemaphoreType.DMA((2 * L,)),
        ] + Gather.scratch(pl_.ndp, 1 + 2 * L),
        compiler_params=pltpu.CompilerParams(
            collective_id=1, has_side_effects=True, vmem_limit_bytes=ROOM
        ),
    )(w_gate, w_conv, w_step, in_gain, conv_weight, conv_bias, out_gain, w_out,
      step_bias, decay_log, skip_gain)


def fwd_kernel(sz, layer, spans, u, win, wout, table, proj, y, unext, conv, normed, nout, colb, rowt):
    d = lax.axis_index("dir")
    flags = run_flags(spans, d)
    forward_layer(sz, table_params(sz, table.at[layer]), flags, u.at[d] if layer == 0 else u,
                  win, wout, proj, y, unext, conv, normed, nout, colb, rowt)


def forward_scratch(sz):
    return [
        pltpu.VMEM((sz.T, sz.CW), F32),
        pltpu.VMEM((sz.T, sz.D), BF16),
        pltpu.VMEM((sz.T, sz.E), BF16),
        pltpu.VMEM((1, sz.H, sz.T, BLK), F32),
        pltpu.VMEM((2, 2, LANES, BLK), F32),
    ]


def saved_shapes(sz):
    return [
        jax.ShapeDtypeStruct((sz.T, sz.NP), F32),
        jax.ShapeDtypeStruct((sz.T, sz.E), F32),
        jax.ShapeDtypeStruct((sz.T, sz.D), F32),
    ]


def fwd_call(sz, layer, spans, u, win, wout, table):
    return pl.pallas_call(
        functools.partial(fwd_kernel, sz, layer),
        out_shape=saved_shapes(sz),
        in_specs=[SM] + [VM] * 4,
        out_specs=[VM] * 3,
        scratch_shapes=forward_scratch(sz),
        compiler_params=pltpu.CompilerParams(vmem_limit_bytes=ROOM),
    )(spans, u, win, wout, table)


def bwd_kernel(sz, layer, last, names, spans, g, u, win, wout, proj, y, table, gu, gwin, gwout,
               small, head, *rest):
    d = lax.axis_index("dir")
    flags = run_flags(spans, d)
    backward_layer(sz, table_params(sz, table.at[layer]), flags, g.at[d] if last else g,
                   u.at[d] if layer == 0 else u, win, wout, proj, y, gu, gwin, gwout, small, head,
                   dict(zip(names, rest)))


def grad_shapes(sz):
    return [
        jax.ShapeDtypeStruct((sz.T, sz.D), F32),
        jax.ShapeDtypeStruct((sz.D, sz.NP), BF16),
        jax.ShapeDtypeStruct((sz.E, sz.D), BF16),
        jax.ShapeDtypeStruct((8, sz.CW), F32),
        jax.ShapeDtypeStruct((8, LANES), F32),
    ]


def bwd_call(sz, layer, last, spans, g, u, win, wout, proj, y, table):
    s = backward_scratch(sz)
    return pl.pallas_call(
        functools.partial(bwd_kernel, sz, layer, last, tuple(s)),
        out_shape=grad_shapes(sz),
        in_specs=[SM] + [VM] * 7,
        out_specs=[VM] * 5,
        scratch_shapes=list(s.values()),
        compiler_params=pltpu.CompilerParams(vmem_limit_bytes=ROOM),
    )(spans, g, u, win, wout, proj, y, table)


class Exchange:
    def __init__(self, ring, value, buf, sems, n):
        self.r, self.buf = ring, buf
        buf[0] = value[...].astype(BF16)
        self.copy = remote(buf.at[0], buf.at[1], sems.at[0, n], sems.at[1, n], ring.mate)
        self.copy.start()

    def result(self, out):
        self.copy.wait()
        out[self.r.d] = self.buf[0].astype(out.dtype)
        out[1 - self.r.d] = self.buf[1].astype(out.dtype)


def own_small(pl_, acc, picks, outs, me):
    L, K = pl_.L, pl_.K
    for q in range(pl_.ndp):
        for n, count in enumerate((pl_.n_in, pl_.n_conv, pl_.n_out)):
            picks[q, n, :, :count] = acc[:, q * count : (q + 1) * count]
    p_in, p_conv, p_out = picks[me, 0], picks[me, 1], picks[me, 2]
    g_in, g_taps, g_bias, g_out = outs
    for l in range(L):
        r = 8 * l
        g_in[l : l + 1, :] = p_in[r : r + 1, : pl_.n_in]
        g_taps[l] = p_conv[r + 1 : r + 1 + K, : pl_.n_conv]
        g_bias[l : l + 1, :] = p_conv[r + 5 : r + 6, : pl_.n_conv]
        g_out[l : l + 1, :] = p_out[r + 6 : r + 7, : pl_.n_out]


def head_grads(pl_, acc, g_bias, g_decay, g_skip):
    sz = pl_.sz
    for l in range(pl_.L):
        r = 8 * l
        part = acc[r : r + 8, sz.CW :]
        g_bias[l : l + 1, :] = part[0:1, : 2 * sz.H]
        g_decay[l : l + 1, :] = part[1:2, : sz.H] + part[1:2, sz.H : 2 * sz.H]
        g_skip[l : l + 1, :] = part[2:3, : sz.H]


def weave(main, side):
    out, done = [], 0
    for n, call in enumerate(main):
        out.append(call)
        upto = (n + 1) * len(side) // max(len(main), 1)
        out += side[done:upto]
        done = upto
    return out + side[done:]


def scatter_kernel(pl_, nbuf, *refs):
    sz, L = pl_.sz, pl_.L
    u, g = refs[0], refs[1]
    grads = refs[2 : 2 + 2 * L]
    smalls = refs[2 + 2 * L : 2 + 3 * L]
    heads = refs[2 + 3 * L : 2 + 4 * L]
    rest = refs[2 + 4 * L :]
    (resid, grad_in, g_in, g_gate, g_conv, g_step, g_taps, g_cbias, g_sbias, g_decay, g_skip,
     g_gout, g_out) = rest[:13]
    acc, picks, whole, ubuf, gbuf, xsems = rest[13:19]
    sum_bufs = rest[19:22]
    bufs = rest[22 : 22 + nbuf]
    sems = rest[22 + nbuf :]
    ring = Ring(pl_.ndp)
    ring.barrier(ring.flips())
    parts = [pl_.rs_in, pl_.rs_out] * L
    scatter = Scatter(ring, grads, parts, bufs, sems)
    everything = range(2 * L)
    scatter.begin(everything)
    for l in range(L):
        acc[8 * l : 8 * l + 8, : sz.CW] = smalls[l][...]
        acc[8 * l : 8 * l + 8, sz.CW :] = heads[l][...]
    total = AllSum(ring, acc, sum_bufs)
    calls = weave(scatter.schedule(everything), total.schedule())
    mid = len(calls) // 3
    for call, args in calls[:mid]:
        call(*args)
    give_u = Exchange(ring, u, ubuf, xsems, 0)
    give_g = Exchange(ring, g, gbuf, xsems, 1)
    for call, args in calls[mid:]:
        call(*args)
    give_u.result(resid)
    give_g.result(grad_in)
    own_small(pl_, acc, picks, (g_in, g_taps, g_cbias, g_gout), ring.me)
    head_grads(pl_, acc, g_sbias, g_decay, g_skip)
    for l in range(L):
        scatter.result(2 * l + 1, g_out.at[l])
        scatter.result(2 * l, whole)
        g_gate[l] = whole[:, : sz.E]
        g_conv[l] = whole[:, sz.E : sz.STEP]
        g_step[l] = whole[:, sz.STEP : sz.STEP + 2 * sz.H]
    scatter.drain(everything)


def scatter_call(pl_, u, g, grads, smalls, heads):
    sz, L, ndp = pl_.sz, pl_.L, pl_.ndp
    shape = lambda *s: jax.ShapeDtypeStruct(s, F32)
    r_in, r_out = sz.D // ndp, sz.E // ndp
    out = [
        jax.ShapeDtypeStruct((2, sz.T, sz.D), BF16),
        shape(2, sz.T, sz.D),
        shape(L, pl_.n_in),
        shape(L, r_in, sz.E),
        shape(L, r_in, sz.CW),
        shape(L, r_in, 2 * sz.H),
        shape(L, pl_.K, pl_.n_conv),
        shape(L, pl_.n_conv),
        shape(L, 2 * sz.H),
        shape(L, sz.H),
        shape(L, sz.H),
        shape(L, pl_.n_out),
        shape(L, r_out, sz.D),
    ]
    bufs, sems = Scatter.scratch(ndp, [(r_in, sz.NP), (r_out, sz.D)] * L, [pl_.rs_in, pl_.rs_out] * L)
    acc_shape = (8 * L, sz.CW + LANES)
    return pl.pallas_call(
        functools.partial(scatter_kernel, pl_, len(bufs)),
        out_shape=out,
        in_specs=[VM] * (2 + 4 * L),
        out_specs=[VM] * len(out),
        scratch_shapes=[
            pltpu.VMEM(acc_shape, F32),
            pltpu.VMEM((ndp, 3, 8 * L, LANES), F32),
            pltpu.VMEM((r_in, sz.NP), F32),
            pltpu.VMEM((2, sz.T, sz.D), BF16),
            pltpu.VMEM((2, sz.T, sz.D), BF16),
            pltpu.SemaphoreType.DMA((2, 2)),
        ] + AllSum.scratch(ndp, acc_shape) + bufs + sems,
        compiler_params=pltpu.CompilerParams(
            collective_id=2, has_side_effects=True, vmem_limit_bytes=ROOM
        ),
    )(u, g, *grads, *smalls, *heads)


def pad_lanes(v, width=LANES):
    return jnp.pad(v, [(0, 0)] * (v.ndim - 1) + [(0, width - v.shape[-1])])


def plain_gather(pl_, w_gate, w_conv, w_step, in_gain, conv_weight, conv_bias, out_gain, w_out,
                 step_bias, decay_log, skip_gain):
    sz = pl_.sz
    fetch = lambda v, axis=0: lax.all_gather(v, "dp", axis=axis, tiled=True)
    shard = jnp.concatenate([w_gate, w_conv, pad_lanes(w_step)], axis=2)
    full = []
    for l in range(pl_.L):
        full += [fetch(shard[l]), fetch(w_out[l])]
    wide = lambda v: pad_lanes(v.astype(F32), sz.CW)[:, None]
    decay = jnp.exp(decay_log)
    table = jnp.concatenate(
        [wide(fetch(in_gain, 1)), fetch(conv_weight, 2).astype(F32), wide(fetch(conv_bias, 1)),
         wide(fetch(out_gain, 1)), wide(step_bias), wide(jnp.concatenate([decay, decay], 1)),
         wide(jnp.repeat(skip_gain, HD, axis=1))], axis=1)
    return full + [jnp.pad(table, ((0, 0), (0, TABLE_ROWS - table.shape[1]), (0, 0)))]


def plain_scatter(pl_, u, g, grads, smalls, heads):
    sz, K = pl_.sz, pl_.K
    me = lax.axis_index("dp")
    summed = [
        lax.psum(lax.psum_scatter(v, "dp", scatter_dimension=0, tiled=True).astype(F32), "dir")
        for v in grads
    ]
    small, head = lax.psum((jnp.stack(smalls), jnp.stack(heads)), ("dir", "dp"))
    own = lambda v, n: lax.dynamic_slice_in_dim(v, me * n, n, axis=v.ndim - 1)
    win = jnp.stack(summed[0::2])
    return (
        lax.all_gather(u.astype(BF16), "dir"),
        lax.all_gather(g, "dir"),
        own(small[:, 0], pl_.n_in),
        win[:, :, : sz.E],
        win[:, :, sz.E : sz.STEP],
        win[:, :, sz.STEP : sz.STEP + 2 * sz.H],
        own(small[:, 1 : 1 + K], pl_.n_conv),
        own(small[:, 5], pl_.n_conv),
        head[:, 0, : 2 * sz.H],
        head[:, 1, : sz.H] + head[:, 1, sz.H : 2 * sz.H],
        head[:, 2, : sz.H],
        own(small[:, 6], pl_.n_out),
        jnp.stack(summed[1::2]),
    )


def shards(resid_in, grad_out, seq_spans, in_gain, w_gate_in, w_conv_in, w_step, conv_weight,
           conv_bias, step_bias, decay_log, skip_gain, out_gain, w_out):
    layers, taps = conv_weight.shape[:2]
    ndp = lax.axis_size("dp")
    sz = Sizes(resid_in.shape[2], w_gate_in.shape[2], w_conv_in.shape[2], skip_gain.shape[1])
    pl_ = Plan(layers, taps, ndp, sz, in_gain.shape[1], conv_weight.shape[2], out_gain.shape[1])
    whole_tiles = w_gate_in.shape[1] % 16 == 0 and w_out.shape[1] % 16 == 0
    gathered = (gather_call if whole_tiles else plain_gather)(
        pl_, w_gate_in, w_conv_in, w_step, in_gain, conv_weight, conv_bias, out_gain, w_out,
        step_bias, decay_log, skip_gain)
    win, wout, table = gathered[0:-1:2], gathered[1:-1:2], gathered[-1]

    u, saved = resid_in, []
    for l in range(layers):
        proj, y, unext = fwd_call(sz, l, seq_spans, u, win[l], wout[l], table)
        saved.append((u, proj, y))
        u = unext
    g = grad_out
    grads, smalls, heads = [None] * (2 * layers), [None] * layers, [None] * layers
    for l in reversed(range(layers)):
        u_in, proj, y = saved[l]
        g, grads[2 * l], grads[2 * l + 1], smalls[l], heads[l] = bwd_call(
            sz, l, l == layers - 1, seq_spans, g, u_in, win[l], wout[l], proj, y, table)
    out = (scatter_call if whole_tiles else plain_scatter)(pl_, u, g, grads, smalls, heads)
    return tuple(out)


def solution(mesh):
    rows, cols_, last = P(None, "dp", None), P(None, "dp"), P(None, None, "dp")
    placed = (rows, rows, cols_, cols_, rows, rows, rows, last, cols_, P(), P(), P(), cols_, rows)
    out = (rows, rows, cols_, rows, rows, rows, last, cols_, P(), P(), P(), cols_, rows)
    return jax.shard_map(shards, mesh=mesh, in_specs=placed, out_specs=out, check_vma=False)
```

```python
import functools
import jax
import jax.numpy as jnp
from jax import lax
from jax.experimental import pallas as pl
from jax.experimental.pallas import tpu as pltpu
from jax.sharding import PartitionSpec as P

BLK = 128
HD = 64
F32 = jnp.float32
BF16 = jnp.bfloat16
HIGH = lax.Precision.HIGHEST
LANES = 128


def mm(a, b):
    return lax.dot_general(a, b, (((1,), (0,)), ((), ())), preferred_element_type=F32)


def mm_nt(a, b):
    return lax.dot_general(a, b, (((1,), (1,)), ((), ())), preferred_element_type=F32)


def mm_tn(a, b):
    return lax.dot_general(a, b, (((0,), (0,)), ((), ())), preferred_element_type=F32)


def mm_exact(a, b):
    return lax.dot_general(
        a, b, (((1,), (0,)), ((), ())), precision=HIGH, preferred_element_type=F32
    )


def iota(shape, dim):
    return lax.broadcasted_iota(jnp.int32, shape, dim)


def square_masks():
    row, col = iota((BLK, BLK), 0), iota((BLK, BLK), 1)
    return row, col


def lag_keep(keep1, lag, rows=2 * BLK):
    at = iota((rows, 1), 0)
    first = (at >= lag).astype(F32)
    edge = ((at >= BLK) & (at < BLK + lag)).astype(F32)
    return first - edge * (1.0 - keep1)


def silu(v):
    return v * jax.nn.sigmoid(v)


class Sizes:
    def __init__(self, width, inner, convw, heads):
        self.D, self.E, self.CW, self.H = width, inner, convw, heads
        self.NP = inner + convw + LANES
        self.STEP = inner + convw
        self.T = 2 * BLK


def spread_matrix(sz, base):
    row = iota((LANES, sz.E), 0)
    col = iota((LANES, sz.E), 1)
    return (row % 64 == col // HD + base).astype(BF16)


def spread(values, matrix):
    high = values.astype(BF16).astype(F32)
    low = values - high
    lane = iota(values.shape, 1)
    packed = jnp.where(lane < 64, high, pltpu.roll(low, 64, 1)).astype(BF16)
    return mm(packed, matrix)


def conv_phase(sz, cin_of, taps, bias, keep1, out_ref, slope_ref):
    keeps = [None] + [lag_keep(keep1, k) for k in range(1, 4)]

    def chunk(n, _):
        at = pl.ds(pl.multiple_of(n * LANES, LANES), LANES)
        cin = cin_of(n)
        z = bias[:, at] + taps[0:1, at] * cin
        for k in range(1, 4):
            z = z + taps[k : k + 1, at] * (pltpu.roll(cin, k, 0) * keeps[k])
        sig = jax.nn.sigmoid(z)
        act = z * sig
        out_ref[:, at] = act
        if slope_ref is not None:
            slope_ref[:, at] = sig + act * (1.0 - sig)
        return 0

    lax.fori_loop(0, sz.CW // LANES, chunk, 0)


def step_phase(sz, raw, sbias, decay):
    z = raw + sbias
    dt = jnp.maximum(z, 0.0) + jnp.log1p(jnp.exp(-jnp.abs(z)))
    a = -dt * decay
    row, col = square_masks()
    lower = (row >= col).astype(F32)
    upper = (row <= col).astype(F32)
    lane = iota((BLK, LANES), 1)
    sums = []
    for b in range(2):
        part = a[b * BLK : (b + 1) * BLK]
        down, up = mm_exact(lower, part), mm_exact(upper, part)
        sums.append(jnp.where(lane < sz.H, down, up))
    return z, dt, a, sums


def b_and_c(sz, conv_ref):
    lane = iota((sz.T, LANES), 1)
    out = []
    for way in range(2):
        pair = conv_ref[:, sz.E + way * LANES : sz.E + (way + 1) * LANES]
        bp = jnp.where(lane < 64, pair, 0.0)
        cp = jnp.where(lane < 64, pltpu.roll(pair, 64, 1), 0.0)
        cp = pltpu.roll(cp, 1 if way == 0 else sz.T - 1, 0)
        out.append((bp.astype(BF16), cp.astype(BF16)))
    return out


def blk(v, b):
    return v[b * BLK : (b + 1) * BLK]


def carry_weights(sz, dt, sums):
    end0 = jnp.exp(sums[0][BLK - 1 : BLK, :] - sums[0])
    end1 = jnp.exp(sums[1][0:1, :] - sums[1])
    lane = iota((BLK, LANES), 1)
    fwd = jnp.where(lane < sz.H, end0, 0.0)
    rev = jnp.where((lane >= sz.H) & (lane < 2 * sz.H), end1, 0.0)
    return fwd, rev


def forward_scan(sz, conv_ref, y_ref, colb, rowt, bc, dt, a, sums, keep1, spreads):
    row, col = square_masks()
    low = row > col
    (bf, cf), (bb, cb) = bc
    excl = [sums[b] - blk(a, b) for b in range(2)]
    scores = []
    for b in range(2):
        sf = mm_nt(blk(cf, b), blk(bf, b))
        sb = mm_nt(blk(cb, b), blk(bb, b))
        scores.append(jnp.where(low, sf, jnp.where(row < col, sb, 0.0)))
        rowt[0, b] = sums[b].T
        rowt[1, b] = blk(dt, b).T
        for h in range(sz.H):
            ef = jnp.broadcast_to(excl[b][:, h : h + 1], (BLK, BLK))
            eb = jnp.broadcast_to(excl[b][:, sz.H + h : sz.H + h + 1], (BLK, BLK))
            colb[0, h, b * BLK : (b + 1) * BLK] = jnp.where(low, ef, eb)
    left = iota((BLK, LANES), 1) < HD

    def pair(p, _):
        at = pl.ds(pl.multiple_of(p * LANES, LANES), LANES)
        for b in range(2):
            rows = slice(b * BLK, (b + 1) * BLK)
            x = conv_ref[rows, at].astype(BF16)
            ys = []
            for hh in range(2):
                h = 2 * p + hh
                sum_row = jnp.where(low, rowt[0, b, pl.ds(h, 1)], rowt[0, b, pl.ds(sz.H + h, 1)])
                dt_row = jnp.where(low, rowt[1, b, pl.ds(h, 1)], rowt[1, b, pl.ds(sz.H + h, 1)])
                decay = jnp.exp(jnp.minimum(colb[0, h, rows] - sum_row, 0.0))
                mix = decay * scores[b] * dt_row
                ys.append(mm(mix.astype(BF16), x))
            y_ref[rows, at] = jnp.where(left, ys[0], ys[1])
        return 0

    lax.fori_loop(0, sz.H // 2, pair, 0)
    states = carry_states(sz, conv_ref, bc, dt, sums, keep1, spreads)
    y_ref[BLK:, :] += mm(blk(cf, 1), states[0]) * spread(jnp.exp(excl[1]), spreads[0])
    y_ref[:BLK, :] += mm(blk(cb, 0), states[1]) * spread(jnp.exp(excl[0]), spreads[1])


def carry_states(sz, conv_ref, bc, dt, sums, keep1, spreads):
    (bf, _), (bb, _) = bc
    fwd, rev = carry_weights(sz, dt, sums)
    xf = conv_ref[:BLK, : sz.E] * spread(fwd * blk(dt, 0), spreads[0])
    xb = conv_ref[BLK:, : sz.E] * spread(rev * blk(dt, 1), spreads[1])
    sf = mm_tn(blk(bf, 0), xf.astype(BF16)) * keep1
    sb = mm_tn(blk(bb, 1), xb.astype(BF16)) * keep1
    return sf.astype(BF16), sb.astype(BF16)


ROWS = 16


def row_loop(sz, body, init):
    def step(n, carry):
        return body(pl.ds(pl.multiple_of(n * ROWS, ROWS), ROWS), n, carry)

    return lax.fori_loop(0, sz.T // ROWS, step, init)


def live_rows(n, live1):
    later = (n >= BLK // ROWS).astype(F32)
    return 1.0 + later * (live1 - 1.0)


def norm_in(sz, u_ref, gain, normed_ref):
    def body(at, n, _):
        u = u_ref[at, :].astype(F32)
        r = lax.rsqrt(jnp.mean(u * u, axis=-1, keepdims=True) + 1e-05)
        normed_ref[at, :] = (u * r * gain[...]).astype(BF16)
        return 0

    row_loop(sz, body, 0)


def project(sz, normed_ref, win_ref, proj_ref, cols=None):
    width = sz.NP // 9
    normed = normed_ref[...]
    for n in range(9):
        proj_ref[:, n * width : (n + 1) * width] = mm(normed, win_ref[:, n * width : (n + 1) * width])


def gate_mix(sz, at, y_ref, conv_ref, proj_ref, skipw):
    x = conv_ref[at, : sz.E]
    gate = proj_ref[at, : sz.E]
    mixed = y_ref[at, :] + x * skipw[...]
    sig = jax.nn.sigmoid(gate)
    act = gate * sig
    gated = mixed * act
    scale = lax.rsqrt(jnp.mean(gated * gated, axis=-1, keepdims=True) + 1e-05)
    return x, gate, mixed, sig, act, gated, scale


def post_mix(sz, y_ref, conv_ref, proj_ref, skipw, gain, nout_ref):
    def body(at, n, _):
        _, _, _, _, _, gated, scale = gate_mix(sz, at, y_ref, conv_ref, proj_ref, skipw)
        nout_ref[at, :] = (gated * scale * gain[...]).astype(BF16)
        return 0

    row_loop(sz, body, 0)


def forward_layer(sz, p, flags, u_ref, win_ref, wout_ref, proj_ref, y_ref, unext_ref, conv_ref,
                  normed_ref, nout_ref, colb, rowt, slope_ref=None, hook=lambda n: None):
    keep1, live1 = flags[0], flags[1]
    norm_in(sz, u_ref, p["gain_in"], normed_ref)
    hook(0)
    project(sz, normed_ref, win_ref, proj_ref)
    hook(1)
    cin_of = lambda n: proj_ref[:, pl.ds(pl.multiple_of(sz.E + n * LANES, LANES), LANES)]
    conv_phase(sz, cin_of, p["taps"], p["cbias"], keep1, conv_ref, slope_ref)
    hook(2)
    _, dt, a, sums = step_phase(sz, proj_ref[:, sz.STEP :], p["sbias"][...], p["decay"][...])
    spreads = (spread_matrix(sz, 0), spread_matrix(sz, sz.H))
    bc = b_and_c(sz, conv_ref)
    forward_scan(sz, conv_ref, y_ref, colb, rowt, bc, dt, a, sums, keep1, spreads)
    hook(3)
    post_mix(sz, y_ref, conv_ref, proj_ref, p["skipw"], p["gain_out"], nout_ref)
    hook(4)
    branch = mm(nout_ref[...], wout_ref[...])
    unext_ref[:BLK, :] = u_ref[:BLK, :].astype(F32) + branch[:BLK]
    unext_ref[BLK:, :] = u_ref[BLK:, :].astype(F32) + live1 * branch[BLK:]


def fold8(v):
    out = v[0:8]
    for n in range(1, v.shape[0] // 8):
        out = out + v[n * 8 : (n + 1) * 8]
    return out


def colsum(v):
    return jnp.sum(v, axis=0, keepdims=True)


def backward_scan(sz, conv_ref, gy_ref, gx_ref, gbc_ref, colb, rowt, accs, z, dt, a, sums, keep1,
                  spreads, decay, hook):
    row, col = square_masks()
    low = row < col
    bc = b_and_c(sz, conv_ref)
    (bf, cf), (bb, cb) = bc
    excl = [sums[b] - blk(a, b) for b in range(2)]
    scores = []
    for b in range(2):
        sf = mm_nt(blk(bf, b), blk(cf, b))
        sb = mm_nt(blk(bb, b), blk(cb, b))
        scores.append(jnp.where(low, sf, jnp.where(row > col, sb, 0.0)))
        rowt[0, b] = excl[b].T
        here = slice(b * BLK, (b + 1) * BLK)
        for h in range(sz.H):
            for n, v in ((0, sums[b]), (1, blk(dt, b))):
                vf = jnp.broadcast_to(v[:, h : h + 1], (BLK, BLK))
                vb = jnp.broadcast_to(v[:, sz.H + h : sz.H + h + 1], (BLK, BLK))
                colb[n, h, here] = jnp.where(low, vf, vb)
    gscore, rho_ref, kappa_ref = accs
    gscore[...] = jnp.zeros_like(gscore)
    kappa_ref[...] = jnp.zeros_like(kappa_ref)
    rho_ref[...] = jnp.zeros_like(rho_ref)
    lane = iota((BLK, LANES), 1)
    left = lane < HD

    def pair(p, _):
        at = pl.ds(pl.multiple_of(p * LANES, LANES), LANES)
        for b in range(2):
            rows = slice(b * BLK, (b + 1) * BLK)
            x = conv_ref[rows, at]
            gy = gy_ref[rows, at]
            x_two = jnp.concatenate([jnp.where(left, x, 0.0), jnp.where(left, 0.0, x)], axis=0)
            w_two = mm_nt(x_two.astype(BF16), gy)
            gxs = []
            gs = gscore[rows]
            kap = kappa_ref[rows]
            for hh in range(2):
                h = 2 * p + hh
                ex_row = jnp.where(low, rowt[0, b, pl.ds(h, 1)], rowt[0, b, pl.ds(sz.H + h, 1)])
                decay_m = jnp.exp(jnp.minimum(ex_row - colb[0, h, rows], 0.0))
                dtc = colb[1, h, rows]
                w = w_two[hh * BLK : (hh + 1) * BLK]
                es = decay_m * scores[b]
                gxs.append(mm((es * dtc).astype(BF16), gy))
                gs = gs + decay_m * w * dtc
                r = es * w
                q = r * dtc
                rl = jnp.where(low, r, 0.0)
                kap = jnp.where(lane == h, jnp.sum(rl, axis=1, keepdims=True), kap)
                kap = jnp.where(lane == sz.H + h, jnp.sum(r - rl, axis=1, keepdims=True), kap)
                ql = jnp.where(low, q, 0.0)
                rho_ref[b, pl.ds(h, 1)] = colsum(ql)
                rho_ref[b, pl.ds(sz.H + h, 1)] = colsum(q - ql)
            gscore[rows] = gs
            kappa_ref[rows] = kap
            gx_ref[rows, at] += jnp.where(left, gxs[0], gxs[1])
        hook(p)
        return 0

    lax.fori_loop(0, sz.H // 2, pair, 0)

    states = carry_states(sz, conv_ref, bc, dt, sums, keep1, spreads)
    ends = carry_weights(sz, dt, sums)
    values, enters = [], []
    gbs, gcs = [], []
    for way in range(2):
        src, dst = (0, 1) if way == 0 else (1, 0)
        bw, cw = bc[way]
        rows_s = slice(src * BLK, (src + 1) * BLK)
        rows_d = slice(dst * BLK, (dst + 1) * BLK)
        gcar = gy_ref[rows_d, :].astype(F32) * spread(jnp.exp(excl[dst]), spreads[way])
        gcar_low = gcar.astype(BF16)
        inner = mm(blk(cw, dst), states[way])
        enters.append(mm_nt((gcar * inner).astype(BF16), spreads[way]))
        gstate = (mm_tn(blk(cw, dst), gcar_low) * keep1).astype(BF16)
        gc_d = mm_nt(gcar_low, states[way])
        weight = spread(ends[way] * blk(dt, src), spreads[way])
        x = conv_ref[rows_s, : sz.E]
        gb_s = mm_nt((x * weight).astype(BF16), gstate)
        bg = mm(blk(bw, src), gstate)
        gx_ref[rows_s, :] += weight * bg
        values.append(mm_nt((x * bg).astype(BF16), spreads[way]))
        gb, gc = [None, None], [None, None]
        for b in range(2):
            g = gscore[b * BLK : (b + 1) * BLK]
            g = jnp.where(low if way == 0 else row > col, g, 0.0).astype(BF16)
            gb[b] = mm(g, blk(cw, b))
            gc[b] = mm_tn(g, blk(bw, b))
        gb[src] = gb[src] + gb_s
        gc[dst] = gc[dst] + gc_d
        gc_all = jnp.concatenate(gc, axis=0)
        at = iota((sz.T, 1), 0)
        if way == 0:
            gc_all = jnp.where(at == sz.T - 1, 0.0, pltpu.roll(gc_all, sz.T - 1, 0))
        else:
            gc_all = jnp.where(at == 0, 0.0, pltpu.roll(gc_all, 1, 0))
        gb_all = jnp.concatenate(gb, axis=0)
        wide_lane = iota((sz.T, LANES), 1)
        gbc_ref[:, way * LANES : (way + 1) * LANES] = jnp.where(
            wide_lane < 64, gb_all, pltpu.roll(gc_all, 64, 1)
        )

    strict_low = (row > col).astype(F32)
    strict_up = (row < col).astype(F32)
    is_f = lane < sz.H
    is_b = (lane >= sz.H) & (lane < 2 * sz.H)
    gsteps, gdecay = [], None
    for b in range(2):
        kr = kappa_ref[b * BLK : (b + 1) * BLK]
        kap = kr * blk(dt, b)
        rho = rho_ref[b].T
        if b == 1:
            rho = rho + jnp.where(is_f, enters[0], 0.0)
            zr = jnp.where(is_b, values[1], 0.0) * ends[1]
        else:
            rho = rho + jnp.where(is_b, enters[1], 0.0)
            zr = jnp.where(is_f, values[0], 0.0) * ends[0]
        zed = zr * blk(dt, b)
        diff = rho - kap
        both = jnp.concatenate([diff, zed], axis=1)
        up, down = mm_exact(strict_up, both), mm_exact(strict_low, both)
        ga = jnp.where(
            is_f, up[:, :LANES] + down[:, LANES:], down[:, :LANES] + up[:, LANES:]
        ) - kap
        ga = jnp.where(is_f | is_b, ga, 0.0)
        gdt = jnp.where(is_f | is_b, kr + zr, 0.0) - ga * decay
        gsteps.append(gdt * jax.nn.sigmoid(blk(z, b)))
        part = colsum(ga * blk(a, b))
        gdecay = part if gdecay is None else gdecay + part
    return jnp.concatenate(gsteps, axis=0), gdecay


def backward_layer(sz, p, flags, g_ref, u_ref, win_ref, wout_ref, proj_ref, y_ref, gu_ref,
                   gwin_ref, gwout_ref, small_ref, head_ref, s, hook=lambda n: None,
                   recompute=True):
    keep1, live1 = flags[0], flags[1]
    conv_ref, slope_ref = s["conv"], s["slope"]
    D, E, CW = sz.D, sz.E, sz.CW
    if recompute:
        cin_of = lambda n: proj_ref[:, pl.ds(pl.multiple_of(E + n * LANES, LANES), LANES)]
        conv_phase(sz, cin_of, p["taps"], p["cbias"], keep1, conv_ref, slope_ref)
        norm_in(sz, u_ref, p["gain_in"], s["normed"])
    hook(0)

    def mask_g(at, n, _):
        s["gb"][at, :] = (g_ref[at, :].astype(F32) * live_rows(n, live1)).astype(BF16)
        return 0

    row_loop(sz, mask_g, 0)
    s["gx"][...] = mm_nt(s["gb"][...], wout_ref[...])
    hook(1)
    s["acc"][...] = jnp.zeros_like(s["acc"])

    def post_back(at, n, _):
        x, gate, mixed, sig, act, gated, scale = gate_mix(sz, at, y_ref, conv_ref, proj_ref, p["skipw"])
        hat = gated * scale
        gn = s["gx"][at, :]
        s["acc"][0] += fold8(gn * hat)
        s["nout"][at, :] = (hat * p["gain_out"][...]).astype(BF16)
        gh = gn * p["gain_out"][...]
        gg = scale * (gh - hat * jnp.mean(gh * hat, axis=-1, keepdims=True))
        gm = gg * act
        s["gproj"][at, :E] = (gg * mixed * (sig + act * (1.0 - sig))).astype(BF16)
        s["gy"][at, :] = gm.astype(BF16)
        s["gx"][at, :] = gm * p["skipw"][...]
        s["acc"][1] += fold8(gm * x)
        return 0

    row_loop(sz, post_back, 0)
    hook(2)
    small_ref[6:7, :E] = colsum(s["acc"][0])
    gwout_ref[...] = mm_tn(s["nout"][...], s["gb"][...]).astype(BF16)
    hook(3)
    spreads = (spread_matrix(sz, 0), spread_matrix(sz, sz.H))
    z, dt, a, sums = step_phase(sz, proj_ref[:, sz.STEP :], p["sbias"][...], p["decay"][...])
    gsteps, gdecay = backward_scan(
        sz, conv_ref, s["gy"], s["gx"], s["gbc"], s["colb"], s["rowt"],
        (s["gscore"], s["rho"], s["kappa"]), z, dt, a, sums, keep1, spreads, p["decay"][...],
        lambda n: None,
    )
    hook(4)
    s["gproj"][:, sz.STEP :] = gsteps.astype(BF16)
    skip_sum = s["acc"][1]
    first = skip_sum.astype(BF16)
    rest = (skip_sum - first.astype(F32)).astype(BF16)
    gskip = colsum(mm_nt(first, spreads[0]) + mm_nt(rest, spreads[0]))
    head_ref[...] = jnp.zeros_like(head_ref)
    head_ref[0:1, :] = colsum(gsteps)
    head_ref[1:2, :] = gdecay
    head_ref[2:3, :] = gskip

    keeps = [None] + [lag_keep(keep1, k) for k in range(1, 4)]

    def conv_chunk(n, gout):
        at = pl.ds(pl.multiple_of(n * LANES, LANES), LANES)
        wide = pl.ds(pl.multiple_of(E + n * LANES, LANES), LANES)
        cin = proj_ref[:, wide]
        gz = gout * slope_ref[:, at]
        taps = p["taps"]
        gc = taps[0:1, at] * gz
        small_ref[1:2, at] = colsum(gz * cin)
        for k in range(1, 4):
            gk = gz * keeps[k]
            small_ref[1 + k : 2 + k, at] = colsum(gk * pltpu.roll(cin, k, 0))
            gc = gc + taps[k : k + 1, at] * pltpu.roll(gk, sz.T - k, 0)
        small_ref[5:6, at] = colsum(gz)
        s["gproj"][:, wide] = gc.astype(BF16)

    def x_chunk(n, _):
        conv_chunk(n, s["gx"][:, pl.ds(pl.multiple_of(n * LANES, LANES), LANES)])
        return 0

    lax.fori_loop(0, E // LANES, x_chunk, 0)
    for n in range((CW - E) // LANES):
        conv_chunk(E // LANES + n, s["gbc"][:, n * LANES : (n + 1) * LANES])
    hook(5)
    width = sz.NP // 9
    normed = s["normed"][...]
    total = None
    for n in range(9):
        cols = slice(n * width, (n + 1) * width)
        gp = s["gproj"][:, cols]
        gwin_ref[:, cols] = mm_tn(normed, gp).astype(BF16)
        part = mm_nt(gp, win_ref[:, cols])
        total = part if total is None else total + part
    s["gn"][...] = total
    hook(6)
    s["acc"][0] = jnp.zeros_like(s["acc"][0])

    def in_back(at, n, _):
        u = u_ref[at, :].astype(F32)
        r = lax.rsqrt(jnp.mean(u * u, axis=-1, keepdims=True) + 1e-05)
        hat = u * r
        gn = s["gn"][at, :]
        s["acc"][0, :, :D] += fold8(gn * hat)
        gh = gn * p["gain_in"][...]
        gu = r * (gh - hat * jnp.mean(gh * hat, axis=-1, keepdims=True))
        gu_ref[at, :] = g_ref[at, :].astype(F32) + gu
        return 0

    row_loop(sz, in_back, 0)
    small_ref[0:1, :D] = colsum(s["acc"][0, :, :D])
    hook(7)


def backward_scratch(sz):
    T, E, CW, D, H = sz.T, sz.E, sz.CW, sz.D, sz.H
    return dict(
        conv=pltpu.VMEM((T, CW), F32),
        slope=pltpu.VMEM((T, CW), F32),
        normed=pltpu.VMEM((T, D), BF16),
        gb=pltpu.VMEM((T, D), BF16),
        gx=pltpu.VMEM((T, E), F32),
        gy=pltpu.VMEM((T, E), BF16),
        nout=pltpu.VMEM((T, E), BF16),
        gproj=pltpu.VMEM((T, sz.NP), BF16),
        gbc=pltpu.VMEM((T, 2 * LANES), F32),
        gn=pltpu.VMEM((T, D), F32),
        acc=pltpu.VMEM((2, 8, E), F32),
        colb=pltpu.VMEM((2, H, T, BLK), F32),
        rowt=pltpu.VMEM((2, 2, LANES, BLK), F32),
        gscore=pltpu.VMEM((T, BLK), F32),
        rho=pltpu.VMEM((2, LANES, BLK), F32),
        kappa=pltpu.VMEM((T, LANES), F32),
    )


PARAMS = ("gain_in", "taps", "cbias", "sbias", "decay", "skipw", "gain_out")


MESH = pl.DeviceIdType.MESH


def remote(src, dst, ssem, rsem, device):
    return pltpu.make_async_remote_copy(
        src, dst, ssem, rsem, device_id=device, device_id_type=MESH
    )


class Ring:
    def __init__(self, ndp, both_ways=True):
        nc = ndp // 2
        self.nc, self.ndp = nc, ndp
        self.plus = nc // 2 if both_ways else nc - 1
        self.minus = nc - 1 - self.plus
        self.d, self.me = lax.axis_index("dir"), lax.axis_index("dp")
        p, self.c = self.me // 2, self.me % 2
        odd = p % 2
        self.pos = (1 - odd) * (p // 2) + odd * (nc - 1 - p // 2)
        self.turn = 1 - 2 * self.c
        self.nxt = (self.d, 2 * self.chip(1) + self.c)
        self.prv = (self.d, 2 * self.chip(-1) + self.c)
        self.sib = (self.d, 2 * p + 1 - self.c)
        self.mate = (1 - self.d, self.me)

    def chip(self, ahead):
        nc = self.nc
        pos = (self.pos + ahead * self.turn + nc) % nc
        half = pos // (nc // 2)
        return (1 - half) * 2 * pos + half * (2 * (nc - 1 - pos) + 1)

    def flip(self, bit):
        return (self.d, self.me + (1 - 2 * ((self.me // bit) % 2)) * bit)

    def flips(self):
        return [self.flip(1 << n) for n in range(self.ndp.bit_length() - 1)]

    def barrier(self, more=()):
        bar = pltpu.get_barrier_semaphore()
        greeted = (self.nxt, self.prv, self.sib, self.mate) + tuple(more)
        for device in greeted:
            pl.semaphore_signal(bar, inc=1, device_id=device, device_id_type=MESH)
        pl.semaphore_wait(bar, len(greeted))

    def hops(self):
        out = []
        for s in range(1, self.plus + 1):
            out.append((1, s))
            if s <= self.minus:
                out.append((-1, s))
        return out

    def index(self, sign, hop):
        return hop if sign > 0 else self.plus + hop


def cols(start, width):
    if isinstance(start, int):
        return pl.ds(start, width)
    return pl.ds(pl.multiple_of(start, LANES), width)


def rows_at(slot, count):
    return pl.ds(pl.multiple_of(slot * count, 16), count)


class Gather:
    def __init__(self, ring, groups, parts, sems):
        self.r, self.g, self.parts = ring, groups, parts
        self.arrive, self.beside, self.along, self.aside, self.across = sems[:5]
        self.local = sems[5]

    @staticmethod
    def scratch(ndp, groups):
        return [pltpu.SemaphoreType.DMA((3 * groups, ndp // 2))] * 5 + [
            pltpu.SemaphoreType.DMA((groups,))
        ]

    def view(self, g, ref, slot, k):
        rows = self.g[g][0].shape[0]
        w, w2 = self.parts[g]
        at = cols(2 * w, w2) if k == 1 else cols((self.r.d if k == 0 else 1 - self.r.d) * w, w)
        return ref.at[:, at] if slot is None else ref.at[rows_at(slot, rows), at]

    def copies(self, g, k, sign, hop):
        r, (src, dst) = self.r, self.g[g]
        m, n = 3 * g + k, (0 if hop == 0 else r.index(sign, hop))
        here = self.view(g, dst, 2 * r.chip(-sign * hop) + r.c, k)
        frm = self.view(g, src, None, k) if hop == 0 else here
        out = []
        if k < 2:
            for way, limit, device in ((1, r.plus, r.nxt), (-1, r.minus, r.prv)):
                if (hop == 0 or way == sign) and hop < limit:
                    to = r.index(way, hop + 1)
                    out.append(remote(frm, here, self.along.at[m, to], self.arrive.at[m, to], device))
        if k == 0 and hop > 0:
            out.append(
                remote(frm, here, self.across.at[m, n], self.arrive.at[m + 2, n], r.mate)
            )
        out.append(remote(frm, here, self.aside.at[m, n], self.beside.at[m, n], r.sib))
        return here, out

    def own(self, g):
        src, dst = self.g[g]
        return pltpu.make_async_copy(
            src, dst.at[rows_at(self.r.me, src.shape[0])], self.local.at[g]
        )

    def event(self, g, k, sign, hop):
        here, out = self.copies(g, k, sign, hop)
        if hop > 0:
            m, n = 3 * g + k, self.r.index(sign, hop)
            remote(here, here, self.along.at[m, n], self.arrive.at[m, n], self.r.nxt).wait_recv()
        for copy in out:
            copy.start()

    def kinds(self, g):
        return (0, 1, 2) if self.parts[g][0] else (1,)

    def begin(self, groups):
        for g in groups:
            for k in self.kinds(g):
                self.event(g, k, 1, 0)
            self.own(g).start()

    def schedule(self, groups):
        order, late = [], []
        for sign, hop in self.r.hops():
            now = [(self.event, (g, k, sign, hop)) for g in groups for k in self.kinds(g) if k < 2]
            order += now + late
            late = [(self.event, (g, 2, sign, hop)) for g in groups if 2 in self.kinds(g)]
        return order + late

    def finish(self, groups):
        r = self.r
        for g in groups:
            src, dst = self.g[g]
            for k in self.kinds(g):
                for sign, hop in [(1, 0)] + r.hops():
                    m, n = 3 * g + k, (0 if hop == 0 else r.index(sign, hop))
                    there = self.view(g, dst, 2 * r.chip(sign * hop) + 1 - r.c, k)
                    remote(
                        there, there, self.aside.at[m, n], self.beside.at[m, n], r.sib
                    ).wait_recv()
            self.own(g).wait()

    def drain(self, groups):
        for g in groups:
            for k in self.kinds(g):
                for sign, hop in [(1, 0)] + self.r.hops():
                    for copy in self.copies(g, k, sign, hop)[1]:
                        copy.wait_send()


class Scatter:
    def __init__(self, ring, groups, parts, bufs, sems):
        self.r, self.g, self.parts, self.bufs = ring, groups, parts, bufs
        (self.s_sib, self.r_sib, self.s_mate, self.r_mate, self.s_ring, self.r_ring,
         self.s_end, self.r_end) = sems

    @staticmethod
    def scratch(ndp, shapes, parts):
        nc = ndp // 2
        bufs = []
        for (rows, width), (w, w2) in zip(shapes, parts):
            bufs += [
                pltpu.VMEM((nc, rows, width), BF16),
                pltpu.VMEM((nc, rows, w), BF16),
                pltpu.VMEM((nc + 1, rows, w + w2), BF16),
                pltpu.VMEM((2, rows, w + w2), BF16),
            ]
        n = len(shapes)
        sems = [pltpu.SemaphoreType.DMA((n, nc))] * 4 + [
            pltpu.SemaphoreType.DMA((2 * n, nc + 1))
        ] * 2 + [pltpu.SemaphoreType.DMA((n,))] * 2
        return bufs, sems

    def buf(self, g):
        return self.bufs[4 * g : 4 * g + 4]

    def span(self, g, k):
        w, w2 = self.parts[g]
        if k == 1:
            return cols(2 * w, w2)
        return cols((self.r.d if k == 0 else 1 - self.r.d) * w, w)

    def packed(self, g, k):
        w, w2 = self.parts[g]
        return pl.ds(0, w) if k == 0 else pl.ds(w, w2)

    def order(self):
        r, out = self.r, []
        for s in range(r.plus):
            out.append(r.plus - s)
            if s < r.minus:
                out.append(-(r.minus - s))
        return out + [0]

    def number(self, ahead):
        return ahead % self.r.nc

    def sib_copy(self, g, ahead):
        r, own, n = self.r, self.g[g], self.number(ahead)
        sib = self.buf(g)[0]
        rows = sib.shape[1]
        src = own.at[rows_at(2 * r.chip(-ahead) + 1 - r.c, rows)]
        return remote(src, sib.at[n], self.s_sib.at[g, n], self.r_sib.at[g, n], r.sib)

    def mate_copy(self, g, ahead):
        r, n = self.r, self.number(ahead)
        sib, mate = self.buf(g)[:2]
        src = sib.at[n, :, self.span(g, 2)]
        return remote(src, mate.at[n], self.s_mate.at[g, n], self.r_mate.at[g, n], r.mate)

    def ring_copy(self, g, k, sign, step):
        r = self.r
        run = self.buf(g)[2]
        frm = run.at[self.slot(sign, step), :, self.packed(g, k)]
        to = run.at[self.slot(sign, step + 1), :, self.packed(g, k)]
        n = self.slot(sign, step + 1)
        device = r.nxt if sign > 0 else r.prv
        return remote(
            frm, to, self.s_ring.at[2 * g + k, n], self.r_ring.at[2 * g + k, n], device
        )

    def slot(self, sign, step):
        return step if sign > 0 else self.r.plus + 1 + step

    def begin(self, groups):
        for g in groups:
            for ahead in self.order():
                self.sib_copy(g, ahead).start()

    def hand_over(self, g, ahead):
        r, own, n = self.r, self.g[g], self.number(ahead)
        sib = self.buf(g)[0]
        rows = sib.shape[1]
        self.sib_copy(g, ahead).wait_recv()
        first = (2 * r.chip(ahead) + r.c) * rows
        at = self.span(g, 2)

        def part(n16, _):
            inner = pl.ds(pl.multiple_of(n16 * 16, 16), 16)
            outer = pl.ds(pl.multiple_of(first + n16 * 16, 16), 16)
            sib[n, inner, at] = (own[outer, at].astype(F32) + sib[n, inner, at].astype(F32)).astype(BF16)
            return 0

        lax.fori_loop(0, rows // 16, part, 0)
        self.mate_copy(g, ahead).start()

    def step(self, g, k, sign, step):
        r, own = self.r, self.g[g]
        sib, mate, run, end = self.buf(g)
        rows = sib.shape[1]
        last = r.plus if sign > 0 else r.minus
        ahead = sign * (last - step)
        n = self.number(ahead)
        if k == 0:
            self.mate_copy(g, ahead).wait_recv()
        if step > 0:
            self.ring_copy(g, k, sign, step - 1).wait_recv()
        first = (2 * r.chip(ahead) + r.c) * rows
        at, mine = self.span(g, k), self.packed(g, k)
        here = self.slot(sign, step)

        def part(n16, _):
            inner = pl.ds(pl.multiple_of(n16 * 16, 16), 16)
            outer = pl.ds(pl.multiple_of(first + n16 * 16, 16), 16)
            total = own[outer, at].astype(F32) + sib[n, inner, at].astype(F32)
            if k == 0:
                total = total + mate[n, inner, :].astype(F32)
            if step > 0:
                total = total + run[here, inner, mine].astype(F32)
            run[here, inner, mine] = total.astype(BF16)
            return 0

        lax.fori_loop(0, rows // 16, part, 0)
        self.ring_copy(g, k, sign, step).start()

    def own_sum(self, g):
        r, own = self.r, self.g[g]
        sib, mate, run, end = self.buf(g)
        rows = sib.shape[1]
        self.mate_copy(g, 0).wait_recv()
        for k in range(2):
            self.ring_copy(g, k, 1, r.plus - 1).wait_recv()
            self.ring_copy(g, k, -1, r.minus - 1).wait_recv()
        first = (2 * r.chip(0) + r.c) * rows

        def part(n16, _):
            inner = pl.ds(pl.multiple_of(n16 * 16, 16), 16)
            outer = pl.ds(pl.multiple_of(first + n16 * 16, 16), 16)
            for k in range(2):
                at, mine = self.span(g, k), self.packed(g, k)
                total = own[outer, at].astype(F32) + sib[0, inner, at].astype(F32)
                if k == 0:
                    total = total + mate[0, inner, :].astype(F32)
                total = total + run[self.slot(1, r.plus), inner, mine].astype(F32)
                total = total + run[self.slot(-1, r.minus), inner, mine].astype(F32)
                end[0, inner, mine] = total.astype(BF16)
            return 0

        lax.fori_loop(0, rows // 16, part, 0)
        self.end_copy(g).start()

    def end_copy(self, g):
        end = self.buf(g)[3]
        return remote(end.at[0], end.at[1], self.s_end.at[g], self.r_end.at[g], self.r.mate)

    def result(self, g, out):
        end = self.buf(g)[3]
        rows = end.shape[1]
        self.end_copy(g).wait_recv()

        def part(n16, _):
            inner = pl.ds(pl.multiple_of(n16 * 16, 16), 16)
            mine0, mine1 = self.packed(g, 0), self.packed(g, 1)
            out[inner, self.span(g, 0)] = end[0, inner, mine0].astype(F32)
            out[inner, self.span(g, 2)] = end[1, inner, mine0].astype(F32)
            out[inner, self.span(g, 1)] = end[0, inner, mine1].astype(F32) + end[1, inner, mine1].astype(F32)
            return 0

        lax.fori_loop(0, rows // 16, part, 0)

    def schedule(self, groups):
        r, calls = self.r, []
        over = [[(self.hand_over, (g, ahead)) for g in groups] for ahead in self.order()]

        def hand(count):
            for _ in range(min(count, len(over))):
                calls.extend(over.pop(0))

        hand(4)
        for s in range(r.plus):
            for sign in (1, -1) if s < r.minus else (1,):
                calls.extend((self.step, (g, k, sign, s)) for g in groups for k in (1, 0))
            hand(2)
        hand(len(over))
        calls.extend((self.own_sum, (g,)) for g in groups)
        return calls

    def drain(self, groups):
        r = self.r
        for g in groups:
            for ahead in self.order():
                self.sib_copy(g, ahead).wait_send()
                self.mate_copy(g, ahead).wait_send()
            for k in range(2):
                for s in range(r.plus):
                    self.ring_copy(g, k, 1, s).wait_send()
                for s in range(r.minus):
                    self.ring_copy(g, k, -1, s).wait_send()
            self.end_copy(g).wait_send()


class AllSum:
    @staticmethod
    def scratch(ndp, shape):
        n = ndp.bit_length()
        return [pltpu.VMEM((n,) + shape, F32), pltpu.SemaphoreType.DMA((n,)), pltpu.SemaphoreType.DMA((n,))]

    def __init__(self, ring, acc, bufs):
        self.acc, (self.buf, self.s, self.r) = acc, bufs
        self.partners = [ring.mate] + ring.flips()

    def copy(self, n):
        return remote(self.acc, self.buf.at[n], self.s.at[n], self.r.at[n], self.partners[n])

    def start(self, n):
        self.copy(n).start()

    def end(self, n):
        self.copy(n).wait()
        self.acc[...] += self.buf[n]

    def schedule(self):
        calls = [(self.start, (0,))]
        for n in range(len(self.partners)):
            calls.append((self.end, (n,)))
            if n + 1 < len(self.partners):
                calls.append((self.start, (n + 1,)))
        return calls


VM = pl.BlockSpec(memory_space=pltpu.VMEM)
SM = pl.BlockSpec(memory_space=pltpu.SMEM)
ANY = pl.BlockSpec(memory_space=pl.ANY)
ROOM = 62 << 20
TABLE_ROWS = 16


def table_params(sz, tab):
    return dict(
        gain_in=tab.at[0:1, : sz.D],
        taps=tab.at[1:5],
        cbias=tab.at[5:6],
        gain_out=tab.at[6:7, : sz.E],
        sbias=tab.at[7:8, :LANES],
        decay=tab.at[8:9, :LANES],
        skipw=tab.at[9:10, : sz.E],
    )


def run_flags(spans, d):
    begin, opens = jnp.int32(0), jnp.int32(0)
    for s in range(spans.shape[1]):
        length = spans[d, s]
        starts = jnp.where(begin == 1, 1, 0) * jnp.where(length > 0, 1, 0)
        opens = jnp.maximum(opens, starts)
        begin = begin + length
    live = jnp.where(begin > 1, 1.0, 0.0).astype(F32)
    opened = jnp.maximum(opens.astype(F32), 1.0 - live)
    return 1.0 - opened, live


class Plan:
    def __init__(self, layers, taps, ndp, sz, n_in, n_conv, n_out):
        self.L, self.K, self.ndp, self.sz = layers, taps, ndp, sz
        self.n_in, self.n_conv, self.n_out = n_in, n_conv, n_out
        tiles_in, tiles_out = sz.NP // LANES, sz.D // LANES
        third_in, third_out = tiles_in // 3 * LANES, tiles_out // 3 * LANES
        self.ag_in = (third_in, sz.NP - 2 * third_in)
        self.ag_out = (third_out, sz.D - 2 * third_out)
        part_in, part_out = tiles_in * 2 // 9 * LANES, tiles_out // 6 * LANES
        self.rs_in = (part_in, sz.NP - 2 * part_in)
        self.rs_out = (part_out, sz.D - 2 * part_out)


def stage_own(pl_, ins, stage, smallf, small, sems):
    sz = pl_.sz
    w_gate, w_conv, w_step, in_gain, conv_weight, conv_bias, out_gain = ins
    copies = []
    for l in range(pl_.L):
        copies.append(
            pltpu.make_async_copy(w_gate.at[l], stage.at[l, :, pl.ds(0, sz.E)], sems.at[2 * l])
        )
        copies.append(
            pltpu.make_async_copy(
                w_conv.at[l], stage.at[l, :, pl.ds(sz.E, sz.CW)], sems.at[2 * l + 1]
            )
        )
    for copy in copies:
        copy.start()
    smallf[...] = jnp.zeros_like(smallf)
    L, K = pl_.L, pl_.K
    smallf[0:L, : pl_.n_in] = in_gain[...].astype(F32)
    for l in range(L):
        smallf[L + l * K : L + (l + 1) * K, : pl_.n_conv] = conv_weight[l].astype(F32)
    smallf[L + L * K : 2 * L + L * K, : pl_.n_conv] = conv_bias[...].astype(F32)
    smallf[2 * L + L * K : 3 * L + L * K, : pl_.n_out] = out_gain[...].astype(F32)
    small[...] = smallf[...].astype(BF16)
    for l in range(L):
        stage[l, :, sz.STEP :] = jnp.zeros((stage.shape[1], LANES), BF16)
        stage[l, :, sz.STEP : sz.STEP + 2 * sz.H] = w_step[l]
    for copy in copies:
        copy.wait()


def fill_table(pl_, table, gathered, step_bias, decay_log, skip_gain):
    sz, L, K = pl_.sz, pl_.L, pl_.K
    table[...] = jnp.zeros_like(table)
    rows = gathered.shape[0] // pl_.ndp
    for q in range(pl_.ndp):
        part = gathered[q * rows : (q + 1) * rows, :].astype(F32)
        for l in range(L):
            table[l, 0:1, q * pl_.n_in : (q + 1) * pl_.n_in] = part[l : l + 1, : pl_.n_in]
            conv = slice(q * pl_.n_conv, (q + 1) * pl_.n_conv)
            table[l, 1 : 1 + K, conv] = part[L + l * K : L + (l + 1) * K, : pl_.n_conv]
            at = L + L * K + l
            table[l, 5:6, conv] = part[at : at + 1, : pl_.n_conv]
            out = slice(q * pl_.n_out, (q + 1) * pl_.n_out)
            table[l, 6:7, out] = part[at + L : at + L + 1, : pl_.n_out]
    head_of = iota((sz.H, sz.E), 1) // HD
    one_hot = (iota((sz.H, sz.E), 0) == head_of).astype(F32)
    wide = mm_exact(skip_gain[...], one_hot)
    decay = jnp.exp(decay_log[...])
    for l in range(L):
        table[l, 7:8, : 2 * sz.H] = step_bias[l : l + 1, :]
        table[l, 8:9, : sz.H] = decay[l : l + 1]
        table[l, 8:9, sz.H : 2 * sz.H] = decay[l : l + 1]
        table[l, 9:10, : sz.E] = wide[l : l + 1]


class Cursor:
    def __init__(self, calls):
        self.calls, self.at = calls, 0

    def take(self, count):
        upto = min(self.at + count, len(self.calls))
        while self.at < upto:
            call, args = self.calls[self.at]
            call(*args)
            self.at += 1

    def through(self, last):
        self.take(last + 1 - self.at)

    def rest(self):
        self.take(len(self.calls))


def staggered(gather, starts):
    rounds = gather.r.hops()
    pairs = [[]]
    for sign, hop in rounds:
        if sign > 0:
            pairs.append([])
        pairs[hop].append((sign, hop))
    calls, ends = [], {}
    late = []
    for n in range(max(starts) + len(pairs) + 1):
        now_late = []
        for g, start in enumerate(starts):
            h = n - start
            if h == 0:
                calls.append((gather.begin, ([g],)))
            elif 0 < h < len(pairs):
                for sign, hop in pairs[h]:
                    for k in gather.kinds(g):
                        if k < 2:
                            calls.append((gather.event, (g, k, sign, hop)))
                        else:
                            now_late.append((gather.event, (g, 2, sign, hop)))
                ends[g] = len(calls) - 1
        for call in late:
            calls.append(call)
            ends[call[1][0]] = len(calls) - 1
        late = now_late
    return calls, ends


def forward_kernel(pl_, *refs):
    sz, L = pl_.sz, pl_.L
    (spans, u0, w_gate, w_conv, w_step, in_gain, conv_weight, conv_bias, out_gain, w_out,
     step_bias, decay_log, skip_gain) = refs[:13]
    out_w = refs[13 : 13 + 2 * L]
    out_s = refs[13 + 2 * L : 13 + 5 * L]
    table = refs[13 + 5 * L]
    rest = refs[14 + 5 * L :]
    full, rest = rest[: 2 * L], rest[2 * L :]
    saved, rest = rest[: 3 * L], rest[3 * L :]
    conv, normed, nout, colb, rowt, stage, smallf, small, gathered, own_sems, out_sems = rest[:11]
    sems = rest[11:]
    ring = Ring(pl_.ndp)
    ring.barrier()
    flags = run_flags(spans, ring.d)
    stage_own(pl_, (w_gate, w_conv, w_step, in_gain, conv_weight, conv_bias, out_gain),
              stage, smallf, small, own_sems)
    groups, parts = [(small, gathered)], [(0, LANES)]
    for l in range(L):
        groups += [(stage.at[l], full[2 * l]), (w_out.at[l], full[2 * l + 1])]
        parts += [pl_.ag_in, pl_.ag_out]
    gather = Gather(ring, groups, parts, sems)
    calls, ends = staggered(gather, STARTS)
    cursor = Cursor(calls)
    cursor.through(max(ends[0], ends[1]))
    gather.finish([0])
    fill_table(pl_, table, gathered, step_bias, decay_log, skip_gain)
    outward = []

    def send_out(src, dst):
        copy = pltpu.make_async_copy(src, dst, out_sems.at[len(outward)])
        copy.start()
        outward.append(copy)

    u = u0.at[ring.d]
    for l in range(L):
        g_in, g_out = 1 + 2 * l, 2 + 2 * l
        cursor.through(ends[g_in])
        gather.finish([g_in])
        send_out(full[2 * l], out_w[2 * l])
        proj, y, unext = saved[3 * l : 3 * l + 3]

        def hook(n):
            if n == 1:
                send_out(proj, out_s[3 * l])
            if n == 4:
                send_out(y, out_s[3 * l + 1])
                cursor.through(ends[g_out])
                gather.finish([g_out])
                send_out(full[2 * l + 1], out_w[2 * l + 1])
            else:
                cursor.take(HOOK)

        forward_layer(sz, table_params(sz, table.at[l]), flags, u, full[2 * l], full[2 * l + 1],
                      proj, y, unext, conv, normed, nout, colb, rowt, hook=hook)
        send_out(unext, out_s[3 * l + 2])
        u = unext
    cursor.rest()
    gather.drain(range(len(groups)))
    for copy in outward:
        copy.wait()


STARTS = (0, 0, 1, 3, 4)
HOOK = 4


def forward_call(pl_, spans, u0, w_gate, w_conv, w_step, in_gain, conv_weight, conv_bias, out_gain,
                 w_out, step_bias, decay_log, skip_gain):
    sz, L = pl_.sz, pl_.L
    full = [((sz.D, sz.NP), BF16), ((sz.E, sz.D), BF16)] * L
    kept = [((sz.T, sz.NP), F32), ((sz.T, sz.E), F32), ((sz.T, sz.D), F32)] * L
    shapes = [jax.ShapeDtypeStruct(*s) for s in full + kept]
    return pl.pallas_call(
        functools.partial(forward_kernel, pl_),
        out_shape=shapes + [jax.ShapeDtypeStruct((L, TABLE_ROWS, sz.CW), F32)],
        in_specs=[SM, VM, ANY, ANY] + [VM] * 5 + [ANY] + [VM] * 3,
        out_specs=[ANY] * len(shapes) + [VM],
        scratch_shapes=[pltpu.VMEM(*s) for s in full + kept] + forward_scratch(sz) + [
            pltpu.VMEM((L, w_gate.shape[1], sz.NP), BF16),
            pltpu.VMEM((16, LANES), F32),
            pltpu.VMEM((16, LANES), BF16),
            pltpu.VMEM((16 * pl_.ndp, LANES), BF16),
            pltpu.SemaphoreType.DMA((2 * L,)),
            pltpu.SemaphoreType.DMA((len(shapes),)),
        ] + Gather.scratch(pl_.ndp, 1 + 2 * L),
        compiler_params=pltpu.CompilerParams(
            collective_id=1, has_side_effects=True, vmem_limit_bytes=ROOM
        ),
    )(spans, u0, w_gate, w_conv, w_step, in_gain, conv_weight, conv_bias, out_gain, w_out,
      step_bias, decay_log, skip_gain)


def fwd_kernel(sz, layer, spans, u, win, wout, table, proj, y, unext, conv, normed, nout, colb, rowt):
    d = lax.axis_index("dir")
    flags = run_flags(spans, d)
    forward_layer(sz, table_params(sz, table.at[layer]), flags, u.at[d] if layer == 0 else u,
                  win, wout, proj, y, unext, conv, normed, nout, colb, rowt)


def forward_scratch(sz):
    return [
        pltpu.VMEM((sz.T, sz.CW), F32),
        pltpu.VMEM((sz.T, sz.D), BF16),
        pltpu.VMEM((sz.T, sz.E), BF16),
        pltpu.VMEM((1, sz.H, sz.T, BLK), F32),
        pltpu.VMEM((2, 2, LANES, BLK), F32),
    ]


def saved_shapes(sz):
    return [
        jax.ShapeDtypeStruct((sz.T, sz.NP), F32),
        jax.ShapeDtypeStruct((sz.T, sz.E), F32),
        jax.ShapeDtypeStruct((sz.T, sz.D), F32),
    ]


def fwd_call(sz, layer, spans, u, win, wout, table):
    return pl.pallas_call(
        functools.partial(fwd_kernel, sz, layer),
        out_shape=saved_shapes(sz),
        in_specs=[SM] + [VM] * 4,
        out_specs=[VM] * 3,
        scratch_shapes=forward_scratch(sz),
        compiler_params=pltpu.CompilerParams(vmem_limit_bytes=ROOM),
    )(spans, u, win, wout, table)


def bwd_kernel(sz, layer, last, names, spans, g, u, win, wout, proj, y, table, gu, gwin, gwout,
               small, head, *rest):
    d = lax.axis_index("dir")
    flags = run_flags(spans, d)
    backward_layer(sz, table_params(sz, table.at[layer]), flags, g.at[d] if last else g,
                   u.at[d] if layer == 0 else u, win, wout, proj, y, gu, gwin, gwout, small, head,
                   dict(zip(names, rest)))


def grad_shapes(sz):
    return [
        jax.ShapeDtypeStruct((sz.T, sz.D), F32),
        jax.ShapeDtypeStruct((sz.D, sz.NP), BF16),
        jax.ShapeDtypeStruct((sz.E, sz.D), BF16),
        jax.ShapeDtypeStruct((8, sz.CW), F32),
        jax.ShapeDtypeStruct((8, LANES), F32),
    ]


def bwd_call(sz, layer, last, spans, g, u, win, wout, proj, y, table):
    s = backward_scratch(sz)
    return pl.pallas_call(
        functools.partial(bwd_kernel, sz, layer, last, tuple(s)),
        out_shape=grad_shapes(sz),
        in_specs=[SM] + [VM] * 7,
        out_specs=[VM] * 5,
        scratch_shapes=list(s.values()),
        compiler_params=pltpu.CompilerParams(vmem_limit_bytes=ROOM),
    )(spans, g, u, win, wout, proj, y, table)


class Exchange:
    def __init__(self, ring, value, buf, sems, n):
        self.r, self.buf = ring, buf
        buf[0] = value[...].astype(BF16)
        self.copy = remote(buf.at[0], buf.at[1], sems.at[0, n], sems.at[1, n], ring.mate)
        self.copy.start()

    def result(self, out):
        self.copy.wait()
        out[self.r.d] = self.buf[0].astype(out.dtype)
        out[1 - self.r.d] = self.buf[1].astype(out.dtype)


def own_small(pl_, acc, picks, outs, me):
    L, K = pl_.L, pl_.K
    for q in range(pl_.ndp):
        for n, count in enumerate((pl_.n_in, pl_.n_conv, pl_.n_out)):
            picks[q, n, :, :count] = acc[:, q * count : (q + 1) * count]
    p_in, p_conv, p_out = picks[me, 0], picks[me, 1], picks[me, 2]
    g_in, g_taps, g_bias, g_out = outs
    for l in range(L):
        r = 8 * l
        g_in[l : l + 1, :] = p_in[r : r + 1, : pl_.n_in]
        g_taps[l] = p_conv[r + 1 : r + 1 + K, : pl_.n_conv]
        g_bias[l : l + 1, :] = p_conv[r + 5 : r + 6, : pl_.n_conv]
        g_out[l : l + 1, :] = p_out[r + 6 : r + 7, : pl_.n_out]


def head_grads(pl_, acc, g_bias, g_decay, g_skip):
    sz = pl_.sz
    for l in range(pl_.L):
        r = 8 * l
        part = acc[r : r + 8, sz.CW :]
        g_bias[l : l + 1, :] = part[0:1, : 2 * sz.H]
        g_decay[l : l + 1, :] = part[1:2, : sz.H] + part[1:2, sz.H : 2 * sz.H]
        g_skip[l : l + 1, :] = part[2:3, : sz.H]


def weave(main, side):
    out, done = [], 0
    for n, call in enumerate(main):
        out.append(call)
        upto = (n + 1) * len(side) // max(len(main), 1)
        out += side[done:upto]
        done = upto
    return out + side[done:]


def scatter_kernel(pl_, nbuf, *refs):
    sz, L = pl_.sz, pl_.L
    u, g = refs[0], refs[1]
    grads = refs[2 : 2 + 2 * L]
    smalls = refs[2 + 2 * L : 2 + 3 * L]
    heads = refs[2 + 3 * L : 2 + 4 * L]
    rest = refs[2 + 4 * L :]
    (resid, grad_in, g_in, g_gate, g_conv, g_step, g_taps, g_cbias, g_sbias, g_decay, g_skip,
     g_gout, g_out) = rest[:13]
    acc, picks, whole, ubuf, gbuf, xsems = rest[13:19]
    sum_bufs = rest[19:22]
    bufs = rest[22 : 22 + nbuf]
    sems = rest[22 + nbuf :]
    ring = Ring(pl_.ndp)
    ring.barrier(ring.flips())
    parts = [pl_.rs_in, pl_.rs_out] * L
    scatter = Scatter(ring, grads, parts, bufs, sems)
    everything = range(2 * L)
    scatter.begin(everything)
    for l in range(L):
        acc[8 * l : 8 * l + 8, : sz.CW] = smalls[l][...]
        acc[8 * l : 8 * l + 8, sz.CW :] = heads[l][...]
    total = AllSum(ring, acc, sum_bufs)
    calls = weave(scatter.schedule(everything), total.schedule())
    mid = len(calls) // 3
    for call, args in calls[:mid]:
        call(*args)
    give_u = Exchange(ring, u, ubuf, xsems, 0)
    give_g = Exchange(ring, g, gbuf, xsems, 1)
    for call, args in calls[mid:]:
        call(*args)
    give_u.result(resid)
    give_g.result(grad_in)
    own_small(pl_, acc, picks, (g_in, g_taps, g_cbias, g_gout), ring.me)
    head_grads(pl_, acc, g_sbias, g_decay, g_skip)
    for l in range(L):
        scatter.result(2 * l + 1, g_out.at[l])
        scatter.result(2 * l, whole)
        g_gate[l] = whole[:, : sz.E]
        g_conv[l] = whole[:, sz.E : sz.STEP]
        g_step[l] = whole[:, sz.STEP : sz.STEP + 2 * sz.H]
    scatter.drain(everything)


def scatter_call(pl_, u, g, grads, smalls, heads):
    sz, L, ndp = pl_.sz, pl_.L, pl_.ndp
    shape = lambda *s: jax.ShapeDtypeStruct(s, F32)
    r_in, r_out = sz.D // ndp, sz.E // ndp
    out = [
        jax.ShapeDtypeStruct((2, sz.T, sz.D), BF16),
        shape(2, sz.T, sz.D),
        shape(L, pl_.n_in),
        shape(L, r_in, sz.E),
        shape(L, r_in, sz.CW),
        shape(L, r_in, 2 * sz.H),
        shape(L, pl_.K, pl_.n_conv),
        shape(L, pl_.n_conv),
        shape(L, 2 * sz.H),
        shape(L, sz.H),
        shape(L, sz.H),
        shape(L, pl_.n_out),
        shape(L, r_out, sz.D),
    ]
    bufs, sems = Scatter.scratch(ndp, [(r_in, sz.NP), (r_out, sz.D)] * L, [pl_.rs_in, pl_.rs_out] * L)
    acc_shape = (8 * L, sz.CW + LANES)
    return pl.pallas_call(
        functools.partial(scatter_kernel, pl_, len(bufs)),
        out_shape=out,
        in_specs=[VM] * (2 + 4 * L),
        out_specs=[VM] * len(out),
        scratch_shapes=[
            pltpu.VMEM(acc_shape, F32),
            pltpu.VMEM((ndp, 3, 8 * L, LANES), F32),
            pltpu.VMEM((r_in, sz.NP), F32),
            pltpu.VMEM((2, sz.T, sz.D), BF16),
            pltpu.VMEM((2, sz.T, sz.D), BF16),
            pltpu.SemaphoreType.DMA((2, 2)),
        ] + AllSum.scratch(ndp, acc_shape) + bufs + sems,
        compiler_params=pltpu.CompilerParams(
            collective_id=2, has_side_effects=True, vmem_limit_bytes=ROOM
        ),
    )(u, g, *grads, *smalls, *heads)


def pad_lanes(v, width=LANES):
    return jnp.pad(v, [(0, 0)] * (v.ndim - 1) + [(0, width - v.shape[-1])])


def plain_gather(pl_, w_gate, w_conv, w_step, in_gain, conv_weight, conv_bias, out_gain, w_out,
                 step_bias, decay_log, skip_gain):
    sz = pl_.sz
    fetch = lambda v, axis=0: lax.all_gather(v, "dp", axis=axis, tiled=True)
    shard = jnp.concatenate([w_gate, w_conv, pad_lanes(w_step)], axis=2)
    full = []
    for l in range(pl_.L):
        full += [fetch(shard[l]), fetch(w_out[l])]
    wide = lambda v: pad_lanes(v.astype(F32), sz.CW)[:, None]
    decay = jnp.exp(decay_log)
    table = jnp.concatenate(
        [wide(fetch(in_gain, 1)), fetch(conv_weight, 2).astype(F32), wide(fetch(conv_bias, 1)),
         wide(fetch(out_gain, 1)), wide(step_bias), wide(jnp.concatenate([decay, decay], 1)),
         wide(jnp.repeat(skip_gain, HD, axis=1))], axis=1)
    return full + [jnp.pad(table, ((0, 0), (0, TABLE_ROWS - table.shape[1]), (0, 0)))]


def plain_scatter(pl_, u, g, grads, smalls, heads):
    sz, K = pl_.sz, pl_.K
    me = lax.axis_index("dp")
    summed = [
        lax.psum(lax.psum_scatter(v, "dp", scatter_dimension=0, tiled=True).astype(F32), "dir")
        for v in grads
    ]
    small, head = lax.psum((jnp.stack(smalls), jnp.stack(heads)), ("dir", "dp"))
    own = lambda v, n: lax.dynamic_slice_in_dim(v, me * n, n, axis=v.ndim - 1)
    win = jnp.stack(summed[0::2])
    return (
        lax.all_gather(u.astype(BF16), "dir"),
        lax.all_gather(g, "dir"),
        own(small[:, 0], pl_.n_in),
        win[:, :, : sz.E],
        win[:, :, sz.E : sz.STEP],
        win[:, :, sz.STEP : sz.STEP + 2 * sz.H],
        own(small[:, 1 : 1 + K], pl_.n_conv),
        own(small[:, 5], pl_.n_conv),
        head[:, 0, : 2 * sz.H],
        head[:, 1, : sz.H] + head[:, 1, sz.H : 2 * sz.H],
        head[:, 2, : sz.H],
        own(small[:, 6], pl_.n_out),
        jnp.stack(summed[1::2]),
    )


def shards(resid_in, grad_out, seq_spans, in_gain, w_gate_in, w_conv_in, w_step, conv_weight,
           conv_bias, step_bias, decay_log, skip_gain, out_gain, w_out):
    layers, taps = conv_weight.shape[:2]
    ndp = lax.axis_size("dp")
    sz = Sizes(resid_in.shape[2], w_gate_in.shape[2], w_conv_in.shape[2], skip_gain.shape[1])
    pl_ = Plan(layers, taps, ndp, sz, in_gain.shape[1], conv_weight.shape[2], out_gain.shape[1])
    whole_tiles = w_gate_in.shape[1] % 16 == 0 and w_out.shape[1] % 16 == 0
    weights = (w_gate_in, w_conv_in, w_step, in_gain, conv_weight, conv_bias, out_gain, w_out,
               step_bias, decay_log, skip_gain)
    u, saved = resid_in, []
    if whole_tiles:
        got = forward_call(pl_, seq_spans, resid_in, *weights)
        win, wout, table = got[0 : 2 * layers : 2], got[1 : 2 * layers : 2], got[-1]
        for l in range(layers):
            proj, y, unext = got[2 * layers + 3 * l : 2 * layers + 3 * l + 3]
            saved.append((u, proj, y))
            u = unext
    else:
        got = plain_gather(pl_, *weights)
        win, wout, table = got[0:-1:2], got[1:-1:2], got[-1]
        for l in range(layers):
            proj, y, unext = fwd_call(sz, l, seq_spans, u, win[l], wout[l], table)
            saved.append((u, proj, y))
            u = unext
    g = grad_out
    grads, smalls, heads = [None] * (2 * layers), [None] * layers, [None] * layers
    for l in reversed(range(layers)):
        u_in, proj, y = saved[l]
        g, grads[2 * l], grads[2 * l + 1], smalls[l], heads[l] = bwd_call(
            sz, l, l == layers - 1, seq_spans, g, u_in, win[l], wout[l], proj, y, table)
    out = (scatter_call if whole_tiles else plain_scatter)(pl_, u, g, grads, smalls, heads)
    return tuple(out)


def solution(mesh):
    rows, cols_, last = P(None, "dp", None), P(None, "dp"), P(None, None, "dp")
    placed = (rows, rows, cols_, cols_, rows, rows, rows, last, cols_, P(), P(), P(), cols_, rows)
    out = (rows, rows, cols_, rows, rows, rows, last, cols_, P(), P(), P(), cols_, rows)
    return jax.shard_map(shards, mesh=mesh, in_specs=placed, out_specs=out, check_vma=False)
```

```python
import functools
import jax
import jax.numpy as jnp
from jax import lax
from jax.experimental import pallas as pl
from jax.experimental.pallas import tpu as pltpu
from jax.sharding import PartitionSpec as P

BLK = 128
HD = 64
F32 = jnp.float32
BF16 = jnp.bfloat16
HIGH = lax.Precision.HIGHEST
LANES = 128


def mm(a, b):
    return lax.dot_general(a, b, (((1,), (0,)), ((), ())), preferred_element_type=F32)


def mm_nt(a, b):
    return lax.dot_general(a, b, (((1,), (1,)), ((), ())), preferred_element_type=F32)


def mm_tn(a, b):
    return lax.dot_general(a, b, (((0,), (0,)), ((), ())), preferred_element_type=F32)


def mm_exact(a, b):
    return lax.dot_general(
        a, b, (((1,), (0,)), ((), ())), precision=HIGH, preferred_element_type=F32
    )


def iota(shape, dim):
    return lax.broadcasted_iota(jnp.int32, shape, dim)


def square_masks():
    row, col = iota((BLK, BLK), 0), iota((BLK, BLK), 1)
    return row, col


def lag_keep(keep1, lag, rows=2 * BLK):
    at = iota((rows, 1), 0)
    first = (at >= lag).astype(F32)
    edge = ((at >= BLK) & (at < BLK + lag)).astype(F32)
    return first - edge * (1.0 - keep1)


def silu(v):
    return v * jax.nn.sigmoid(v)


class Sizes:
    def __init__(self, width, inner, convw, heads):
        self.D, self.E, self.CW, self.H = width, inner, convw, heads
        self.NP = inner + convw + LANES
        self.STEP = inner + convw
        self.T = 2 * BLK


CHUNK = 1536


def spread_matrix(head0, base, width):
    row = iota((LANES, width), 0)
    col = iota((LANES, width), 1)
    return (row % 64 == col // HD + (base + head0)).astype(BF16)


def halves(values):
    high = values.astype(BF16).astype(F32)
    low = values - high
    lane = iota(values.shape, 1)
    return jnp.where(lane < 64, high, pltpu.roll(low, 64, 1)).astype(BF16)


def conv_phase(sz, cin_of, taps, bias, keep1, out_ref, slope_ref):
    keeps = [None] + [lag_keep(keep1, k) for k in range(1, 4)]

    def chunk(n, _):
        at = pl.ds(pl.multiple_of(n * LANES, LANES), LANES)
        cin = cin_of(n)
        z = bias[:, at] + taps[0:1, at] * cin
        for k in range(1, 4):
            z = z + taps[k : k + 1, at] * (pltpu.roll(cin, k, 0) * keeps[k])
        sig = jax.nn.sigmoid(z)
        act = z * sig
        out_ref[:, at] = act
        if slope_ref is not None:
            slope_ref[:, at] = (sig + act * (1.0 - sig)).astype(slope_ref.dtype)
        return 0

    lax.fori_loop(0, sz.CW // LANES, chunk, 0)


def step_phase(sz, raw, sbias, decay):
    z = raw + sbias
    dt = jnp.maximum(z, 0.0) + jnp.log1p(jnp.exp(-jnp.abs(z)))
    a = -dt * decay
    row, col = square_masks()
    lower = (row >= col).astype(F32)
    upper = (row <= col).astype(F32)
    lane = iota((BLK, LANES), 1)
    sums = []
    for b in range(2):
        part = a[b * BLK : (b + 1) * BLK]
        down, up = mm_exact(lower, part), mm_exact(upper, part)
        sums.append(jnp.where(lane < sz.H, down, up))
    return z, dt, a, sums


def b_and_c(sz, conv_ref):
    lane = iota((sz.T, LANES), 1)
    out = []
    for way in range(2):
        pair = conv_ref[:, sz.E + way * LANES : sz.E + (way + 1) * LANES]
        bp = jnp.where(lane < 64, pair, 0.0)
        cp = jnp.where(lane < 64, pltpu.roll(pair, 64, 1), 0.0)
        cp = pltpu.roll(cp, 1 if way == 0 else sz.T - 1, 0)
        out.append((bp.astype(BF16), cp.astype(BF16)))
    return out


def blk(v, b):
    return v[b * BLK : (b + 1) * BLK]


def carry_weights(sz, dt, sums):
    end0 = jnp.exp(sums[0][BLK - 1 : BLK, :] - sums[0])
    end1 = jnp.exp(sums[1][0:1, :] - sums[1])
    lane = iota((BLK, LANES), 1)
    fwd = jnp.where(lane < sz.H, end0, 0.0)
    rev = jnp.where((lane >= sz.H) & (lane < 2 * sz.H), end1, 0.0)
    return fwd, rev


def forward_scan(sz, conv_ref, y_ref, colb, rowt, bc, dt, a, sums, keep1):
    row, col = square_masks()
    low = row > col
    (bf, cf), (bb, cb) = bc
    excl = [sums[b] - blk(a, b) for b in range(2)]
    scores = []
    for b in range(2):
        sf = mm_nt(blk(cf, b), blk(bf, b))
        sb = mm_nt(blk(cb, b), blk(bb, b))
        scores.append(jnp.where(low, sf, jnp.where(row < col, sb, 0.0)))
        rowt[0, b] = sums[b].T
        rowt[1, b] = blk(dt, b).T
        for h in range(sz.H):
            ef = jnp.broadcast_to(excl[b][:, h : h + 1], (BLK, BLK))
            eb = jnp.broadcast_to(excl[b][:, sz.H + h : sz.H + h + 1], (BLK, BLK))
            colb[0, h, b * BLK : (b + 1) * BLK] = jnp.where(low, ef, eb)
    left = iota((BLK, LANES), 1) < HD

    def pair(p, _):
        at = pl.ds(pl.multiple_of(p * LANES, LANES), LANES)
        for b in range(2):
            rows = slice(b * BLK, (b + 1) * BLK)
            x = conv_ref[rows, at].astype(BF16)
            ys = []
            for hh in range(2):
                h = 2 * p + hh
                sum_row = jnp.where(low, rowt[0, b, pl.ds(h, 1)], rowt[0, b, pl.ds(sz.H + h, 1)])
                dt_row = jnp.where(low, rowt[1, b, pl.ds(h, 1)], rowt[1, b, pl.ds(sz.H + h, 1)])
                decay = jnp.exp(jnp.minimum(colb[0, h, rows] - sum_row, 0.0))
                mix = decay * scores[b] * dt_row
                ys.append(mm(mix.astype(BF16), x))
            y_ref[rows, at] = jnp.where(left, ys[0], ys[1])
        return 0

    lax.fori_loop(0, sz.H // 2, pair, 0, unroll=2)
    ends = carry_weights(sz, dt, sums)
    for way, (src, dst) in enumerate(((0, 1), (1, 0))):
        bw, cw = bc[way]
        weight = halves(ends[way] * blk(dt, src))
        enter = halves(jnp.exp(excl[dst]))
        rows_s, rows_d = slice(src * BLK, (src + 1) * BLK), slice(dst * BLK, (dst + 1) * BLK)
        for c0 in range(0, sz.E, CHUNK):
            at = slice(c0, c0 + CHUNK)
            matrix = spread_matrix(c0 // HD, sz.H * way, CHUNK)
            xw = (conv_ref[rows_s, at] * mm(weight, matrix)).astype(BF16)
            state = (mm_tn(blk(bw, src), xw) * keep1).astype(BF16)
            y_ref[rows_d, at] += mm(blk(cw, dst), state) * mm(enter, matrix)


ROWS = 64
SEGMENTS = 4


def row_loop(sz, body, init):
    def step(n, carry):
        return body(pl.ds(pl.multiple_of(n * ROWS, ROWS), ROWS), n, carry)

    return lax.fori_loop(0, sz.T // ROWS, step, init)


def live_rows(n, live1):
    later = (n >= BLK // ROWS).astype(F32)
    return 1.0 + later * (live1 - 1.0)


def norm_in(sz, u_ref, gain, normed_ref):
    def body(at, n, _):
        u = u_ref[at, :].astype(F32)
        r = lax.rsqrt(jnp.mean(u * u, axis=-1, keepdims=True) + 1e-05)
        normed_ref[at, :] = (u * r * gain[...]).astype(BF16)
        return 0

    row_loop(sz, body, 0)


def project(sz, normed_ref, win_ref, proj_ref, cols=None):
    width = sz.NP // 9
    normed = normed_ref[...]
    for n in range(9):
        proj_ref[:, n * width : (n + 1) * width] = mm(normed, win_ref[:, n * width : (n + 1) * width])


def gate_mix(sz, at, y_ref, conv_ref, proj_ref, skipw):
    x = conv_ref[at, : sz.E]
    gate = proj_ref[at, : sz.E]
    mixed = y_ref[at, :] + x * skipw[...]
    sig = jax.nn.sigmoid(gate)
    act = gate * sig
    gated = mixed * act
    scale = lax.rsqrt(jnp.mean(gated * gated, axis=-1, keepdims=True) + 1e-05)
    return x, gate, mixed, sig, act, gated, scale


def post_mix(sz, y_ref, conv_ref, proj_ref, skipw, gain, nout_ref):
    def body(at, n, _):
        _, _, _, _, _, gated, scale = gate_mix(sz, at, y_ref, conv_ref, proj_ref, skipw)
        nout_ref[at, :] = (gated * scale * gain[...]).astype(BF16)
        return 0

    row_loop(sz, body, 0)


def forward_layer(sz, p, flags, u_ref, win_ref, wout_ref, proj_ref, y_ref, unext_ref, conv_ref,
                  normed_ref, nout_ref, colb, rowt, slope_ref=None, hook=lambda n: None):
    keep1, live1 = flags[0], flags[1]
    norm_in(sz, u_ref, p["gain_in"], normed_ref)
    hook(0)
    project(sz, normed_ref, win_ref, proj_ref)
    hook(1)
    cin_of = lambda n: proj_ref[:, pl.ds(pl.multiple_of(sz.E + n * LANES, LANES), LANES)]
    conv_phase(sz, cin_of, p["taps"], p["cbias"], keep1, conv_ref, slope_ref)
    hook(2)
    _, dt, a, sums = step_phase(sz, proj_ref[:, sz.STEP :], p["sbias"][...], p["decay"][...])
    bc = b_and_c(sz, conv_ref)
    forward_scan(sz, conv_ref, y_ref, colb, rowt, bc, dt, a, sums, keep1)
    hook(3)
    post_mix(sz, y_ref, conv_ref, proj_ref, p["skipw"], p["gain_out"], nout_ref)
    hook(4)
    branch = mm(nout_ref[...], wout_ref[...])
    first = u_ref[:BLK, :].astype(F32) + branch[:BLK]
    second = u_ref[BLK:, :].astype(F32) + live1 * branch[BLK:]
    unext_ref[:BLK, :] = first.astype(unext_ref.dtype)
    unext_ref[BLK:, :] = second.astype(unext_ref.dtype)


def fold8(v):
    out = v[0:8]
    for n in range(1, v.shape[0] // 8):
        out = out + v[n * 8 : (n + 1) * 8]
    return out


def colsum(v):
    return jnp.sum(v, axis=0, keepdims=True)


def backward_scan(sz, conv_ref, gy_ref, gx_ref, gbc_ref, colb, rowt, accs, z, dt, a, sums, keep1,
                  decay, hook):
    row, col = square_masks()
    low = row < col
    bc = b_and_c(sz, conv_ref)
    (bf, cf), (bb, cb) = bc
    excl = [sums[b] - blk(a, b) for b in range(2)]
    scores = []
    for b in range(2):
        sf = mm_nt(blk(bf, b), blk(cf, b))
        sb = mm_nt(blk(bb, b), blk(cb, b))
        scores.append(jnp.where(low, sf, jnp.where(row > col, sb, 0.0)))
        rowt[0, b] = excl[b].T
    gscore, rho_ref, kappa_ref = accs
    gscore[...] = jnp.zeros_like(gscore)
    kappa_ref[...] = jnp.zeros_like(kappa_ref)
    rho_ref[...] = jnp.zeros_like(rho_ref)
    lane = iota((BLK, LANES), 1)
    left = lane < HD

    def pair(first, p, _):
        at = pl.ds(pl.multiple_of(p * LANES, LANES), LANES)
        for b in range(2):
            rows = slice(b * BLK, (b + 1) * BLK)
            x = conv_ref[rows, at]
            gy = gy_ref[rows, at]
            x_two = jnp.concatenate([jnp.where(left, x, 0.0), jnp.where(left, 0.0, x)], axis=0)
            w_two = mm_nt(x_two.astype(BF16), gy)
            gxs = []
            gs = gscore[rows]
            kap = kappa_ref[rows]
            for hh in range(2):
                h = 2 * p + hh
                ex_row = jnp.where(low, rowt[0, b, pl.ds(h, 1)], rowt[0, b, pl.ds(sz.H + h, 1)])
                decay_m = jnp.exp(jnp.minimum(ex_row - colb[0, h - first, rows], 0.0))
                dtc = colb[1, h - first, rows]
                w = w_two[hh * BLK : (hh + 1) * BLK]
                es = decay_m * scores[b]
                gxs.append(mm((es * dtc).astype(BF16), gy))
                gs = gs + decay_m * w * dtc
                r = es * w
                q = r * dtc
                rl = jnp.where(low, r, 0.0)
                kap = jnp.where(lane == h, jnp.sum(rl, axis=1, keepdims=True), kap)
                kap = jnp.where(lane == sz.H + h, jnp.sum(r - rl, axis=1, keepdims=True), kap)
                ql = jnp.where(low, q, 0.0)
                rho_ref[b, pl.ds(h, 1)] = colsum(ql)
                rho_ref[b, pl.ds(sz.H + h, 1)] = colsum(q - ql)
            gscore[rows] = gs
            kappa_ref[rows] = kap
            gx_ref[rows, at] += jnp.where(left, gxs[0], gxs[1])
        return 0

    count = sz.H // SEGMENTS
    for seg in range(SEGMENTS):
        first = seg * count
        for h in range(first, first + count):
            for b in range(2):
                for n, v in ((0, sums[b]), (1, blk(dt, b))):
                    vf = jnp.broadcast_to(v[:, h : h + 1], (BLK, BLK))
                    vb = jnp.broadcast_to(v[:, sz.H + h : sz.H + h + 1], (BLK, BLK))
                    colb[n, h - first, b * BLK : (b + 1) * BLK] = jnp.where(low, vf, vb)
        lax.fori_loop(first // 2, (first + count) // 2, functools.partial(pair, first), 0, unroll=3)
        hook("scan")

    ends = carry_weights(sz, dt, sums)
    values, enters = [], []
    for way, (src, dst) in enumerate(((0, 1), (1, 0))):
        bw, cw = bc[way]
        rows_s, rows_d = slice(src * BLK, (src + 1) * BLK), slice(dst * BLK, (dst + 1) * BLK)
        weight_of = halves(ends[way] * blk(dt, src))
        enter_of = halves(jnp.exp(excl[dst]))
        value = enter = gb_s = gc_d = jnp.zeros((BLK, LANES), F32)
        for c0 in range(0, sz.E, CHUNK):
            at = slice(c0, c0 + CHUNK)
            matrix = spread_matrix(c0 // HD, sz.H * way, CHUNK)
            weight = mm(weight_of, matrix)
            x = conv_ref[rows_s, at]
            xw = (x * weight).astype(BF16)
            state = (mm_tn(blk(bw, src), xw) * keep1).astype(BF16)
            gcar = gy_ref[rows_d, at].astype(F32) * mm(enter_of, matrix)
            gcar_low = gcar.astype(BF16)
            enter = enter + mm_nt((gcar * mm(blk(cw, dst), state)).astype(BF16), matrix)
            gstate = (mm_tn(blk(cw, dst), gcar_low) * keep1).astype(BF16)
            gc_d = gc_d + mm_nt(gcar_low, state)
            gb_s = gb_s + mm_nt(xw, gstate)
            bg = mm(blk(bw, src), gstate)
            gx_ref[rows_s, at] += weight * bg
            value = value + mm_nt((x * bg).astype(BF16), matrix)
        values.append(value)
        enters.append(enter)
        gb, gc = [None, None], [None, None]
        for b in range(2):
            g = gscore[b * BLK : (b + 1) * BLK]
            g = jnp.where(low if way == 0 else row > col, g, 0.0).astype(BF16)
            gb[b] = mm(g, blk(cw, b))
            gc[b] = mm_tn(g, blk(bw, b))
        gb[src] = gb[src] + gb_s
        gc[dst] = gc[dst] + gc_d
        gc_all = jnp.concatenate(gc, axis=0)
        at = iota((sz.T, 1), 0)
        if way == 0:
            gc_all = jnp.where(at == sz.T - 1, 0.0, pltpu.roll(gc_all, sz.T - 1, 0))
        else:
            gc_all = jnp.where(at == 0, 0.0, pltpu.roll(gc_all, 1, 0))
        gb_all = jnp.concatenate(gb, axis=0)
        wide_lane = iota((sz.T, LANES), 1)
        gbc_ref[:, way * LANES : (way + 1) * LANES] = jnp.where(
            wide_lane < 64, gb_all, pltpu.roll(gc_all, 64, 1)
        )

    strict_low = (row > col).astype(F32)
    strict_up = (row < col).astype(F32)
    is_f = lane < sz.H
    is_b = (lane >= sz.H) & (lane < 2 * sz.H)
    gsteps, gdecay = [], None
    for b in range(2):
        kr = kappa_ref[b * BLK : (b + 1) * BLK]
        kap = kr * blk(dt, b)
        rho = rho_ref[b].T
        if b == 1:
            rho = rho + jnp.where(is_f, enters[0], 0.0)
            zr = jnp.where(is_b, values[1], 0.0) * ends[1]
        else:
            rho = rho + jnp.where(is_b, enters[1], 0.0)
            zr = jnp.where(is_f, values[0], 0.0) * ends[0]
        zed = zr * blk(dt, b)
        diff = rho - kap
        both = jnp.concatenate([diff, zed], axis=1)
        up, down = mm_exact(strict_up, both), mm_exact(strict_low, both)
        ga = jnp.where(
            is_f, up[:, :LANES] + down[:, LANES:], down[:, :LANES] + up[:, LANES:]
        ) - kap
        ga = jnp.where(is_f | is_b, ga, 0.0)
        gdt = jnp.where(is_f | is_b, kr + zr, 0.0) - ga * decay
        gsteps.append(gdt * jax.nn.sigmoid(blk(z, b)))
        part = colsum(ga * blk(a, b))
        gdecay = part if gdecay is None else gdecay + part
    return jnp.concatenate(gsteps, axis=0), gdecay


def backward_layer(sz, p, flags, g_ref, u_ref, win_ref, wout_ref, proj_ref, y_ref, gu_ref,
                   gwin_ref, gwout_ref, small_ref, head_ref, s, hook=lambda name: None):
    keep1, live1 = flags[0], flags[1]
    conv_ref, slope_ref, gx_ref, gproj_ref = s["conv"], s["slope"], s["gx"], s["gproj"]
    D, E, CW = sz.D, sz.E, sz.CW
    hook("start")

    def mask_g(at, n, _):
        s["gb"][at, :] = (g_ref[at, :].astype(F32) * live_rows(n, live1)).astype(BF16)
        return 0

    row_loop(sz, mask_g, 0)
    hook("w_out")
    gx_ref[...] = mm_nt(s["gb"][...], wout_ref[...])
    hook("proj")
    cin_of = lambda n: proj_ref[:, pl.ds(pl.multiple_of(E + n * LANES, LANES), LANES)]
    conv_phase(sz, cin_of, p["taps"], p["cbias"], keep1, conv_ref, slope_ref)
    s["acc"][...] = jnp.zeros_like(s["acc"])
    hook("y")

    def post_back(at, n, _):
        x, gate, mixed, sig, act, gated, scale = gate_mix(sz, at, y_ref, conv_ref, proj_ref, p["skipw"])
        hat = gated * scale
        gn = gx_ref[at, :]
        s["acc"][0] += fold8(gn * hat)
        gproj_ref[at, E : 2 * E] = (hat * p["gain_out"][...]).astype(BF16)
        gh = gn * p["gain_out"][...]
        gg = scale * (gh - hat * jnp.mean(gh * hat, axis=-1, keepdims=True))
        gm = gg * act
        gproj_ref[at, :E] = (gg * mixed * (sig + act * (1.0 - sig))).astype(BF16)
        s["gy"][at, :] = gm.astype(BF16)
        gx_ref[at, :] = gm * p["skipw"][...]
        s["acc"][1] += fold8(gm * x)
        return 0

    row_loop(sz, post_back, 0)
    hook("post")
    small_ref[6:7, :E] = colsum(s["acc"][0])
    for c0 in range(0, E, 2 * LANES):
        part = mm_tn(gproj_ref[:, E + c0 : E + c0 + 2 * LANES], s["gb"][...])
        gwout_ref[c0 : c0 + 2 * LANES, :] = part.astype(BF16)
    hook("g_out")
    norm_in(sz, u_ref, p["gain_in"], s["normed"])
    width = sz.NP // 9
    normed = s["normed"][...]

    def grad_win(columns):
        for n in columns:
            at = slice(n * width, (n + 1) * width)
            gwin_ref[:, at] = mm_tn(normed, gproj_ref[:, at]).astype(BF16)

    grad_win(range(E // width))
    hook("g_gate")
    z, dt, a, sums = step_phase(sz, proj_ref[:, sz.STEP :], p["sbias"][...], p["decay"][...])
    gsteps, gdecay = backward_scan(
        sz, conv_ref, s["gy"], gx_ref, s["gbc"], s["colb"], s["rowt"],
        (s["gscore"], s["rho"], s["kappa"]), z, dt, a, sums, keep1, p["decay"][...], hook,
    )
    hook("scan")
    gproj_ref[:, sz.STEP :] = gsteps.astype(BF16)
    skip_sum = s["acc"][1]
    first = skip_sum.astype(BF16)
    rest = (skip_sum - first.astype(F32)).astype(BF16)
    matrix = spread_matrix(0, 0, E)
    gskip = colsum(mm_nt(first, matrix) + mm_nt(rest, matrix))
    head_ref[...] = jnp.zeros_like(head_ref)
    head_ref[0:1, :] = colsum(gsteps)
    head_ref[1:2, :] = gdecay
    head_ref[2:3, :] = gskip

    keeps = [None] + [lag_keep(keep1, k) for k in range(1, 4)]

    def conv_chunk(n, gout):
        at = pl.ds(pl.multiple_of(n * LANES, LANES), LANES)
        wide = pl.ds(pl.multiple_of(E + n * LANES, LANES), LANES)
        cin = proj_ref[:, wide]
        gz = gout * slope_ref[:, at].astype(F32)
        taps = p["taps"]
        gc = taps[0:1, at] * gz
        small_ref[1:2, at] = colsum(gz * cin)
        for k in range(1, 4):
            gk = gz * keeps[k]
            small_ref[1 + k : 2 + k, at] = colsum(gk * pltpu.roll(cin, k, 0))
            gc = gc + taps[k : k + 1, at] * pltpu.roll(gk, sz.T - k, 0)
        small_ref[5:6, at] = colsum(gz)
        gproj_ref[:, wide] = gc.astype(BF16)

    def x_chunk(n, _):
        conv_chunk(n, gx_ref[:, pl.ds(pl.multiple_of(n * LANES, LANES), LANES)])
        return 0

    lax.fori_loop(0, E // LANES, x_chunk, 0)
    for n in range((CW - E) // LANES):
        conv_chunk(E // LANES + n, s["gbc"][:, n * LANES : (n + 1) * LANES])
    hook("conv")
    grad_win(range(E // width, 9))
    hook("g_conv")
    hook("w_in")
    for n in range(9):
        at = slice(n * width, (n + 1) * width)
        part = mm_nt(gproj_ref[:, at], win_ref[:, at])
        gx_ref[:, :D] = part if n == 0 else gx_ref[:, :D] + part
    s["acc"][0] = jnp.zeros_like(s["acc"][0])
    hook("normed")

    def in_back(at, n, _):
        u = u_ref[at, :].astype(F32)
        r = lax.rsqrt(jnp.mean(u * u, axis=-1, keepdims=True) + 1e-05)
        hat = u * r
        gn = gx_ref[at, :D]
        s["acc"][0, :, :D] += fold8(gn * hat)
        gh = gn * p["gain_in"][...]
        gu = r * (gh - hat * jnp.mean(gh * hat, axis=-1, keepdims=True))
        gu_ref[at, :] = (g_ref[at, :].astype(F32) + gu).astype(gu_ref.dtype)
        return 0

    row_loop(sz, in_back, 0)
    small_ref[0:1, :D] = colsum(s["acc"][0, :, :D])
    hook("end")


def backward_scratch(sz):
    T, E, CW, D, H = sz.T, sz.E, sz.CW, sz.D, sz.H
    return dict(
        conv=pltpu.VMEM((T, CW), F32),
        slope=pltpu.VMEM((T, CW), BF16),
        normed=pltpu.VMEM((T, D), BF16),
        gb=pltpu.VMEM((T, D), BF16),
        gx=pltpu.VMEM((T, E), F32),
        gy=pltpu.VMEM((T, E), BF16),
        gproj=pltpu.VMEM((T, sz.NP), BF16),
        gbc=pltpu.VMEM((T, 2 * LANES), F32),
        acc=pltpu.VMEM((2, 8, E), F32),
        colb=pltpu.VMEM((2, H // SEGMENTS, T, BLK), F32),
        rowt=pltpu.VMEM((2, 2, LANES, BLK), F32),
        gscore=pltpu.VMEM((T, BLK), F32),
        rho=pltpu.VMEM((2, LANES, BLK), F32),
        kappa=pltpu.VMEM((T, LANES), F32),
    )


PARAMS = ("gain_in", "taps", "cbias", "sbias", "decay", "skipw", "gain_out")


MESH = pl.DeviceIdType.MESH


def remote(src, dst, ssem, rsem, device):
    return pltpu.make_async_remote_copy(
        src, dst, ssem, rsem, device_id=device, device_id_type=MESH
    )


class Ring:
    def __init__(self, ndp, both_ways=True):
        nc = ndp // 2
        self.nc, self.ndp = nc, ndp
        self.plus = nc // 2 if both_ways else nc - 1
        self.minus = nc - 1 - self.plus
        self.d, self.me = lax.axis_index("dir"), lax.axis_index("dp")
        p, self.c = self.me // 2, self.me % 2
        odd = p % 2
        self.pos = (1 - odd) * (p // 2) + odd * (nc - 1 - p // 2)
        self.turn = 1 - 2 * self.c
        self.nxt = (self.d, 2 * self.chip(1) + self.c)
        self.prv = (self.d, 2 * self.chip(-1) + self.c)
        self.sib = (self.d, 2 * p + 1 - self.c)
        self.mate = (1 - self.d, self.me)

    def chip(self, ahead):
        nc = self.nc
        pos = (self.pos + ahead * self.turn + nc) % nc
        half = pos // (nc // 2)
        return (1 - half) * 2 * pos + half * (2 * (nc - 1 - pos) + 1)

    def flip(self, bit):
        return (self.d, self.me + (1 - 2 * ((self.me // bit) % 2)) * bit)

    def flips(self):
        return [self.flip(1 << n) for n in range(self.ndp.bit_length() - 1)]

    def barrier(self, more=()):
        bar = pltpu.get_barrier_semaphore()
        greeted = (self.nxt, self.prv, self.sib, self.mate) + tuple(more)
        for device in greeted:
            pl.semaphore_signal(bar, inc=1, device_id=device, device_id_type=MESH)
        pl.semaphore_wait(bar, len(greeted))

    def hops(self):
        out = []
        for s in range(1, self.plus + 1):
            out.append((1, s))
            if s <= self.minus:
                out.append((-1, s))
        return out

    def index(self, sign, hop):
        return hop if sign > 0 else self.plus + hop


def cols(start, width):
    if isinstance(start, int):
        return pl.ds(start, width)
    return pl.ds(pl.multiple_of(start, LANES), width)


def rows_at(slot, count):
    return pl.ds(pl.multiple_of(slot * count, 16), count)


class Gather:
    def __init__(self, ring, groups, parts, sems):
        self.r, self.g, self.parts = ring, groups, parts
        self.arrive, self.beside, self.along, self.aside, self.across = sems[:5]
        self.local = sems[5]

    @staticmethod
    def scratch(ndp, groups):
        return [pltpu.SemaphoreType.DMA((3 * groups, ndp // 2))] * 5 + [
            pltpu.SemaphoreType.DMA((groups,))
        ]

    def view(self, g, ref, slot, k):
        rows = self.g[g][0].shape[0]
        w, w2 = self.parts[g]
        at = cols(2 * w, w2) if k == 1 else cols((self.r.d if k == 0 else 1 - self.r.d) * w, w)
        return ref.at[:, at] if slot is None else ref.at[rows_at(slot, rows), at]

    def copies(self, g, k, sign, hop):
        r, (src, dst) = self.r, self.g[g]
        m, n = 3 * g + k, (0 if hop == 0 else r.index(sign, hop))
        here = self.view(g, dst, 2 * r.chip(-sign * hop) + r.c, k)
        frm = self.view(g, src, None, k) if hop == 0 else here
        out = []
        if k < 2:
            for way, limit, device in ((1, r.plus, r.nxt), (-1, r.minus, r.prv)):
                if (hop == 0 or way == sign) and hop < limit:
                    to = r.index(way, hop + 1)
                    out.append(remote(frm, here, self.along.at[m, to], self.arrive.at[m, to], device))
        if k == 0 and hop > 0:
            out.append(
                remote(frm, here, self.across.at[m, n], self.arrive.at[m + 2, n], r.mate)
            )
        out.append(remote(frm, here, self.aside.at[m, n], self.beside.at[m, n], r.sib))
        return here, out

    def own(self, g):
        src, dst = self.g[g]
        return pltpu.make_async_copy(
            src, dst.at[rows_at(self.r.me, src.shape[0])], self.local.at[g]
        )

    def event(self, g, k, sign, hop):
        here, out = self.copies(g, k, sign, hop)
        if hop > 0:
            m, n = 3 * g + k, self.r.index(sign, hop)
            remote(here, here, self.along.at[m, n], self.arrive.at[m, n], self.r.nxt).wait_recv()
        for copy in out:
            copy.start()

    def kinds(self, g):
        return (0, 1, 2) if self.parts[g][0] else (1,)

    def begin(self, groups):
        for g in groups:
            for k in self.kinds(g):
                self.event(g, k, 1, 0)
            self.own(g).start()

    def rounds(self, g):
        near = {}
        for sign, hop in self.r.hops():
            near.setdefault(hop, []).append(sign)
        out, late = [[(self.begin, ([g],))]], []
        for hop, signs in near.items():
            now = [
                (self.event, (g, k, sign, hop))
                for k in self.kinds(g) if k < 2 for sign in signs
            ]
            out.append(now + late)
            late = [(self.event, (g, 2, sign, hop)) for sign in signs if 2 in self.kinds(g)]
        return out + ([late] if late else [])

    def finish(self, groups):
        r = self.r
        for g in groups:
            src, dst = self.g[g]
            for k in self.kinds(g):
                for sign, hop in [(1, 0)] + r.hops():
                    m, n = 3 * g + k, (0 if hop == 0 else r.index(sign, hop))
                    there = self.view(g, dst, 2 * r.chip(sign * hop) + 1 - r.c, k)
                    remote(
                        there, there, self.aside.at[m, n], self.beside.at[m, n], r.sib
                    ).wait_recv()
            self.own(g).wait()

    def drain(self, groups):
        for g in groups:
            for k in self.kinds(g):
                for sign, hop in [(1, 0)] + self.r.hops():
                    for copy in self.copies(g, k, sign, hop)[1]:
                        copy.wait_send()


class Scatter:
    def __init__(self, ring, groups, parts, bufs, sems):
        self.r, self.g, self.parts, self.bufs = ring, groups, parts, bufs
        (self.s_sib, self.r_sib, self.s_mate, self.r_mate, self.s_ring, self.r_ring,
         self.s_end, self.r_end) = sems

    @staticmethod
    def scratch(ndp, shapes, parts):
        nc = ndp // 2
        bufs = []
        for (rows, width), (w, w2) in zip(shapes, parts):
            bufs += [
                pltpu.VMEM((nc, rows, width), BF16),
                pltpu.VMEM((nc, rows, w), BF16),
                pltpu.VMEM((nc + 1, rows, w + w2), BF16),
                pltpu.VMEM((2, rows, w + w2), BF16),
            ]
        n = len(shapes)
        sems = [pltpu.SemaphoreType.DMA((n, nc))] * 4 + [
            pltpu.SemaphoreType.DMA((2 * n, nc + 1))
        ] * 2 + [pltpu.SemaphoreType.DMA((n,))] * 2
        return bufs, sems

    def buf(self, g):
        return self.bufs[4 * g : 4 * g + 4]

    def span(self, g, k):
        w, w2 = self.parts[g]
        if k == 1:
            return cols(2 * w, w2)
        return cols((self.r.d if k == 0 else 1 - self.r.d) * w, w)

    def packed(self, g, k):
        w, w2 = self.parts[g]
        return pl.ds(0, w) if k == 0 else pl.ds(w, w2)

    def order(self):
        r, out = self.r, []
        for s in range(r.plus):
            out.append(r.plus - s)
            if s < r.minus:
                out.append(-(r.minus - s))
        return out + [0]

    def number(self, ahead):
        return ahead % self.r.nc

    def sib_copy(self, g, ahead):
        r, own, n = self.r, self.g[g], self.number(ahead)
        sib = self.buf(g)[0]
        rows = sib.shape[1]
        src = own.at[rows_at(2 * r.chip(-ahead) + 1 - r.c, rows)]
        return remote(src, sib.at[n], self.s_sib.at[g, n], self.r_sib.at[g, n], r.sib)

    def mate_copy(self, g, ahead):
        r, n = self.r, self.number(ahead)
        sib, mate = self.buf(g)[:2]
        src = sib.at[n, :, self.span(g, 2)]
        return remote(src, mate.at[n], self.s_mate.at[g, n], self.r_mate.at[g, n], r.mate)

    def ring_copy(self, g, k, sign, step):
        r = self.r
        run = self.buf(g)[2]
        frm = run.at[self.slot(sign, step), :, self.packed(g, k)]
        to = run.at[self.slot(sign, step + 1), :, self.packed(g, k)]
        n = self.slot(sign, step + 1)
        device = r.nxt if sign > 0 else r.prv
        return remote(
            frm, to, self.s_ring.at[2 * g + k, n], self.r_ring.at[2 * g + k, n], device
        )

    def slot(self, sign, step):
        return step if sign > 0 else self.r.plus + 1 + step

    def begin(self, groups):
        for g in groups:
            for ahead in self.order():
                self.sib_copy(g, ahead).start()

    def hand_over(self, g, ahead):
        r, own, n = self.r, self.g[g], self.number(ahead)
        sib = self.buf(g)[0]
        rows = sib.shape[1]
        self.sib_copy(g, ahead).wait_recv()
        first = (2 * r.chip(ahead) + r.c) * rows
        at = self.span(g, 2)

        def part(n16, _):
            inner = pl.ds(pl.multiple_of(n16 * 16, 16), 16)
            outer = pl.ds(pl.multiple_of(first + n16 * 16, 16), 16)
            sib[n, inner, at] = (own[outer, at].astype(F32) + sib[n, inner, at].astype(F32)).astype(BF16)
            return 0

        lax.fori_loop(0, rows // 16, part, 0)
        self.mate_copy(g, ahead).start()

    def step(self, g, k, sign, step):
        r, own = self.r, self.g[g]
        sib, mate, run, end = self.buf(g)
        rows = sib.shape[1]
        last = r.plus if sign > 0 else r.minus
        ahead = sign * (last - step)
        n = self.number(ahead)
        if k == 0:
            self.mate_copy(g, ahead).wait_recv()
        if step > 0:
            self.ring_copy(g, k, sign, step - 1).wait_recv()
        first = (2 * r.chip(ahead) + r.c) * rows
        at, mine = self.span(g, k), self.packed(g, k)
        here = self.slot(sign, step)

        def part(n16, _):
            inner = pl.ds(pl.multiple_of(n16 * 16, 16), 16)
            outer = pl.ds(pl.multiple_of(first + n16 * 16, 16), 16)
            total = own[outer, at].astype(F32) + sib[n, inner, at].astype(F32)
            if k == 0:
                total = total + mate[n, inner, :].astype(F32)
            if step > 0:
                total = total + run[here, inner, mine].astype(F32)
            run[here, inner, mine] = total.astype(BF16)
            return 0

        lax.fori_loop(0, rows // 16, part, 0)
        self.ring_copy(g, k, sign, step).start()

    def own_sum(self, g):
        r, own = self.r, self.g[g]
        sib, mate, run, end = self.buf(g)
        rows = sib.shape[1]
        self.mate_copy(g, 0).wait_recv()
        for k in range(2):
            self.ring_copy(g, k, 1, r.plus - 1).wait_recv()
            self.ring_copy(g, k, -1, r.minus - 1).wait_recv()
        first = (2 * r.chip(0) + r.c) * rows

        def part(n16, _):
            inner = pl.ds(pl.multiple_of(n16 * 16, 16), 16)
            outer = pl.ds(pl.multiple_of(first + n16 * 16, 16), 16)
            for k in range(2):
                at, mine = self.span(g, k), self.packed(g, k)
                total = own[outer, at].astype(F32) + sib[0, inner, at].astype(F32)
                if k == 0:
                    total = total + mate[0, inner, :].astype(F32)
                total = total + run[self.slot(1, r.plus), inner, mine].astype(F32)
                total = total + run[self.slot(-1, r.minus), inner, mine].astype(F32)
                end[0, inner, mine] = total.astype(BF16)
            return 0

        lax.fori_loop(0, rows // 16, part, 0)
        self.end_copy(g).start()

    def end_copy(self, g):
        end = self.buf(g)[3]
        return remote(end.at[0], end.at[1], self.s_end.at[g], self.r_end.at[g], self.r.mate)

    def result(self, g, out):
        end = self.buf(g)[3]
        rows = end.shape[1]
        self.end_copy(g).wait_recv()

        def part(n16, _):
            inner = pl.ds(pl.multiple_of(n16 * 16, 16), 16)
            mine0, mine1 = self.packed(g, 0), self.packed(g, 1)
            out[inner, self.span(g, 0)] = end[0, inner, mine0].astype(F32)
            out[inner, self.span(g, 2)] = end[1, inner, mine0].astype(F32)
            out[inner, self.span(g, 1)] = end[0, inner, mine1].astype(F32) + end[1, inner, mine1].astype(F32)
            return 0

        lax.fori_loop(0, rows // 16, part, 0)

    def rounds(self, g):
        r = self.r
        over = [(self.hand_over, (g, ahead)) for ahead in self.order()]
        out, waiting = [], []
        for s in range(r.plus):
            signs = (1, -1) if s < r.minus else (1,)
            hand, over = over[: 4 if s == 0 else 2], over[4 if s == 0 else 2 :]
            steps = [(self.step, (g, 1, sign, s)) for sign in signs]
            out.append((hand if s == 0 else []) + steps + waiting + (hand if s > 0 else []))
            waiting = [(self.step, (g, 0, sign, s)) for sign in signs]
        return out + [waiting + over, [(self.own_sum, (g,))]]

    def drain(self, groups):
        r = self.r
        for g in groups:
            for ahead in self.order():
                self.sib_copy(g, ahead).wait_send()
                self.mate_copy(g, ahead).wait_send()
            for k in range(2):
                for s in range(r.plus):
                    self.ring_copy(g, k, 1, s).wait_send()
                for s in range(r.minus):
                    self.ring_copy(g, k, -1, s).wait_send()
            self.end_copy(g).wait_send()


class AllSum:
    @staticmethod
    def scratch(ndp, shape):
        n = ndp.bit_length()
        return [pltpu.VMEM((n,) + shape, F32), pltpu.SemaphoreType.DMA((n,)), pltpu.SemaphoreType.DMA((n,))]

    def __init__(self, ring, acc, bufs):
        self.acc, (self.buf, self.s, self.r) = acc, bufs
        self.partners = [ring.mate] + ring.flips()

    def copy(self, n):
        return remote(self.acc, self.buf.at[n], self.s.at[n], self.r.at[n], self.partners[n])

    def start(self, n):
        self.copy(n).start()

    def end(self, n):
        self.copy(n).wait()
        self.acc[...] += self.buf[n]

    def rounds(self):
        out = [[(self.start, (0,))]]
        for n in range(len(self.partners)):
            out.append([(self.end, (n,))])
            if n + 1 < len(self.partners):
                out[-1].append((self.start, (n + 1,)))
        return out


class Pump:
    def __init__(self):
        self.active = {}

    def add(self, key, rounds, delay=0):
        self.active[key] = [[]] * delay + list(rounds)

    def tick(self, skip=()):
        queues = [self.active[key].pop(0) for key in list(self.active) if key not in skip]
        for n in range(max([len(q) for q in queues], default=0)):
            for queue in queues:
                if n < len(queue):
                    call, args = queue[n]
                    call(*args)
        self.active = {key: rounds for key, rounds in self.active.items() if rounds}

    def until(self, *keys):
        while any(key in self.active for key in keys):
            self.tick()


VM = pl.BlockSpec(memory_space=pltpu.VMEM)
SM = pl.BlockSpec(memory_space=pltpu.SMEM)
ANY = pl.BlockSpec(memory_space=pl.ANY)
ROOM = 127 << 19
TABLE_ROWS = 16


def table_params(sz, tab):
    return dict(
        gain_in=tab.at[0:1, : sz.D],
        taps=tab.at[1:5],
        cbias=tab.at[5:6],
        gain_out=tab.at[6:7, : sz.E],
        sbias=tab.at[7:8, :LANES],
        decay=tab.at[8:9, :LANES],
        skipw=tab.at[9:10, : sz.E],
    )


def run_flags(spans, d):
    begin, opens = jnp.int32(0), jnp.int32(0)
    for s in range(spans.shape[1]):
        length = spans[d, s]
        starts = jnp.where(begin == 1, 1, 0) * jnp.where(length > 0, 1, 0)
        opens = jnp.maximum(opens, starts)
        begin = begin + length
    live = jnp.where(begin > 1, 1.0, 0.0).astype(F32)
    opened = jnp.maximum(opens.astype(F32), 1.0 - live)
    return 1.0 - opened, live


class Plan:
    def __init__(self, layers, taps, ndp, sz, n_in, n_conv, n_out):
        self.L, self.K, self.ndp, self.sz = layers, taps, ndp, sz
        self.n_in, self.n_conv, self.n_out = n_in, n_conv, n_out
        tiles_in, tiles_out = sz.NP // LANES, sz.D // LANES
        third_in, third_out = tiles_in // 3 * LANES, tiles_out // 3 * LANES
        self.ag_in = (third_in, sz.NP - 2 * third_in)
        self.ag_out = (third_out, sz.D - 2 * third_out)
        tiles = lambda width: width // LANES
        gate, rest, out = tiles(sz.E), tiles(sz.NP - sz.E), tiles(sz.D)
        cut = lambda width, part: (part * LANES, (width - 2 * part) * LANES)
        self.rs_parts = [
            [cut(out, OUT_PARTS[l]), cut(gate, GATE_PARTS[l]), cut(rest, REST_PARTS[l])]
            for l in range(layers)
        ]
        self.rs_widths = [sz.D, sz.E, sz.NP - sz.E]
        self.rs_rows = [sz.E // ndp, sz.D // ndp, sz.D // ndp]


OUT_PARTS, GATE_PARTS, REST_PARTS = (1, 1), (3, 3), (1, 3)


def stage_own(pl_, ins, stage, smallf, small, sems):
    sz = pl_.sz
    w_gate, w_conv, w_step, in_gain, conv_weight, conv_bias, out_gain = ins
    copies = []
    for l in range(pl_.L):
        copies.append(
            pltpu.make_async_copy(w_gate.at[l], stage.at[l, :, pl.ds(0, sz.E)], sems.at[2 * l])
        )
        copies.append(
            pltpu.make_async_copy(
                w_conv.at[l], stage.at[l, :, pl.ds(sz.E, sz.CW)], sems.at[2 * l + 1]
            )
        )
    for copy in copies:
        copy.start()
    smallf[...] = jnp.zeros_like(smallf)
    L, K = pl_.L, pl_.K
    smallf[0:L, : pl_.n_in] = in_gain[...].astype(F32)
    for l in range(L):
        smallf[L + l * K : L + (l + 1) * K, : pl_.n_conv] = conv_weight[l].astype(F32)
    smallf[L + L * K : 2 * L + L * K, : pl_.n_conv] = conv_bias[...].astype(F32)
    smallf[2 * L + L * K : 3 * L + L * K, : pl_.n_out] = out_gain[...].astype(F32)
    small[...] = smallf[...].astype(BF16)
    for l in range(L):
        stage[l, :, sz.STEP :] = jnp.zeros((stage.shape[1], LANES), BF16)
        stage[l, :, sz.STEP : sz.STEP + 2 * sz.H] = w_step[l]
    for copy in copies:
        copy.wait()


def fill_table(pl_, table, gathered, step_bias, decay_log, skip_gain):
    sz, L, K = pl_.sz, pl_.L, pl_.K
    table[...] = jnp.zeros_like(table)
    rows = gathered.shape[0] // pl_.ndp
    for q in range(pl_.ndp):
        part = gathered[q * rows : (q + 1) * rows, :].astype(F32)
        for l in range(L):
            table[l, 0:1, q * pl_.n_in : (q + 1) * pl_.n_in] = part[l : l + 1, : pl_.n_in]
            conv = slice(q * pl_.n_conv, (q + 1) * pl_.n_conv)
            table[l, 1 : 1 + K, conv] = part[L + l * K : L + (l + 1) * K, : pl_.n_conv]
            at = L + L * K + l
            table[l, 5:6, conv] = part[at : at + 1, : pl_.n_conv]
            out = slice(q * pl_.n_out, (q + 1) * pl_.n_out)
            table[l, 6:7, out] = part[at + L : at + L + 1, : pl_.n_out]
    head_of = iota((sz.H, sz.E), 1) // HD
    one_hot = (iota((sz.H, sz.E), 0) == head_of).astype(F32)
    wide = mm_exact(skip_gain[...], one_hot)
    decay = jnp.exp(decay_log[...])
    for l in range(L):
        table[l, 7:8, : 2 * sz.H] = step_bias[l : l + 1, :]
        table[l, 8:9, : sz.H] = decay[l : l + 1]
        table[l, 8:9, sz.H : 2 * sz.H] = decay[l : l + 1]
        table[l, 9:10, : sz.E] = wide[l : l + 1]


def forward_kernel(pl_, *refs):
    sz, L = pl_.sz, pl_.L
    (spans, u0, w_gate, w_conv, w_step, in_gain, conv_weight, conv_bias, out_gain, w_out,
     step_bias, decay_log, skip_gain) = refs[:13]
    out_w = refs[13 : 13 + 2 * L]
    out_s = refs[13 + 2 * L : 13 + 5 * L]
    table = refs[13 + 5 * L]
    rest = refs[14 + 5 * L :]
    full, rest = rest[: 2 * L], rest[2 * L :]
    saved, rest = rest[: 3 * L], rest[3 * L :]
    conv, normed, nout, colb, rowt, stage, smallf, small, gathered, own_sems, out_sems = rest[:11]
    sems = rest[11:]
    ring = Ring(pl_.ndp)
    ring.barrier()
    flags = run_flags(spans, ring.d)
    stage_own(pl_, (w_gate, w_conv, w_step, in_gain, conv_weight, conv_bias, out_gain),
              stage, smallf, small, own_sems)
    groups, parts = [(small, gathered)], [(0, LANES)]
    for l in range(L):
        groups += [(stage.at[l], full[2 * l]), (w_out.at[l], full[2 * l + 1])]
        parts += [pl_.ag_in, pl_.ag_out]
    gather = Gather(ring, groups, parts, sems)
    pump = Pump()
    for g, start in enumerate(STARTS):
        pump.add(g, gather.rounds(g), start)
    pump.until(0, 1)
    gather.finish([0])
    fill_table(pl_, table, gathered, step_bias, decay_log, skip_gain)
    outward = []

    def send_out(src, dst):
        copy = pltpu.make_async_copy(src, dst, out_sems.at[len(outward)])
        copy.start()
        outward.append(copy)

    u = u0.at[ring.d]
    for l in range(L):
        g_in, g_out = 1 + 2 * l, 2 + 2 * l
        pump.until(g_in)
        gather.finish([g_in])
        send_out(full[2 * l], out_w[2 * l])
        proj, y, unext = saved[3 * l : 3 * l + 3]

        def hook(n):
            if n == 1:
                send_out(proj, out_s[3 * l])
            if n == 4:
                send_out(y, out_s[3 * l + 1])
                pump.until(g_out)
                gather.finish([g_out])
                send_out(full[2 * l + 1], out_w[2 * l + 1])
            elif n in TICKS_F:
                pump.tick()

        forward_layer(sz, table_params(sz, table.at[l]), flags, u, full[2 * l], full[2 * l + 1],
                      proj, y, unext, conv, normed, nout, colb, rowt, hook=hook)
        send_out(unext, out_s[3 * l + 2])
        u = unext
    gather.drain(range(len(groups)))
    for copy in outward:
        copy.wait()


STARTS = (0, 0, 1, 3, 4)
TICKS_F = (0, 2, 3)


def forward_call(pl_, spans, u0, w_gate, w_conv, w_step, in_gain, conv_weight, conv_bias, out_gain,
                 w_out, step_bias, decay_log, skip_gain):
    sz, L = pl_.sz, pl_.L
    full = [((sz.D, sz.NP), BF16), ((sz.E, sz.D), BF16)] * L
    kept = []
    for l in range(L):
        kept += [((sz.T, sz.NP), F32), ((sz.T, sz.E), F32), ((sz.T, sz.D), BF16 if l == L - 1 else F32)]
    shapes = [jax.ShapeDtypeStruct(*s) for s in full + kept]
    return pl.pallas_call(
        functools.partial(forward_kernel, pl_),
        out_shape=shapes + [jax.ShapeDtypeStruct((L, TABLE_ROWS, sz.CW), F32)],
        in_specs=[SM, VM, ANY, ANY] + [VM] * 5 + [ANY] + [VM] * 3,
        out_specs=[ANY] * len(shapes) + [VM],
        scratch_shapes=[pltpu.VMEM(*s) for s in full + kept] + forward_scratch(sz) + [
            pltpu.VMEM((L, w_gate.shape[1], sz.NP), BF16),
            pltpu.VMEM((16, LANES), F32),
            pltpu.VMEM((16, LANES), BF16),
            pltpu.VMEM((16 * pl_.ndp, LANES), BF16),
            pltpu.SemaphoreType.DMA((2 * L,)),
            pltpu.SemaphoreType.DMA((len(shapes),)),
        ] + Gather.scratch(pl_.ndp, 1 + 2 * L),
        compiler_params=pltpu.CompilerParams(
            collective_id=1, has_side_effects=True, vmem_limit_bytes=ROOM
        ),
    )(spans, u0, w_gate, w_conv, w_step, in_gain, conv_weight, conv_bias, out_gain, w_out,
      step_bias, decay_log, skip_gain)


def fwd_kernel(sz, layer, spans, u, win, wout, table, proj, y, unext, conv, normed, nout, colb, rowt):
    d = lax.axis_index("dir")
    flags = run_flags(spans, d)
    forward_layer(sz, table_params(sz, table.at[layer]), flags, u.at[d] if layer == 0 else u,
                  win, wout, proj, y, unext, conv, normed, nout, colb, rowt)


def forward_scratch(sz):
    return [
        pltpu.VMEM((sz.T, sz.CW), F32),
        pltpu.VMEM((sz.T, sz.D), BF16),
        pltpu.VMEM((sz.T, sz.E), BF16),
        pltpu.VMEM((1, sz.H, sz.T, BLK), F32),
        pltpu.VMEM((2, 2, LANES, BLK), F32),
    ]


def saved_shapes(sz):
    return [
        jax.ShapeDtypeStruct((sz.T, sz.NP), F32),
        jax.ShapeDtypeStruct((sz.T, sz.E), F32),
        jax.ShapeDtypeStruct((sz.T, sz.D), F32),
    ]


def fwd_call(sz, layer, spans, u, win, wout, table):
    return pl.pallas_call(
        functools.partial(fwd_kernel, sz, layer),
        out_shape=saved_shapes(sz),
        in_specs=[SM] + [VM] * 4,
        out_specs=[VM] * 3,
        scratch_shapes=forward_scratch(sz),
        compiler_params=pltpu.CompilerParams(vmem_limit_bytes=ROOM),
    )(spans, u, win, wout, table)


def bwd_kernel(sz, layer, last, names, spans, g, u, win, wout, proj, y, table, gu, gwin, gwout,
               small, head, *rest):
    d = lax.axis_index("dir")
    flags = run_flags(spans, d)
    backward_layer(sz, table_params(sz, table.at[layer]), flags, g.at[d] if last else g,
                   u.at[d] if layer == 0 else u, win, wout, proj, y, gu, gwin, gwout, small, head,
                   dict(zip(names, rest)))


def grad_shapes(sz):
    return [
        jax.ShapeDtypeStruct((sz.T, sz.D), F32),
        jax.ShapeDtypeStruct((sz.D, sz.NP), BF16),
        jax.ShapeDtypeStruct((sz.E, sz.D), BF16),
        jax.ShapeDtypeStruct((8, sz.CW), F32),
        jax.ShapeDtypeStruct((8, LANES), F32),
    ]


def bwd_call(sz, layer, last, spans, g, u, win, wout, proj, y, table):
    s = backward_scratch(sz)
    return pl.pallas_call(
        functools.partial(bwd_kernel, sz, layer, last, tuple(s)),
        out_shape=grad_shapes(sz),
        in_specs=[SM] + [VM] * 7,
        out_specs=[VM] * 5,
        scratch_shapes=list(s.values()),
        compiler_params=pltpu.CompilerParams(vmem_limit_bytes=ROOM),
    )(spans, g, u, win, wout, proj, y, table)


def own_small(pl_, acc, picks, outs, me):
    L, K = pl_.L, pl_.K
    for q in range(pl_.ndp):
        for n, count in enumerate((pl_.n_in, pl_.n_conv, pl_.n_out)):
            for l in range(L):
                at = 8 * (L * q + l)
                picks[0, n, at : at + 8, :count] = acc[l, :, q * count : (q + 1) * count]
    mine = rows_at(me, 8 * L)
    p_in, p_conv, p_out = picks[0, 0, mine, :], picks[0, 1, mine, :], picks[0, 2, mine, :]
    g_in, g_taps, g_bias, g_out = outs
    for l in range(L):
        r = 8 * l
        g_in[l : l + 1, :] = p_in[r : r + 1, : pl_.n_in]
        g_taps[l] = p_conv[r + 1 : r + 1 + K, : pl_.n_conv]
        g_bias[l : l + 1, :] = p_conv[r + 5 : r + 6, : pl_.n_conv]
        g_out[l : l + 1, :] = p_out[r + 6 : r + 7, : pl_.n_out]


def head_grads(pl_, acc, g_bias, g_decay, g_skip):
    sz = pl_.sz
    for l in range(pl_.L):
        part = acc[l, :, sz.CW :]
        g_bias[l : l + 1, :] = part[0:1, : 2 * sz.H]
        g_decay[l : l + 1, :] = part[1:2, : sz.H] + part[1:2, sz.H : 2 * sz.H]
        g_skip[l : l + 1, :] = part[2:3, : sz.H]


TICKS = ("proj", "post", "scan1", "scan3", "conv", "normed")


def backward_kernel(pl_, names, nbuf, *refs):
    sz, L = pl_.sz, pl_.L
    E = sz.E
    spans, resid_in, grad_out, resid2, table = refs[:5]
    weights = refs[5 : 5 + 2 * L]
    kept = refs[5 + 2 * L : 5 + 5 * L - 1]
    rest = refs[4 + 5 * L :]
    (resid, grad_in, g_in, g_gate, g_conv, g_step, g_taps, g_cbias, g_sbias, g_decay, g_skip,
     g_gout, g_out) = rest[:13]
    wi1, wo0, wo1, gi1, go1, proj, y, u1, u0, g1, gbuf, accs, load_sems, xsems = rest[13:27]
    sum_bufs, rest = rest[27 : 27 + 3 * L], rest[27 + 3 * L :]
    s = dict(zip(names, rest[: len(names)]))
    rest = rest[len(names) :]
    picks, whole = s["colb"], proj.at[0 : g_conv.shape[1], 0 : sz.NP - E]
    bufs, sems = rest[:nbuf], rest[nbuf:]
    ring = Ring(pl_.ndp)
    flags = run_flags(spans, ring.d)
    proj0, y0, u1_hbm, proj1, y1 = kept
    loads = {}
    for n, (name, src, dst) in enumerate((
        ("wo1", weights[3], wo1), ("proj1", proj1, proj), ("y1", y1, y), ("u1", u1_hbm, u1),
        ("wi1", weights[2], wi1), ("wo0", weights[1], wo0), ("proj0", proj0, proj), ("y0", y0, y),
        ("wi0", weights[0], gi1), ("g1", grad_out.at[ring.d], g1), ("u0", resid_in.at[ring.d], u0),
    )):
        loads[name] = pltpu.make_async_copy(src, dst, load_sems.at[n])
    for name in ("g1", "wo1", "proj1", "y1", "u1", "wi1", "wo0", "u0"):
        loads[name].start()
    ring.barrier(ring.flips())
    give_u = remote(resid2, resid.at[ring.d], xsems.at[0], xsems.at[1], ring.mate)
    keep_u = pltpu.make_async_copy(resid2, resid.at[ring.d], xsems.at[4])
    give_u.start()
    keep_u.start()
    give_g = remote(gbuf.at[0], gbuf.at[1], xsems.at[2], xsems.at[3], ring.mate)

    gwin, gwout = [wi1, gi1], [wo1, go1]
    groups, parts = [], []
    for l in range(L):
        groups += [gwout[l], gwin[l].at[:, pl.ds(0, E)], gwin[l].at[:, pl.ds(E, sz.NP - E)]]
        parts += pl_.rs_parts[l]
    scatter = Scatter(ring, groups, parts, bufs, sems)
    pump = Pump()
    seen = []
    sums = [AllSum(ring, accs.at[l], sum_bufs[3 * l : 3 * l + 3]) for l in range(L)]

    def launch(g):
        scatter.begin([g])
        pump.add(g, scatter.rounds(g))

    def tick(name):
        if name == "scan":
            name = "scan%d" % len(seen)
            seen.append(name)
        else:
            seen.clear()
        if name in TICKS:
            pump.tick()

    def results(l):
        scatter.result(3 * l, g_out.at[l])
        scatter.result(3 * l + 1, g_gate.at[l])
        scatter.result(3 * l + 2, whole)
        g_conv[l] = whole[:, : sz.CW]
        g_step[l] = whole[:, sz.CW : sz.CW + 2 * sz.H]

    def hook1(name):
        if name == "start":
            loads["g1"].wait()
        elif name == "w_out":
            loads["wo1"].wait()
        elif name == "proj":
            loads["proj1"].wait()
        elif name == "y":
            loads["y1"].wait()
        elif name == "post":
            loads["y0"].start()
        elif name == "g_out":
            launch(3)
            loads["u1"].wait()
        elif name == "g_gate":
            launch(4)
        elif name == "conv":
            loads["proj0"].start()
        elif name == "g_conv":
            launch(5)
        elif name == "w_in":
            loads["wi1"].wait()
        tick(name)

    def hook0(name):
        if name == "w_out":
            loads["wo0"].wait()
        elif name == "proj":
            loads["proj0"].wait()
        elif name == "y":
            loads["y0"].wait()
            pump.add("sum1", sums[1].rounds())
        elif name == "g_out":
            launch(0)
            loads["u0"].wait()
        elif name == "g_gate":
            launch(1)
        elif name == "conv":
            pump.until(4, 5)
            scatter.drain([4, 5])
            loads["wi0"].start()
        elif name == "g_conv":
            launch(2)
        elif name == "w_in":
            loads["wi0"].wait()
        tick(name)

    for l, hook in ((1, hook1), (0, hook0)):
        small, head = accs.at[l, :, pl.ds(0, sz.CW)], accs.at[l, :, pl.ds(sz.CW, LANES)]
        if l == 1:
            backward_layer(sz, table_params(sz, table.at[l]), flags, g1, u1, wi1, wo1,
                           proj, y, u1, gi1, go1, small, head, s, hook)
        else:
            backward_layer(sz, table_params(sz, table.at[l]), flags, u1, u0, gi1, wo0,
                           proj, y, gbuf.at[0], wi1, wo1, small, head, s, hook)
    give_g.start()
    pump.add("sum0", sums[0].rounds())
    pump.tick()
    results(1)
    give_u.wait()
    keep_u.wait()
    pump.until(*list(pump.active))
    own_small(pl_, accs, picks, (g_in, g_taps, g_cbias, g_gout), ring.me)
    head_grads(pl_, accs, g_sbias, g_decay, g_skip)
    give_g.wait()
    grad_in[ring.d] = gbuf[0].astype(F32)
    grad_in[1 - ring.d] = gbuf[1].astype(F32)
    results(0)
    scatter.drain([0, 1, 2, 3])


def backward_call(pl_, spans, resid_in, grad_out, weights, kept, table):
    sz, L, ndp = pl_.sz, pl_.L, pl_.ndp
    shape = lambda *s: jax.ShapeDtypeStruct(s, F32)
    r_in, r_out = sz.D // ndp, sz.E // ndp
    out = [
        jax.ShapeDtypeStruct((2, sz.T, sz.D), BF16),
        shape(2, sz.T, sz.D),
        shape(L, pl_.n_in),
        shape(L, r_in, sz.E),
        shape(L, r_in, sz.CW),
        shape(L, r_in, 2 * sz.H),
        shape(L, pl_.K, pl_.n_conv),
        shape(L, pl_.n_conv),
        shape(L, 2 * sz.H),
        shape(L, sz.H),
        shape(L, sz.H),
        shape(L, pl_.n_out),
        shape(L, r_out, sz.D),
    ]
    shapes, parts = [], []
    for l in range(L):
        shapes += list(zip(pl_.rs_rows, pl_.rs_widths))
        parts += pl_.rs_parts[l]
    bufs, sems = Scatter.scratch(ndp, shapes, parts)
    acc = (8, sz.CW + LANES)
    s = backward_scratch(sz)
    scratch = [
        pltpu.VMEM((sz.D, sz.NP), BF16),
        pltpu.VMEM((sz.E, sz.D), BF16),
        pltpu.VMEM((sz.E, sz.D), BF16),
        pltpu.VMEM((sz.D, sz.NP), BF16),
        pltpu.VMEM((sz.E, sz.D), BF16),
        pltpu.VMEM((sz.T, sz.NP), F32),
        pltpu.VMEM((sz.T, sz.E), F32),
        pltpu.VMEM((sz.T, sz.D), F32),
        pltpu.VMEM((sz.T, sz.D), BF16),
        pltpu.VMEM((sz.T, sz.D), BF16),
        pltpu.VMEM((2, sz.T, sz.D), BF16),
        pltpu.VMEM((L,) + acc, F32),
        pltpu.SemaphoreType.DMA((11,)),
        pltpu.SemaphoreType.DMA((5,)),
    ] + AllSum.scratch(ndp, acc) * L + list(s.values()) + bufs + sems
    resid2, kept = kept[-1], kept[:-1]
    return pl.pallas_call(
        functools.partial(backward_kernel, pl_, tuple(s), len(bufs)),
        out_shape=out,
        in_specs=[SM, ANY, ANY, VM, VM] + [ANY] * (2 * L + len(kept)),
        out_specs=[ANY] + [VM] * (len(out) - 1),
        scratch_shapes=scratch,
        compiler_params=pltpu.CompilerParams(
            collective_id=2, has_side_effects=True, vmem_limit_bytes=ROOM
        ),
    )(spans, resid_in, grad_out, resid2, table, *weights, *kept)


def pad_lanes(v, width=LANES):
    return jnp.pad(v, [(0, 0)] * (v.ndim - 1) + [(0, width - v.shape[-1])])


def plain_gather(pl_, w_gate, w_conv, w_step, in_gain, conv_weight, conv_bias, out_gain, w_out,
                 step_bias, decay_log, skip_gain):
    sz = pl_.sz
    fetch = lambda v, axis=0: lax.all_gather(v, "dp", axis=axis, tiled=True)
    shard = jnp.concatenate([w_gate, w_conv, pad_lanes(w_step)], axis=2)
    full = []
    for l in range(pl_.L):
        full += [fetch(shard[l]), fetch(w_out[l])]
    wide = lambda v: pad_lanes(v.astype(F32), sz.CW)[:, None]
    decay = jnp.exp(decay_log)
    table = jnp.concatenate(
        [wide(fetch(in_gain, 1)), fetch(conv_weight, 2).astype(F32), wide(fetch(conv_bias, 1)),
         wide(fetch(out_gain, 1)), wide(step_bias), wide(jnp.concatenate([decay, decay], 1)),
         wide(jnp.repeat(skip_gain, HD, axis=1))], axis=1)
    return full + [jnp.pad(table, ((0, 0), (0, TABLE_ROWS - table.shape[1]), (0, 0)))]


def plain_scatter(pl_, u, g, grads, smalls, heads):
    sz, K = pl_.sz, pl_.K
    me = lax.axis_index("dp")
    summed = [
        lax.psum(lax.psum_scatter(v, "dp", scatter_dimension=0, tiled=True).astype(F32), "dir")
        for v in grads
    ]
    small, head = lax.psum((jnp.stack(smalls), jnp.stack(heads)), ("dir", "dp"))
    own = lambda v, n: lax.dynamic_slice_in_dim(v, me * n, n, axis=v.ndim - 1)
    win = jnp.stack(summed[0::2])
    return (
        lax.all_gather(u.astype(BF16), "dir"),
        lax.all_gather(g, "dir"),
        own(small[:, 0], pl_.n_in),
        win[:, :, : sz.E],
        win[:, :, sz.E : sz.STEP],
        win[:, :, sz.STEP : sz.STEP + 2 * sz.H],
        own(small[:, 1 : 1 + K], pl_.n_conv),
        own(small[:, 5], pl_.n_conv),
        head[:, 0, : 2 * sz.H],
        head[:, 1, : sz.H] + head[:, 1, sz.H : 2 * sz.H],
        head[:, 2, : sz.H],
        own(small[:, 6], pl_.n_out),
        jnp.stack(summed[1::2]),
    )


def shards(resid_in, grad_out, seq_spans, in_gain, w_gate_in, w_conv_in, w_step, conv_weight,
           conv_bias, step_bias, decay_log, skip_gain, out_gain, w_out):
    layers, taps = conv_weight.shape[:2]
    ndp = lax.axis_size("dp")
    sz = Sizes(resid_in.shape[2], w_gate_in.shape[2], w_conv_in.shape[2], skip_gain.shape[1])
    pl_ = Plan(layers, taps, ndp, sz, in_gain.shape[1], conv_weight.shape[2], out_gain.shape[1])
    whole_tiles = w_gate_in.shape[1] % 16 == 0 and w_out.shape[1] % 16 == 0
    weights = (w_gate_in, w_conv_in, w_step, in_gain, conv_weight, conv_bias, out_gain, w_out,
               step_bias, decay_log, skip_gain)
    u, saved = resid_in, []
    if whole_tiles:
        got = forward_call(pl_, seq_spans, resid_in, *weights)
        out = backward_call(pl_, seq_spans, resid_in, grad_out, got[: 2 * layers],
                            got[2 * layers : -1], got[-1])
        return tuple(out)
    got = plain_gather(pl_, *weights)
    win, wout, table = got[0:-1:2], got[1:-1:2], got[-1]
    for l in range(layers):
        proj, y, unext = fwd_call(sz, l, seq_spans, u, win[l], wout[l], table)
        saved.append((u, proj, y))
        u = unext
    g = grad_out
    grads, smalls, heads = [None] * (2 * layers), [None] * layers, [None] * layers
    for l in reversed(range(layers)):
        u_in, proj, y = saved[l]
        g, grads[2 * l], grads[2 * l + 1], smalls[l], heads[l] = bwd_call(
            sz, l, l == layers - 1, seq_spans, g, u_in, win[l], wout[l], proj, y, table)
    return tuple(plain_scatter(pl_, u, g, grads, smalls, heads))


def solution(mesh):
    rows, cols_, last = P(None, "dp", None), P(None, "dp"), P(None, None, "dp")
    placed = (rows, rows, cols_, cols_, rows, rows, rows, last, cols_, P(), P(), P(), cols_, rows)
    out = (rows, rows, cols_, rows, rows, rows, last, cols_, P(), P(), P(), cols_, rows)
    return jax.shard_map(shards, mesh=mesh, in_specs=placed, out_specs=out, check_vma=False)
```

```python
import functools
import jax
import jax.numpy as jnp
from jax import lax
from jax.experimental import pallas as pl
from jax.experimental.pallas import tpu as pltpu
from jax.sharding import PartitionSpec as P

BLK = 128
HD = 64
F32 = jnp.float32
BF16 = jnp.bfloat16
HIGH = lax.Precision.HIGHEST
LANES = 128


def mm(a, b):
    return lax.dot_general(a, b, (((1,), (0,)), ((), ())), preferred_element_type=F32)


def mm_nt(a, b):
    return lax.dot_general(a, b, (((1,), (1,)), ((), ())), preferred_element_type=F32)


def mm_tn(a, b):
    return lax.dot_general(a, b, (((0,), (0,)), ((), ())), preferred_element_type=F32)


def mm_exact(a, b):
    return lax.dot_general(
        a, b, (((1,), (0,)), ((), ())), precision=HIGH, preferred_element_type=F32
    )


def iota(shape, dim):
    return lax.broadcasted_iota(jnp.int32, shape, dim)


def square_masks():
    row, col = iota((BLK, BLK), 0), iota((BLK, BLK), 1)
    return row, col


def lag_keep(keep1, lag, rows=2 * BLK):
    at = iota((rows, 1), 0)
    first = (at >= lag).astype(F32)
    edge = ((at >= BLK) & (at < BLK + lag)).astype(F32)
    return first - edge * (1.0 - keep1)


def silu(v):
    return v * jax.nn.sigmoid(v)


class Sizes:
    def __init__(self, width, inner, convw, heads):
        self.D, self.E, self.CW, self.H = width, inner, convw, heads
        self.NP = inner + convw + LANES
        self.STEP = inner + convw
        self.T = 2 * BLK


CHUNK = 1536


def spread_matrix(head0, base, width):
    row = iota((LANES, width), 0)
    col = iota((LANES, width), 1)
    return (row % 64 == col // HD + (base + head0)).astype(BF16)


def halves(values):
    high = values.astype(BF16).astype(F32)
    low = values - high
    lane = iota(values.shape, 1)
    return jnp.where(lane < 64, high, pltpu.roll(low, 64, 1)).astype(BF16)


def conv_phase(sz, cin_of, taps, bias, keep1, out_ref, slope_ref):
    keeps = [None] + [lag_keep(keep1, k) for k in range(1, 4)]

    def chunk(n, _):
        at = pl.ds(pl.multiple_of(n * LANES, LANES), LANES)
        cin = cin_of(n)
        z = bias[:, at] + taps[0:1, at] * cin
        for k in range(1, 4):
            z = z + taps[k : k + 1, at] * (pltpu.roll(cin, k, 0) * keeps[k])
        sig = jax.nn.sigmoid(z)
        act = z * sig
        out_ref[:, at] = act
        if slope_ref is not None:
            slope_ref[:, at] = (sig + act * (1.0 - sig)).astype(slope_ref.dtype)
        return 0

    lax.fori_loop(0, sz.CW // LANES, chunk, 0)


def step_phase(sz, raw, sbias, decay):
    z = raw + sbias
    dt = jnp.maximum(z, 0.0) + jnp.log1p(jnp.exp(-jnp.abs(z)))
    a = -dt * decay
    row, col = square_masks()
    lower = (row >= col).astype(F32)
    upper = (row <= col).astype(F32)
    lane = iota((BLK, LANES), 1)
    sums = []
    for b in range(2):
        part = a[b * BLK : (b + 1) * BLK]
        down, up = mm_exact(lower, part), mm_exact(upper, part)
        sums.append(jnp.where(lane < sz.H, down, up))
    return z, dt, a, sums


def b_and_c(sz, conv_ref):
    lane = iota((sz.T, LANES), 1)
    out = []
    for way in range(2):
        pair = conv_ref[:, sz.E + way * LANES : sz.E + (way + 1) * LANES]
        bp = jnp.where(lane < 64, pair, 0.0)
        cp = jnp.where(lane < 64, pltpu.roll(pair, 64, 1), 0.0)
        cp = pltpu.roll(cp, 1 if way == 0 else sz.T - 1, 0)
        out.append((bp.astype(BF16), cp.astype(BF16)))
    return out


def blk(v, b):
    return v[b * BLK : (b + 1) * BLK]


def carry_weights(sz, dt, sums):
    end0 = jnp.exp(sums[0][BLK - 1 : BLK, :] - sums[0])
    end1 = jnp.exp(sums[1][0:1, :] - sums[1])
    lane = iota((BLK, LANES), 1)
    fwd = jnp.where(lane < sz.H, end0, 0.0)
    rev = jnp.where((lane >= sz.H) & (lane < 2 * sz.H), end1, 0.0)
    return fwd, rev


def forward_scan(sz, conv_ref, y_ref, colb, rowt, bc, dt, a, sums, keep1):
    row, col = square_masks()
    low = row > col
    (bf, cf), (bb, cb) = bc
    excl = [sums[b] - blk(a, b) for b in range(2)]
    scores = []
    for b in range(2):
        sf = mm_nt(blk(cf, b), blk(bf, b))
        sb = mm_nt(blk(cb, b), blk(bb, b))
        scores.append(jnp.where(low, sf, jnp.where(row < col, sb, 0.0)))
        rowt[0, b] = sums[b].T
        rowt[1, b] = blk(dt, b).T
        for h in range(sz.H):
            ef = jnp.broadcast_to(excl[b][:, h : h + 1], (BLK, BLK))
            eb = jnp.broadcast_to(excl[b][:, sz.H + h : sz.H + h + 1], (BLK, BLK))
            colb[0, h, b * BLK : (b + 1) * BLK] = jnp.where(low, ef, eb)
    left = iota((BLK, LANES), 1) < HD

    def pair(p, _):
        at = pl.ds(pl.multiple_of(p * LANES, LANES), LANES)
        for b in range(2):
            rows = slice(b * BLK, (b + 1) * BLK)
            x = conv_ref[rows, at].astype(BF16)
            ys = []
            for hh in range(2):
                h = 2 * p + hh
                sum_row = jnp.where(low, rowt[0, b, pl.ds(h, 1)], rowt[0, b, pl.ds(sz.H + h, 1)])
                dt_row = jnp.where(low, rowt[1, b, pl.ds(h, 1)], rowt[1, b, pl.ds(sz.H + h, 1)])
                decay = jnp.exp(jnp.minimum(colb[0, h, rows] - sum_row, 0.0))
                mix = decay * scores[b] * dt_row
                ys.append(mm(mix.astype(BF16), x))
            y_ref[rows, at] = jnp.where(left, ys[0], ys[1])
        return 0

    lax.fori_loop(0, sz.H // 2, pair, 0, unroll=2)
    ends = carry_weights(sz, dt, sums)
    for way, (src, dst) in enumerate(((0, 1), (1, 0))):
        bw, cw = bc[way]
        weight = halves(ends[way] * blk(dt, src))
        enter = halves(jnp.exp(excl[dst]))
        rows_s, rows_d = slice(src * BLK, (src + 1) * BLK), slice(dst * BLK, (dst + 1) * BLK)
        for c0 in range(0, sz.E, CHUNK):
            at = slice(c0, c0 + CHUNK)
            matrix = spread_matrix(c0 // HD, sz.H * way, CHUNK)
            xw = (conv_ref[rows_s, at] * mm(weight, matrix)).astype(BF16)
            state = (mm_tn(blk(bw, src), xw) * keep1).astype(BF16)
            y_ref[rows_d, at] += mm(blk(cw, dst), state) * mm(enter, matrix)


ROWS = 64
SEGMENTS = 4


def row_loop(sz, body, init):
    def step(n, carry):
        return body(pl.ds(pl.multiple_of(n * ROWS, ROWS), ROWS), n, carry)

    return lax.fori_loop(0, sz.T // ROWS, step, init)


def live_rows(n, live1):
    later = (n >= BLK // ROWS).astype(F32)
    return 1.0 + later * (live1 - 1.0)


def norm_in(sz, u_ref, gain, normed_ref):
    def body(at, n, _):
        u = u_ref[at, :].astype(F32)
        r = lax.rsqrt(jnp.mean(u * u, axis=-1, keepdims=True) + 1e-05)
        normed_ref[at, :] = (u * r * gain[...]).astype(BF16)
        return 0

    row_loop(sz, body, 0)


def project(sz, normed_ref, win_ref, proj_ref, cols=None):
    width = sz.NP // 9
    normed = normed_ref[...]
    for n in range(9):
        proj_ref[:, n * width : (n + 1) * width] = mm(normed, win_ref[:, n * width : (n + 1) * width])


def gate_mix(sz, at, y_ref, conv_ref, proj_ref, skipw):
    x = conv_ref[at, : sz.E]
    gate = proj_ref[at, : sz.E]
    mixed = y_ref[at, :] + x * skipw[...]
    sig = jax.nn.sigmoid(gate)
    act = gate * sig
    gated = mixed * act
    scale = lax.rsqrt(jnp.mean(gated * gated, axis=-1, keepdims=True) + 1e-05)
    return x, gate, mixed, sig, act, gated, scale


def post_mix(sz, y_ref, conv_ref, proj_ref, skipw, gain, nout_ref):
    def body(at, n, _):
        _, _, _, _, _, gated, scale = gate_mix(sz, at, y_ref, conv_ref, proj_ref, skipw)
        nout_ref[at, :] = (gated * scale * gain[...]).astype(BF16)
        return 0

    row_loop(sz, body, 0)


def forward_layer(sz, p, flags, u_ref, win_ref, wout_ref, proj_ref, y_ref, unext_ref, conv_ref,
                  normed_ref, nout_ref, colb, rowt, slope_ref=None, hook=lambda n: None):
    keep1, live1 = flags[0], flags[1]
    norm_in(sz, u_ref, p["gain_in"], normed_ref)
    hook(0)
    project(sz, normed_ref, win_ref, proj_ref)
    hook(1)
    cin_of = lambda n: proj_ref[:, pl.ds(pl.multiple_of(sz.E + n * LANES, LANES), LANES)]
    conv_phase(sz, cin_of, p["taps"], p["cbias"], keep1, conv_ref, slope_ref)
    hook(2)
    _, dt, a, sums = step_phase(sz, proj_ref[:, sz.STEP :], p["sbias"][...], p["decay"][...])
    bc = b_and_c(sz, conv_ref)
    forward_scan(sz, conv_ref, y_ref, colb, rowt, bc, dt, a, sums, keep1)
    hook(3)
    post_mix(sz, y_ref, conv_ref, proj_ref, p["skipw"], p["gain_out"], nout_ref)
    hook(4)
    branch = mm(nout_ref[...], wout_ref[...])
    first = u_ref[:BLK, :].astype(F32) + branch[:BLK]
    second = u_ref[BLK:, :].astype(F32) + live1 * branch[BLK:]
    unext_ref[:BLK, :] = first.astype(unext_ref.dtype)
    unext_ref[BLK:, :] = second.astype(unext_ref.dtype)


def fold8(v):
    out = v[0:8]
    for n in range(1, v.shape[0] // 8):
        out = out + v[n * 8 : (n + 1) * 8]
    return out


def colsum(v):
    return jnp.sum(v, axis=0, keepdims=True)


def backward_scan(sz, conv_ref, gy_ref, gx_ref, gbc_ref, colb, rowt, accs, z, dt, a, sums, keep1,
                  decay, hook):
    row, col = square_masks()
    low = row < col
    bc = b_and_c(sz, conv_ref)
    (bf, cf), (bb, cb) = bc
    excl = [sums[b] - blk(a, b) for b in range(2)]
    scores = []
    for b in range(2):
        sf = mm_nt(blk(bf, b), blk(cf, b))
        sb = mm_nt(blk(bb, b), blk(cb, b))
        scores.append(jnp.where(low, sf, jnp.where(row > col, sb, 0.0)))
        rowt[0, b] = excl[b].T
    gscore, rho_ref, kappa_ref = accs
    gscore[...] = jnp.zeros_like(gscore)
    kappa_ref[...] = jnp.zeros_like(kappa_ref)
    rho_ref[...] = jnp.zeros_like(rho_ref)
    lane = iota((BLK, LANES), 1)
    left = lane < HD

    def pair(first, p, _):
        at = pl.ds(pl.multiple_of(p * LANES, LANES), LANES)
        for b in range(2):
            rows = slice(b * BLK, (b + 1) * BLK)
            x = conv_ref[rows, at]
            gy = gy_ref[rows, at]
            x_two = jnp.concatenate([jnp.where(left, x, 0.0), jnp.where(left, 0.0, x)], axis=0)
            w_two = mm_nt(x_two.astype(BF16), gy)
            gxs = []
            gs = gscore[rows]
            kap = kappa_ref[rows]
            for hh in range(2):
                h = 2 * p + hh
                ex_row = jnp.where(low, rowt[0, b, pl.ds(h, 1)], rowt[0, b, pl.ds(sz.H + h, 1)])
                decay_m = jnp.exp(jnp.minimum(ex_row - colb[0, h - first, rows], 0.0))
                dtc = colb[1, h - first, rows]
                w = w_two[hh * BLK : (hh + 1) * BLK]
                es = decay_m * scores[b]
                gxs.append(mm((es * dtc).astype(BF16), gy))
                gs = gs + decay_m * w * dtc
                r = es * w
                q = r * dtc
                rl = jnp.where(low, r, 0.0)
                kap = jnp.where(lane == h, jnp.sum(rl, axis=1, keepdims=True), kap)
                kap = jnp.where(lane == sz.H + h, jnp.sum(r - rl, axis=1, keepdims=True), kap)
                ql = jnp.where(low, q, 0.0)
                rho_ref[b, pl.ds(h, 1)] = colsum(ql)
                rho_ref[b, pl.ds(sz.H + h, 1)] = colsum(q - ql)
            gscore[rows] = gs
            kappa_ref[rows] = kap
            gx_ref[rows, at] += jnp.where(left, gxs[0], gxs[1])
        return 0

    count = sz.H // SEGMENTS
    for seg in range(SEGMENTS):
        first = seg * count
        for h in range(first, first + count):
            for b in range(2):
                for n, v in ((0, sums[b]), (1, blk(dt, b))):
                    vf = jnp.broadcast_to(v[:, h : h + 1], (BLK, BLK))
                    vb = jnp.broadcast_to(v[:, sz.H + h : sz.H + h + 1], (BLK, BLK))
                    colb[n, h - first, b * BLK : (b + 1) * BLK] = jnp.where(low, vf, vb)
        lax.fori_loop(first // 2, (first + count) // 2, functools.partial(pair, first), 0, unroll=3)
        hook("scan")

    ends = carry_weights(sz, dt, sums)
    values, enters = [], []
    for way, (src, dst) in enumerate(((0, 1), (1, 0))):
        bw, cw = bc[way]
        rows_s, rows_d = slice(src * BLK, (src + 1) * BLK), slice(dst * BLK, (dst + 1) * BLK)
        weight_of = halves(ends[way] * blk(dt, src))
        enter_of = halves(jnp.exp(excl[dst]))
        value = enter = gb_s = gc_d = jnp.zeros((BLK, LANES), F32)
        for c0 in range(0, sz.E, CHUNK):
            at = slice(c0, c0 + CHUNK)
            matrix = spread_matrix(c0 // HD, sz.H * way, CHUNK)
            weight = mm(weight_of, matrix)
            x = conv_ref[rows_s, at]
            xw = (x * weight).astype(BF16)
            state = (mm_tn(blk(bw, src), xw) * keep1).astype(BF16)
            gcar = gy_ref[rows_d, at].astype(F32) * mm(enter_of, matrix)
            gcar_low = gcar.astype(BF16)
            enter = enter + mm_nt((gcar * mm(blk(cw, dst), state)).astype(BF16), matrix)
            gstate = (mm_tn(blk(cw, dst), gcar_low) * keep1).astype(BF16)
            gc_d = gc_d + mm_nt(gcar_low, state)
            gb_s = gb_s + mm_nt(xw, gstate)
            bg = mm(blk(bw, src), gstate)
            gx_ref[rows_s, at] += weight * bg
            value = value + mm_nt((x * bg).astype(BF16), matrix)
        values.append(value)
        enters.append(enter)
        gb, gc = [None, None], [None, None]
        for b in range(2):
            g = gscore[b * BLK : (b + 1) * BLK]
            g = jnp.where(low if way == 0 else row > col, g, 0.0).astype(BF16)
            gb[b] = mm(g, blk(cw, b))
            gc[b] = mm_tn(g, blk(bw, b))
        gb[src] = gb[src] + gb_s
        gc[dst] = gc[dst] + gc_d
        gc_all = jnp.concatenate(gc, axis=0)
        at = iota((sz.T, 1), 0)
        if way == 0:
            gc_all = jnp.where(at == sz.T - 1, 0.0, pltpu.roll(gc_all, sz.T - 1, 0))
        else:
            gc_all = jnp.where(at == 0, 0.0, pltpu.roll(gc_all, 1, 0))
        gb_all = jnp.concatenate(gb, axis=0)
        wide_lane = iota((sz.T, LANES), 1)
        gbc_ref[:, way * LANES : (way + 1) * LANES] = jnp.where(
            wide_lane < 64, gb_all, pltpu.roll(gc_all, 64, 1)
        )

    strict_low = (row > col).astype(F32)
    strict_up = (row < col).astype(F32)
    is_f = lane < sz.H
    is_b = (lane >= sz.H) & (lane < 2 * sz.H)
    gsteps, gdecay = [], None
    for b in range(2):
        kr = kappa_ref[b * BLK : (b + 1) * BLK]
        kap = kr * blk(dt, b)
        rho = rho_ref[b].T
        if b == 1:
            rho = rho + jnp.where(is_f, enters[0], 0.0)
            zr = jnp.where(is_b, values[1], 0.0) * ends[1]
        else:
            rho = rho + jnp.where(is_b, enters[1], 0.0)
            zr = jnp.where(is_f, values[0], 0.0) * ends[0]
        zed = zr * blk(dt, b)
        diff = rho - kap
        both = jnp.concatenate([diff, zed], axis=1)
        up, down = mm_exact(strict_up, both), mm_exact(strict_low, both)
        ga = jnp.where(
            is_f, up[:, :LANES] + down[:, LANES:], down[:, :LANES] + up[:, LANES:]
        ) - kap
        ga = jnp.where(is_f | is_b, ga, 0.0)
        gdt = jnp.where(is_f | is_b, kr + zr, 0.0) - ga * decay
        gsteps.append(gdt * jax.nn.sigmoid(blk(z, b)))
        part = colsum(ga * blk(a, b))
        gdecay = part if gdecay is None else gdecay + part
    return jnp.concatenate(gsteps, axis=0), gdecay


def backward_layer(sz, p, flags, g_ref, u_ref, win_ref, wout_ref, proj_ref, y_ref, gu_ref,
                   gwin_ref, gwout_ref, small_ref, head_ref, s, hook=lambda name: None):
    keep1, live1 = flags[0], flags[1]
    conv_ref, slope_ref, gx_ref, gproj_ref = s["conv"], s["slope"], s["gx"], s["gproj"]
    D, E, CW = sz.D, sz.E, sz.CW
    hook("start")

    def mask_g(at, n, _):
        s["gb"][at, :] = (g_ref[at, :].astype(F32) * live_rows(n, live1)).astype(BF16)
        return 0

    row_loop(sz, mask_g, 0)
    hook("w_out")
    gx_ref[...] = mm_nt(s["gb"][...], wout_ref[...])
    hook("proj")
    cin_of = lambda n: proj_ref[:, pl.ds(pl.multiple_of(E + n * LANES, LANES), LANES)]
    conv_phase(sz, cin_of, p["taps"], p["cbias"], keep1, conv_ref, slope_ref)
    s["acc"][...] = jnp.zeros_like(s["acc"])
    hook("y")

    def post_back(at, n, _):
        x, gate, mixed, sig, act, gated, scale = gate_mix(sz, at, y_ref, conv_ref, proj_ref, p["skipw"])
        hat = gated * scale
        gn = gx_ref[at, :]
        s["acc"][0] += fold8(gn * hat)
        gproj_ref[at, E : 2 * E] = (hat * p["gain_out"][...]).astype(BF16)
        gh = gn * p["gain_out"][...]
        gg = scale * (gh - hat * jnp.mean(gh * hat, axis=-1, keepdims=True))
        gm = gg * act
        gproj_ref[at, :E] = (gg * mixed * (sig + act * (1.0 - sig))).astype(BF16)
        s["gy"][at, :] = gm.astype(BF16)
        gx_ref[at, :] = gm * p["skipw"][...]
        s["acc"][1] += fold8(gm * x)
        return 0

    row_loop(sz, post_back, 0)
    hook("post")
    small_ref[6:7, :E] = colsum(s["acc"][0])
    for c0 in range(0, E, 2 * LANES):
        part = mm_tn(gproj_ref[:, E + c0 : E + c0 + 2 * LANES], s["gb"][...])
        gwout_ref[c0 : c0 + 2 * LANES, :] = part.astype(BF16)
    hook("g_out")
    norm_in(sz, u_ref, p["gain_in"], s["normed"])
    width = sz.NP // 9
    normed = s["normed"][...]

    def grad_win(columns):
        for n in columns:
            at = slice(n * width, (n + 1) * width)
            gwin_ref[:, at] = mm_tn(normed, gproj_ref[:, at]).astype(BF16)

    grad_win(range(E // width))
    hook("g_gate")
    z, dt, a, sums = step_phase(sz, proj_ref[:, sz.STEP :], p["sbias"][...], p["decay"][...])
    gsteps, gdecay = backward_scan(
        sz, conv_ref, s["gy"], gx_ref, s["gbc"], s["colb"], s["rowt"],
        (s["gscore"], s["rho"], s["kappa"]), z, dt, a, sums, keep1, p["decay"][...], hook,
    )
    hook("scan")
    gproj_ref[:, sz.STEP :] = gsteps.astype(BF16)
    skip_sum = s["acc"][1]
    first = skip_sum.astype(BF16)
    rest = (skip_sum - first.astype(F32)).astype(BF16)
    matrix = spread_matrix(0, 0, E)
    gskip = colsum(mm_nt(first, matrix) + mm_nt(rest, matrix))
    head_ref[...] = jnp.zeros_like(head_ref)
    head_ref[0:1, :] = colsum(gsteps)
    head_ref[1:2, :] = gdecay
    head_ref[2:3, :] = gskip

    keeps = [None] + [lag_keep(keep1, k) for k in range(1, 4)]

    def conv_chunk(n, gout):
        at = pl.ds(pl.multiple_of(n * LANES, LANES), LANES)
        wide = pl.ds(pl.multiple_of(E + n * LANES, LANES), LANES)
        cin = proj_ref[:, wide]
        gz = gout * slope_ref[:, at].astype(F32)
        taps = p["taps"]
        gc = taps[0:1, at] * gz
        small_ref[1:2, at] = colsum(gz * cin)
        for k in range(1, 4):
            gk = gz * keeps[k]
            small_ref[1 + k : 2 + k, at] = colsum(gk * pltpu.roll(cin, k, 0))
            gc = gc + taps[k : k + 1, at] * pltpu.roll(gk, sz.T - k, 0)
        small_ref[5:6, at] = colsum(gz)
        gproj_ref[:, wide] = gc.astype(BF16)

    def x_chunk(n, _):
        conv_chunk(n, gx_ref[:, pl.ds(pl.multiple_of(n * LANES, LANES), LANES)])
        return 0

    early = 2 * width // LANES
    lax.fori_loop(0, early, x_chunk, 0)
    hook("conv")
    grad_win(range(E // width, E // width + 2))
    hook("g_early")
    lax.fori_loop(early, E // LANES, x_chunk, 0)
    for n in range((CW - E) // LANES):
        conv_chunk(E // LANES + n, s["gbc"][:, n * LANES : (n + 1) * LANES])
    hook("conv_end")
    grad_win(range(E // width + 2, 9))
    hook("g_conv")
    hook("w_in")
    for n in range(9):
        at = slice(n * width, (n + 1) * width)
        part = mm_nt(gproj_ref[:, at], win_ref[:, at])
        gx_ref[:, :D] = part if n == 0 else gx_ref[:, :D] + part
    s["acc"][0] = jnp.zeros_like(s["acc"][0])
    hook("normed")

    def in_back(at, n, _):
        u = u_ref[at, :].astype(F32)
        r = lax.rsqrt(jnp.mean(u * u, axis=-1, keepdims=True) + 1e-05)
        hat = u * r
        gn = gx_ref[at, :D]
        s["acc"][0, :, :D] += fold8(gn * hat)
        gh = gn * p["gain_in"][...]
        gu = r * (gh - hat * jnp.mean(gh * hat, axis=-1, keepdims=True))
        gu_ref[at, :] = (g_ref[at, :].astype(F32) + gu).astype(gu_ref.dtype)
        return 0

    row_loop(sz, in_back, 0)
    small_ref[0:1, :D] = colsum(s["acc"][0, :, :D])
    hook("end")


def backward_scratch(sz):
    T, E, CW, D, H = sz.T, sz.E, sz.CW, sz.D, sz.H
    return dict(
        conv=pltpu.VMEM((T, CW), F32),
        slope=pltpu.VMEM((T, CW), BF16),
        normed=pltpu.VMEM((T, D), BF16),
        gb=pltpu.VMEM((T, D), BF16),
        gx=pltpu.VMEM((T, E), F32),
        gy=pltpu.VMEM((T, E), BF16),
        gproj=pltpu.VMEM((T, sz.NP), BF16),
        gbc=pltpu.VMEM((T, 2 * LANES), F32),
        acc=pltpu.VMEM((2, 8, E), F32),
        colb=pltpu.VMEM((2, H // SEGMENTS, T, BLK), F32),
        rowt=pltpu.VMEM((2, 2, LANES, BLK), F32),
        gscore=pltpu.VMEM((T, BLK), F32),
        rho=pltpu.VMEM((2, LANES, BLK), F32),
        kappa=pltpu.VMEM((T, LANES), F32),
    )


PARAMS = ("gain_in", "taps", "cbias", "sbias", "decay", "skipw", "gain_out")


MESH = pl.DeviceIdType.MESH


def remote(src, dst, ssem, rsem, device):
    return pltpu.make_async_remote_copy(
        src, dst, ssem, rsem, device_id=device, device_id_type=MESH
    )


class Ring:
    def __init__(self, ndp, both_ways=True):
        nc = ndp // 2
        self.nc, self.ndp = nc, ndp
        self.plus = nc // 2 if both_ways else nc - 1
        self.minus = nc - 1 - self.plus
        self.d, self.me = lax.axis_index("dir"), lax.axis_index("dp")
        p, self.c = self.me // 2, self.me % 2
        odd = p % 2
        self.pos = (1 - odd) * (p // 2) + odd * (nc - 1 - p // 2)
        self.turn = 1 - 2 * self.c
        self.nxt = (self.d, 2 * self.chip(1) + self.c)
        self.prv = (self.d, 2 * self.chip(-1) + self.c)
        self.sib = (self.d, 2 * p + 1 - self.c)
        self.mate = (1 - self.d, self.me)

    def chip(self, ahead):
        nc = self.nc
        pos = (self.pos + ahead * self.turn + nc) % nc
        half = pos // (nc // 2)
        return (1 - half) * 2 * pos + half * (2 * (nc - 1 - pos) + 1)

    def flip(self, bit):
        return (self.d, self.me + (1 - 2 * ((self.me // bit) % 2)) * bit)

    def flips(self):
        return [self.flip(1 << n) for n in range(self.ndp.bit_length() - 1)]

    def barrier(self, more=()):
        bar = pltpu.get_barrier_semaphore()
        greeted = (self.nxt, self.prv, self.sib, self.mate) + tuple(more)
        for device in greeted:
            pl.semaphore_signal(bar, inc=1, device_id=device, device_id_type=MESH)
        pl.semaphore_wait(bar, len(greeted))

    def hops(self):
        out = []
        for s in range(1, self.plus + 1):
            out.append((1, s))
            if s <= self.minus:
                out.append((-1, s))
        return out

    def index(self, sign, hop):
        return hop if sign > 0 else self.plus + hop


def cols(start, width):
    if isinstance(start, int):
        return pl.ds(start, width)
    return pl.ds(pl.multiple_of(start, LANES), width)


def rows_at(slot, count):
    return pl.ds(pl.multiple_of(slot * count, 16), count)


class Gather:
    def __init__(self, ring, groups, parts, sems):
        self.r, self.g, self.parts = ring, groups, parts
        self.arrive, self.beside, self.along, self.aside, self.across = sems[:5]
        self.local = sems[5]

    @staticmethod
    def scratch(ndp, groups):
        return [pltpu.SemaphoreType.DMA((3 * groups, ndp // 2))] * 5 + [
            pltpu.SemaphoreType.DMA((groups,))
        ]

    def view(self, g, ref, slot, k):
        rows = self.g[g][0].shape[0]
        w, w2 = self.parts[g]
        at = cols(2 * w, w2) if k == 1 else cols((self.r.d if k == 0 else 1 - self.r.d) * w, w)
        return ref.at[:, at] if slot is None else ref.at[rows_at(slot, rows), at]

    def copies(self, g, k, sign, hop):
        r, (src, dst) = self.r, self.g[g]
        m, n = 3 * g + k, (0 if hop == 0 else r.index(sign, hop))
        here = self.view(g, dst, 2 * r.chip(-sign * hop) + r.c, k)
        frm = self.view(g, src, None, k) if hop == 0 else here
        out = []
        if k < 2:
            for way, limit, device in ((1, r.plus, r.nxt), (-1, r.minus, r.prv)):
                if (hop == 0 or way == sign) and hop < limit:
                    to = r.index(way, hop + 1)
                    out.append(remote(frm, here, self.along.at[m, to], self.arrive.at[m, to], device))
        if k == 0 and hop > 0:
            out.append(
                remote(frm, here, self.across.at[m, n], self.arrive.at[m + 2, n], r.mate)
            )
        out.append(remote(frm, here, self.aside.at[m, n], self.beside.at[m, n], r.sib))
        return here, out

    def own(self, g):
        src, dst = self.g[g]
        return pltpu.make_async_copy(
            src, dst.at[rows_at(self.r.me, src.shape[0])], self.local.at[g]
        )

    def event(self, g, k, sign, hop):
        here, out = self.copies(g, k, sign, hop)
        if hop > 0:
            m, n = 3 * g + k, self.r.index(sign, hop)
            remote(here, here, self.along.at[m, n], self.arrive.at[m, n], self.r.nxt).wait_recv()
        for copy in out:
            copy.start()

    def kinds(self, g):
        return (0, 1, 2) if self.parts[g][0] else (1,)

    def begin(self, groups):
        for g in groups:
            for k in self.kinds(g):
                self.event(g, k, 1, 0)
            self.own(g).start()

    def rounds(self, g):
        near = {}
        for sign, hop in self.r.hops():
            near.setdefault(hop, []).append(sign)
        out, late = [[(self.begin, ([g],))]], []
        for hop, signs in near.items():
            now = [
                (self.event, (g, k, sign, hop))
                for k in self.kinds(g) if k < 2 for sign in signs
            ]
            out.append(now + late)
            late = [(self.event, (g, 2, sign, hop)) for sign in signs if 2 in self.kinds(g)]
        return out + ([late] if late else [])

    def finish(self, groups):
        r = self.r
        for g in groups:
            src, dst = self.g[g]
            for k in self.kinds(g):
                for sign, hop in [(1, 0)] + r.hops():
                    m, n = 3 * g + k, (0 if hop == 0 else r.index(sign, hop))
                    there = self.view(g, dst, 2 * r.chip(sign * hop) + 1 - r.c, k)
                    remote(
                        there, there, self.aside.at[m, n], self.beside.at[m, n], r.sib
                    ).wait_recv()
            self.own(g).wait()

    def drain(self, groups):
        for g in groups:
            for k in self.kinds(g):
                for sign, hop in [(1, 0)] + self.r.hops():
                    for copy in self.copies(g, k, sign, hop)[1]:
                        copy.wait_send()


class Scatter:
    def __init__(self, ring, groups, parts, bufs, sems):
        self.r, self.g, self.parts, self.bufs = ring, groups, parts, bufs
        (self.s_sib, self.r_sib, self.s_mate, self.r_mate, self.s_ring, self.r_ring,
         self.s_end, self.r_end) = sems

    @staticmethod
    def scratch(ndp, shapes, parts):
        nc = ndp // 2
        bufs = []
        for (rows, width), (w, w2) in zip(shapes, parts):
            bufs += [
                pltpu.VMEM((nc, rows, width), BF16),
                pltpu.VMEM((nc, rows, w), BF16),
                pltpu.VMEM((nc + 1, rows, w + w2), BF16),
                pltpu.VMEM((2, rows, w + w2), BF16),
            ]
        n = len(shapes)
        sems = [pltpu.SemaphoreType.DMA((n, nc))] * 4 + [
            pltpu.SemaphoreType.DMA((2 * n, nc + 1))
        ] * 2 + [pltpu.SemaphoreType.DMA((n,))] * 2
        return bufs, sems

    def buf(self, g):
        return self.bufs[4 * g : 4 * g + 4]

    def span(self, g, k):
        w, w2 = self.parts[g]
        if k == 1:
            return cols(2 * w, w2)
        return cols((self.r.d if k == 0 else 1 - self.r.d) * w, w)

    def packed(self, g, k):
        w, w2 = self.parts[g]
        return pl.ds(0, w) if k == 0 else pl.ds(w, w2)

    def order(self):
        r, out = self.r, []
        for s in range(r.plus):
            out.append(r.plus - s)
            if s < r.minus:
                out.append(-(r.minus - s))
        return out + [0]

    def number(self, ahead):
        return ahead % self.r.nc

    def sib_copy(self, g, ahead):
        r, own, n = self.r, self.g[g], self.number(ahead)
        sib = self.buf(g)[0]
        rows = sib.shape[1]
        src = own.at[rows_at(2 * r.chip(-ahead) + 1 - r.c, rows)]
        return remote(src, sib.at[n], self.s_sib.at[g, n], self.r_sib.at[g, n], r.sib)

    def mate_copy(self, g, ahead):
        r, n = self.r, self.number(ahead)
        sib, mate = self.buf(g)[:2]
        src = sib.at[n, :, self.span(g, 2)]
        return remote(src, mate.at[n], self.s_mate.at[g, n], self.r_mate.at[g, n], r.mate)

    def ring_copy(self, g, k, sign, step):
        r = self.r
        run = self.buf(g)[2]
        frm = run.at[self.slot(sign, step), :, self.packed(g, k)]
        to = run.at[self.slot(sign, step + 1), :, self.packed(g, k)]
        n = self.slot(sign, step + 1)
        device = r.nxt if sign > 0 else r.prv
        return remote(
            frm, to, self.s_ring.at[2 * g + k, n], self.r_ring.at[2 * g + k, n], device
        )

    def slot(self, sign, step):
        return step if sign > 0 else self.r.plus + 1 + step

    def begin(self, groups):
        for g in groups:
            for ahead in self.order():
                self.sib_copy(g, ahead).start()

    def hand_over(self, g, ahead):
        r, own, n = self.r, self.g[g], self.number(ahead)
        sib = self.buf(g)[0]
        rows = sib.shape[1]
        self.sib_copy(g, ahead).wait_recv()
        first = (2 * r.chip(ahead) + r.c) * rows
        at = self.span(g, 2)

        def part(n16, _):
            inner = pl.ds(pl.multiple_of(n16 * 16, 16), 16)
            outer = pl.ds(pl.multiple_of(first + n16 * 16, 16), 16)
            sib[n, inner, at] = (own[outer, at].astype(F32) + sib[n, inner, at].astype(F32)).astype(BF16)
            return 0

        lax.fori_loop(0, rows // 16, part, 0)
        self.mate_copy(g, ahead).start()

    def step(self, g, k, sign, step):
        r, own = self.r, self.g[g]
        sib, mate, run, end = self.buf(g)
        rows = sib.shape[1]
        last = r.plus if sign > 0 else r.minus
        ahead = sign * (last - step)
        n = self.number(ahead)
        if k == 0:
            self.mate_copy(g, ahead).wait_recv()
        if step > 0:
            self.ring_copy(g, k, sign, step - 1).wait_recv()
        first = (2 * r.chip(ahead) + r.c) * rows
        at, mine = self.span(g, k), self.packed(g, k)
        here = self.slot(sign, step)

        def part(n16, _):
            inner = pl.ds(pl.multiple_of(n16 * 16, 16), 16)
            outer = pl.ds(pl.multiple_of(first + n16 * 16, 16), 16)
            total = own[outer, at].astype(F32) + sib[n, inner, at].astype(F32)
            if k == 0:
                total = total + mate[n, inner, :].astype(F32)
            if step > 0:
                total = total + run[here, inner, mine].astype(F32)
            run[here, inner, mine] = total.astype(BF16)
            return 0

        lax.fori_loop(0, rows // 16, part, 0)
        self.ring_copy(g, k, sign, step).start()

    def own_sum(self, g):
        r, own = self.r, self.g[g]
        sib, mate, run, end = self.buf(g)
        rows = sib.shape[1]
        self.mate_copy(g, 0).wait_recv()
        for k in range(2):
            self.ring_copy(g, k, 1, r.plus - 1).wait_recv()
            self.ring_copy(g, k, -1, r.minus - 1).wait_recv()
        first = (2 * r.chip(0) + r.c) * rows

        def part(n16, _):
            inner = pl.ds(pl.multiple_of(n16 * 16, 16), 16)
            outer = pl.ds(pl.multiple_of(first + n16 * 16, 16), 16)
            for k in range(2):
                at, mine = self.span(g, k), self.packed(g, k)
                total = own[outer, at].astype(F32) + sib[0, inner, at].astype(F32)
                if k == 0:
                    total = total + mate[0, inner, :].astype(F32)
                total = total + run[self.slot(1, r.plus), inner, mine].astype(F32)
                total = total + run[self.slot(-1, r.minus), inner, mine].astype(F32)
                end[0, inner, mine] = total.astype(BF16)
            return 0

        lax.fori_loop(0, rows // 16, part, 0)
        self.end_copy(g).start()

    def end_copy(self, g):
        end = self.buf(g)[3]
        return remote(end.at[0], end.at[1], self.s_end.at[g], self.r_end.at[g], self.r.mate)

    def result(self, g, out):
        end = self.buf(g)[3]
        rows = end.shape[1]
        self.end_copy(g).wait_recv()

        def part(n16, _):
            inner = pl.ds(pl.multiple_of(n16 * 16, 16), 16)
            mine0, mine1 = self.packed(g, 0), self.packed(g, 1)
            out[inner, self.span(g, 0)] = end[0, inner, mine0].astype(F32)
            out[inner, self.span(g, 2)] = end[1, inner, mine0].astype(F32)
            out[inner, self.span(g, 1)] = end[0, inner, mine1].astype(F32) + end[1, inner, mine1].astype(F32)
            return 0

        lax.fori_loop(0, rows // 16, part, 0)

    def rounds(self, g):
        r = self.r
        over = [(self.hand_over, (g, ahead)) for ahead in self.order()]
        out, waiting = [], []
        for s in range(r.plus):
            signs = (1, -1) if s < r.minus else (1,)
            hand, over = over[: 4 if s == 0 else 2], over[4 if s == 0 else 2 :]
            steps = [(self.step, (g, 1, sign, s)) for sign in signs]
            out.append((hand if s == 0 else []) + steps + waiting + (hand if s > 0 else []))
            waiting = [(self.step, (g, 0, sign, s)) for sign in signs]
        return out + [waiting + over, [(self.own_sum, (g,))]]

    def drain(self, groups):
        r = self.r
        for g in groups:
            for ahead in self.order():
                self.sib_copy(g, ahead).wait_send()
                self.mate_copy(g, ahead).wait_send()
            for k in range(2):
                for s in range(r.plus):
                    self.ring_copy(g, k, 1, s).wait_send()
                for s in range(r.minus):
                    self.ring_copy(g, k, -1, s).wait_send()
            self.end_copy(g).wait_send()


class AllSum:
    @staticmethod
    def scratch(ndp, shape):
        n = ndp.bit_length()
        return [pltpu.VMEM((n,) + shape, F32), pltpu.SemaphoreType.DMA((n,)), pltpu.SemaphoreType.DMA((n,))]

    def __init__(self, ring, acc, bufs):
        self.acc, (self.buf, self.s, self.r) = acc, bufs
        self.partners = [ring.mate] + ring.flips()

    def copy(self, n):
        return remote(self.acc, self.buf.at[n], self.s.at[n], self.r.at[n], self.partners[n])

    def start(self, n):
        self.copy(n).start()

    def end(self, n):
        self.copy(n).wait()
        self.acc[...] += self.buf[n]

    def rounds(self):
        out = [[(self.start, (0,))]]
        for n in range(len(self.partners)):
            out.append([(self.end, (n,))])
            if n + 1 < len(self.partners):
                out[-1].append((self.start, (n + 1,)))
        return out


class Pump:
    def __init__(self):
        self.active = {}

    def add(self, kind, number, rounds, delay=0):
        self.active[kind, number] = [[]] * delay + list(rounds)

    def tick(self):
        queues = [self.active[key].pop(0) for key in list(self.active) if key[0] == "t"]
        sums = [self.active[key].pop(0) for key in list(self.active) if key[0] == "s"]
        for n in range(max([len(q) for q in queues], default=0)):
            for queue in queues:
                if n < len(queue):
                    call, args = queue[n]
                    call(*args)
        for queue in sums:
            for call, args in queue:
                call(*args)
        self.active = {key: rounds for key, rounds in self.active.items() if rounds}

    def until(self, *numbers):
        while any(("t", number) in self.active for number in numbers):
            self.tick()

    def rest(self):
        while self.active:
            self.tick()


VM = pl.BlockSpec(memory_space=pltpu.VMEM)
SM = pl.BlockSpec(memory_space=pltpu.SMEM)
ANY = pl.BlockSpec(memory_space=pl.ANY)
ROOM = 127 << 19
TABLE_ROWS = 16


def table_params(sz, tab):
    return dict(
        gain_in=tab.at[0:1, : sz.D],
        taps=tab.at[1:5],
        cbias=tab.at[5:6],
        gain_out=tab.at[6:7, : sz.E],
        sbias=tab.at[7:8, :LANES],
        decay=tab.at[8:9, :LANES],
        skipw=tab.at[9:10, : sz.E],
    )


def run_flags(spans, d):
    begin, opens = jnp.int32(0), jnp.int32(0)
    for s in range(spans.shape[1]):
        length = spans[d, s]
        starts = jnp.where(begin == 1, 1, 0) * jnp.where(length > 0, 1, 0)
        opens = jnp.maximum(opens, starts)
        begin = begin + length
    live = jnp.where(begin > 1, 1.0, 0.0).astype(F32)
    opened = jnp.maximum(opens.astype(F32), 1.0 - live)
    return 1.0 - opened, live


AG_IN, AG_OUT = 9, 2


class Plan:
    def __init__(self, layers, taps, ndp, sz, n_in, n_conv, n_out):
        self.L, self.K, self.ndp, self.sz = layers, taps, ndp, sz
        self.n_in, self.n_conv, self.n_out = n_in, n_conv, n_out
        self.ag_in = (AG_IN * LANES, sz.NP - 2 * AG_IN * LANES)
        self.ag_out = (AG_OUT * LANES, sz.D - 2 * AG_OUT * LANES)
        tiles = lambda width: width // LANES
        self.early = (sz.NP - sz.E) // 5 * 2
        gate, out = tiles(sz.E), tiles(sz.D)
        early, rest = tiles(self.early), tiles(sz.NP - sz.E - self.early)
        cut = lambda width, part: (part * LANES, (width - 2 * part) * LANES)
        self.rs_parts = [
            [cut(out, OUT_PARTS[l]), cut(gate, GATE_PARTS[l]), cut(early, EARLY_PARTS[l]),
             cut(rest, REST_PARTS[l])]
            for l in range(layers)
        ]
        self.rs_widths = [sz.D, sz.E, self.early, sz.NP - sz.E - self.early]
        self.rs_rows = [sz.E // ndp] + [sz.D // ndp] * 3


OUT_PARTS, GATE_PARTS, EARLY_PARTS, REST_PARTS = (1, 1), (3, 3), (1, 1), (1, 2)


def stage_own(pl_, ins, stage, smallf, small, sems):
    sz = pl_.sz
    w_gate, w_conv, w_step, in_gain, conv_weight, conv_bias, out_gain = ins
    copies = []
    for l in range(pl_.L):
        copies.append(
            pltpu.make_async_copy(w_gate.at[l], stage.at[l, :, pl.ds(0, sz.E)], sems.at[2 * l])
        )
        copies.append(
            pltpu.make_async_copy(
                w_conv.at[l], stage.at[l, :, pl.ds(sz.E, sz.CW)], sems.at[2 * l + 1]
            )
        )
    for copy in copies:
        copy.start()
    smallf[...] = jnp.zeros_like(smallf)
    L, K = pl_.L, pl_.K
    smallf[0:L, : pl_.n_in] = in_gain[...].astype(F32)
    for l in range(L):
        smallf[L + l * K : L + (l + 1) * K, : pl_.n_conv] = conv_weight[l].astype(F32)
    smallf[L + L * K : 2 * L + L * K, : pl_.n_conv] = conv_bias[...].astype(F32)
    smallf[2 * L + L * K : 3 * L + L * K, : pl_.n_out] = out_gain[...].astype(F32)
    small[...] = smallf[...].astype(BF16)
    for l in range(L):
        stage[l, :, sz.STEP :] = jnp.zeros((stage.shape[1], LANES), BF16)
        stage[l, :, sz.STEP : sz.STEP + 2 * sz.H] = w_step[l]
    for copy in copies:
        copy.wait()


def fill_table(pl_, table, gathered, step_bias, decay_log, skip_gain):
    sz, L, K = pl_.sz, pl_.L, pl_.K
    table[...] = jnp.zeros_like(table)
    rows = gathered.shape[0] // pl_.ndp
    for q in range(pl_.ndp):
        part = gathered[q * rows : (q + 1) * rows, :].astype(F32)
        for l in range(L):
            table[l, 0:1, q * pl_.n_in : (q + 1) * pl_.n_in] = part[l : l + 1, : pl_.n_in]
            conv = slice(q * pl_.n_conv, (q + 1) * pl_.n_conv)
            table[l, 1 : 1 + K, conv] = part[L + l * K : L + (l + 1) * K, : pl_.n_conv]
            at = L + L * K + l
            table[l, 5:6, conv] = part[at : at + 1, : pl_.n_conv]
            out = slice(q * pl_.n_out, (q + 1) * pl_.n_out)
            table[l, 6:7, out] = part[at + L : at + L + 1, : pl_.n_out]
    head_of = iota((sz.H, sz.E), 1) // HD
    one_hot = (iota((sz.H, sz.E), 0) == head_of).astype(F32)
    wide = mm_exact(skip_gain[...], one_hot)
    decay = jnp.exp(decay_log[...])
    for l in range(L):
        table[l, 7:8, : 2 * sz.H] = step_bias[l : l + 1, :]
        table[l, 8:9, : sz.H] = decay[l : l + 1]
        table[l, 8:9, sz.H : 2 * sz.H] = decay[l : l + 1]
        table[l, 9:10, : sz.E] = wide[l : l + 1]


def forward_kernel(pl_, *refs):
    sz, L = pl_.sz, pl_.L
    (spans, u0, w_gate, w_conv, w_step, in_gain, conv_weight, conv_bias, out_gain, w_out,
     step_bias, decay_log, skip_gain) = refs[:13]
    out_w = refs[13 : 13 + 2 * L]
    out_s = refs[13 + 2 * L : 13 + 5 * L]
    table = refs[13 + 5 * L]
    rest = refs[14 + 5 * L :]
    full, rest = rest[: 2 * L], rest[2 * L :]
    saved, rest = rest[: 3 * L], rest[3 * L :]
    conv, normed, nout, colb, rowt, stage, smallf, small, gathered, own_sems, out_sems = rest[:11]
    sems = rest[11:]
    ring = Ring(pl_.ndp)
    ring.barrier()
    flags = run_flags(spans, ring.d)
    stage_own(pl_, (w_gate, w_conv, w_step, in_gain, conv_weight, conv_bias, out_gain),
              stage, smallf, small, own_sems)
    groups, parts = [(small, gathered)], [(0, LANES)]
    for l in range(L):
        groups += [(stage.at[l], full[2 * l]), (w_out.at[l], full[2 * l + 1])]
        parts += [pl_.ag_in, pl_.ag_out]
    gather = Gather(ring, groups, parts, sems)
    pump = Pump()
    for g, start in enumerate(STARTS):
        pump.add("t", g, gather.rounds(g), start)
    pump.until(0, 1)
    gather.finish([0])
    fill_table(pl_, table, gathered, step_bias, decay_log, skip_gain)
    outward = []

    def send_out(src, dst):
        copy = pltpu.make_async_copy(src, dst, out_sems.at[len(outward)])
        copy.start()
        outward.append(copy)

    u = u0.at[ring.d]
    for l in range(L):
        g_in, g_out = 1 + 2 * l, 2 + 2 * l
        pump.until(g_in)
        gather.finish([g_in])
        send_out(full[2 * l], out_w[2 * l])
        proj, y, unext = saved[3 * l : 3 * l + 3]

        def hook(n):
            if n == 1:
                send_out(proj, out_s[3 * l])
            if n == 4:
                send_out(y, out_s[3 * l + 1])
                pump.until(g_out)
                gather.finish([g_out])
                send_out(full[2 * l + 1], out_w[2 * l + 1])
            elif n in TICKS_F:
                pump.tick()

        forward_layer(sz, table_params(sz, table.at[l]), flags, u, full[2 * l], full[2 * l + 1],
                      proj, y, unext, conv, normed, nout, colb, rowt, hook=hook)
        send_out(unext, out_s[3 * l + 2])
        u = unext
    gather.drain(range(len(groups)))
    for copy in outward:
        copy.wait()


STARTS = (0, 0, 2, 3, 6)
TICKS_F = (0, 2, 3)


def forward_call(pl_, spans, u0, w_gate, w_conv, w_step, in_gain, conv_weight, conv_bias, out_gain,
                 w_out, step_bias, decay_log, skip_gain):
    sz, L = pl_.sz, pl_.L
    full = [((sz.D, sz.NP), BF16), ((sz.E, sz.D), BF16)] * L
    kept = []
    for l in range(L):
        kept += [((sz.T, sz.NP), F32), ((sz.T, sz.E), F32), ((sz.T, sz.D), BF16 if l == L - 1 else F32)]
    shapes = [jax.ShapeDtypeStruct(*s) for s in full + kept]
    return pl.pallas_call(
        functools.partial(forward_kernel, pl_),
        out_shape=shapes + [jax.ShapeDtypeStruct((L, TABLE_ROWS, sz.CW), F32)],
        in_specs=[SM, VM, ANY, ANY] + [VM] * 5 + [ANY] + [VM] * 3,
        out_specs=[ANY] * len(shapes) + [VM],
        scratch_shapes=[pltpu.VMEM(*s) for s in full + kept] + forward_scratch(sz) + [
            pltpu.VMEM((L, w_gate.shape[1], sz.NP), BF16),
            pltpu.VMEM((16, LANES), F32),
            pltpu.VMEM((16, LANES), BF16),
            pltpu.VMEM((16 * pl_.ndp, LANES), BF16),
            pltpu.SemaphoreType.DMA((2 * L,)),
            pltpu.SemaphoreType.DMA((len(shapes),)),
        ] + Gather.scratch(pl_.ndp, 1 + 2 * L),
        compiler_params=pltpu.CompilerParams(
            collective_id=1, has_side_effects=True, vmem_limit_bytes=ROOM
        ),
    )(spans, u0, w_gate, w_conv, w_step, in_gain, conv_weight, conv_bias, out_gain, w_out,
      step_bias, decay_log, skip_gain)


def fwd_kernel(sz, layer, spans, u, win, wout, table, proj, y, unext, conv, normed, nout, colb, rowt):
    d = lax.axis_index("dir")
    flags = run_flags(spans, d)
    forward_layer(sz, table_params(sz, table.at[layer]), flags, u.at[d] if layer == 0 else u,
                  win, wout, proj, y, unext, conv, normed, nout, colb, rowt)


def forward_scratch(sz):
    return [
        pltpu.VMEM((sz.T, sz.CW), F32),
        pltpu.VMEM((sz.T, sz.D), BF16),
        pltpu.VMEM((sz.T, sz.E), BF16),
        pltpu.VMEM((1, sz.H, sz.T, BLK), F32),
        pltpu.VMEM((2, 2, LANES, BLK), F32),
    ]


def saved_shapes(sz):
    return [
        jax.ShapeDtypeStruct((sz.T, sz.NP), F32),
        jax.ShapeDtypeStruct((sz.T, sz.E), F32),
        jax.ShapeDtypeStruct((sz.T, sz.D), F32),
    ]


def fwd_call(sz, layer, spans, u, win, wout, table):
    return pl.pallas_call(
        functools.partial(fwd_kernel, sz, layer),
        out_shape=saved_shapes(sz),
        in_specs=[SM] + [VM] * 4,
        out_specs=[VM] * 3,
        scratch_shapes=forward_scratch(sz),
        compiler_params=pltpu.CompilerParams(vmem_limit_bytes=ROOM),
    )(spans, u, win, wout, table)


def bwd_kernel(sz, layer, last, names, spans, g, u, win, wout, proj, y, table, gu, gwin, gwout,
               small, head, *rest):
    d = lax.axis_index("dir")
    flags = run_flags(spans, d)
    backward_layer(sz, table_params(sz, table.at[layer]), flags, g.at[d] if last else g,
                   u.at[d] if layer == 0 else u, win, wout, proj, y, gu, gwin, gwout, small, head,
                   dict(zip(names, rest)))


def grad_shapes(sz):
    return [
        jax.ShapeDtypeStruct((sz.T, sz.D), F32),
        jax.ShapeDtypeStruct((sz.D, sz.NP), BF16),
        jax.ShapeDtypeStruct((sz.E, sz.D), BF16),
        jax.ShapeDtypeStruct((8, sz.CW), F32),
        jax.ShapeDtypeStruct((8, LANES), F32),
    ]


def bwd_call(sz, layer, last, spans, g, u, win, wout, proj, y, table):
    s = backward_scratch(sz)
    return pl.pallas_call(
        functools.partial(bwd_kernel, sz, layer, last, tuple(s)),
        out_shape=grad_shapes(sz),
        in_specs=[SM] + [VM] * 7,
        out_specs=[VM] * 5,
        scratch_shapes=list(s.values()),
        compiler_params=pltpu.CompilerParams(vmem_limit_bytes=ROOM),
    )(spans, g, u, win, wout, proj, y, table)


def own_small(pl_, acc, picks, outs, me):
    L, K = pl_.L, pl_.K
    for q in range(pl_.ndp):
        for n, count in enumerate((pl_.n_in, pl_.n_conv, pl_.n_out)):
            for l in range(L):
                at = 8 * (L * q + l)
                picks[0, n, at : at + 8, :count] = acc[l, :, q * count : (q + 1) * count]
    mine = rows_at(me, 8 * L)
    p_in, p_conv, p_out = picks[0, 0, mine, :], picks[0, 1, mine, :], picks[0, 2, mine, :]
    g_in, g_taps, g_bias, g_out = outs
    for l in range(L):
        r = 8 * l
        g_in[l : l + 1, :] = p_in[r : r + 1, : pl_.n_in]
        g_taps[l] = p_conv[r + 1 : r + 1 + K, : pl_.n_conv]
        g_bias[l : l + 1, :] = p_conv[r + 5 : r + 6, : pl_.n_conv]
        g_out[l : l + 1, :] = p_out[r + 6 : r + 7, : pl_.n_out]


def head_grads(pl_, acc, g_bias, g_decay, g_skip):
    sz = pl_.sz
    for l in range(pl_.L):
        part = acc[l, :, sz.CW :]
        g_bias[l : l + 1, :] = part[0:1, : 2 * sz.H]
        g_decay[l : l + 1, :] = part[1:2, : sz.H] + part[1:2, sz.H : 2 * sz.H]
        g_skip[l : l + 1, :] = part[2:3, : sz.H]


TICKS = ("proj", "post", "scan1", "scan3", "conv", "normed")


def backward_kernel(pl_, names, nbuf, *refs):
    sz, L = pl_.sz, pl_.L
    E = sz.E
    spans, resid_in, grad_out, resid2, table = refs[:5]
    weights = refs[5 : 5 + 2 * L]
    kept = refs[5 + 2 * L : 5 + 5 * L - 1]
    rest = refs[4 + 5 * L :]
    (resid, grad_in, g_in, g_gate, g_conv, g_step, g_taps, g_cbias, g_sbias, g_decay, g_skip,
     g_gout, g_out) = rest[:13]
    wi1, wo0, wo1, gi1, go1, proj, y, u1, u0, g1, gbuf, accs, load_sems, xsems = rest[13:27]
    sum_bufs, rest = rest[27 : 27 + 3 * L], rest[27 + 3 * L :]
    s = dict(zip(names, rest[: len(names)]))
    rest = rest[len(names) :]
    picks, whole = s["colb"], proj.at[0 : g_conv.shape[1], 0 : sz.NP - E]
    bufs, sems = rest[:nbuf], rest[nbuf:]
    ring = Ring(pl_.ndp)
    flags = run_flags(spans, ring.d)
    proj0, y0, u1_hbm, proj1, y1 = kept
    loads = {}
    for n, (name, src, dst) in enumerate((
        ("wo1", weights[3], wo1), ("proj1", proj1, proj), ("y1", y1, y), ("u1", u1_hbm, u1),
        ("wi1", weights[2], wi1), ("wo0", weights[1], wo0), ("proj0", proj0, proj), ("y0", y0, y),
        ("wi0", weights[0], gi1), ("g1", grad_out.at[ring.d], g1), ("u0", resid_in.at[ring.d], u0),
    )):
        loads[name] = pltpu.make_async_copy(src, dst, load_sems.at[n])
    for name in ("g1", "wo1", "proj1", "y1", "u1", "wi1", "wo0", "u0"):
        loads[name].start()
    ring.barrier(ring.flips())
    give_u = remote(resid2, resid.at[ring.d], xsems.at[0], xsems.at[1], ring.mate)
    keep_u = pltpu.make_async_copy(resid2, resid.at[ring.d], xsems.at[4])
    give_u.start()
    keep_u.start()
    give_g = remote(gbuf.at[0], gbuf.at[1], xsems.at[2], xsems.at[3], ring.mate)

    gwin, gwout = [wi1, gi1], [wo1, go1]
    groups, parts = [], []
    for l in range(L):
        part = lambda start, width: gwin[l].at[:, pl.ds(start, width)]
        late = E + pl_.early
        groups += [gwout[l], part(0, E), part(E, pl_.early), part(late, sz.NP - late)]
        parts += pl_.rs_parts[l]
    scatter = Scatter(ring, groups, parts, bufs, sems)
    pump = Pump()
    seen = []
    sums = [AllSum(ring, accs.at[l], sum_bufs[3 * l : 3 * l + 3]) for l in range(L)]

    def launch(g):
        scatter.begin([g])
        pump.add("t", g, scatter.rounds(g))

    def tick(name):
        if name == "scan":
            name = "scan%d" % len(seen)
            seen.append(name)
        else:
            seen.clear()
        if name in TICKS:
            pump.tick()

    def results(l):
        scatter.result(4 * l, g_out.at[l])
        scatter.result(4 * l + 1, g_gate.at[l])
        scatter.result(4 * l + 2, whole.at[:, 0 : pl_.early])
        scatter.result(4 * l + 3, whole.at[:, pl_.early : sz.NP - E])
        g_conv[l] = whole[:, : sz.CW]
        g_step[l] = whole[:, sz.CW : sz.CW + 2 * sz.H]

    def hook1(name):
        if name == "start":
            loads["g1"].wait()
        elif name == "w_out":
            loads["wo1"].wait()
        elif name == "proj":
            loads["proj1"].wait()
        elif name == "y":
            loads["y1"].wait()
        elif name == "post":
            loads["y0"].start()
        elif name == "g_out":
            launch(4)
            loads["u1"].wait()
        elif name == "g_gate":
            launch(5)
        elif name == "conv_end":
            loads["proj0"].start()
        elif name == "g_early":
            launch(6)
        elif name == "g_conv":
            launch(7)
        elif name == "w_in":
            loads["wi1"].wait()
        tick(name)

    def hook0(name):
        if name == "w_out":
            loads["wo0"].wait()
        elif name == "proj":
            loads["proj0"].wait()
        elif name == "y":
            loads["y0"].wait()
            pump.add("s", 1, sums[1].rounds())
        elif name == "g_out":
            launch(0)
            loads["u0"].wait()
        elif name == "g_gate":
            launch(1)
        elif name == "conv":
            pump.until(5, 6, 7)
            scatter.drain([5, 6, 7])
            loads["wi0"].start()
        elif name == "g_early":
            launch(2)
        elif name == "g_conv":
            launch(3)
        elif name == "w_in":
            loads["wi0"].wait()
        tick(name)

    for l, hook in ((1, hook1), (0, hook0)):
        small, head = accs.at[l, :, pl.ds(0, sz.CW)], accs.at[l, :, pl.ds(sz.CW, LANES)]
        if l == 1:
            backward_layer(sz, table_params(sz, table.at[l]), flags, g1, u1, wi1, wo1,
                           proj, y, u1, gi1, go1, small, head, s, hook)
        else:
            backward_layer(sz, table_params(sz, table.at[l]), flags, u1, u0, gi1, wo0,
                           proj, y, gbuf.at[0], wi1, wo1, small, head, s, hook)
    give_g.start()
    pump.add("s", 0, sums[0].rounds())
    pump.tick()
    results(1)
    give_u.wait()
    keep_u.wait()
    pump.rest()
    own_small(pl_, accs, picks, (g_in, g_taps, g_cbias, g_gout), ring.me)
    head_grads(pl_, accs, g_sbias, g_decay, g_skip)
    give_g.wait()
    grad_in[ring.d] = gbuf[0].astype(F32)
    grad_in[1 - ring.d] = gbuf[1].astype(F32)
    results(0)
    scatter.drain(range(5))


def backward_call(pl_, spans, resid_in, grad_out, weights, kept, table):
    sz, L, ndp = pl_.sz, pl_.L, pl_.ndp
    shape = lambda *s: jax.ShapeDtypeStruct(s, F32)
    r_in, r_out = sz.D // ndp, sz.E // ndp
    out = [
        jax.ShapeDtypeStruct((2, sz.T, sz.D), BF16),
        shape(2, sz.T, sz.D),
        shape(L, pl_.n_in),
        shape(L, r_in, sz.E),
        shape(L, r_in, sz.CW),
        shape(L, r_in, 2 * sz.H),
        shape(L, pl_.K, pl_.n_conv),
        shape(L, pl_.n_conv),
        shape(L, 2 * sz.H),
        shape(L, sz.H),
        shape(L, sz.H),
        shape(L, pl_.n_out),
        shape(L, r_out, sz.D),
    ]
    shapes, parts = [], []
    for l in range(L):
        shapes += list(zip(pl_.rs_rows, pl_.rs_widths))
        parts += pl_.rs_parts[l]
    bufs, sems = Scatter.scratch(ndp, shapes, parts)
    acc = (8, sz.CW + LANES)
    s = backward_scratch(sz)
    scratch = [
        pltpu.VMEM((sz.D, sz.NP), BF16),
        pltpu.VMEM((sz.E, sz.D), BF16),
        pltpu.VMEM((sz.E, sz.D), BF16),
        pltpu.VMEM((sz.D, sz.NP), BF16),
        pltpu.VMEM((sz.E, sz.D), BF16),
        pltpu.VMEM((sz.T, sz.NP), F32),
        pltpu.VMEM((sz.T, sz.E), F32),
        pltpu.VMEM((sz.T, sz.D), F32),
        pltpu.VMEM((sz.T, sz.D), BF16),
        pltpu.VMEM((sz.T, sz.D), BF16),
        pltpu.VMEM((2, sz.T, sz.D), BF16),
        pltpu.VMEM((L,) + acc, F32),
        pltpu.SemaphoreType.DMA((11,)),
        pltpu.SemaphoreType.DMA((5,)),
    ] + AllSum.scratch(ndp, acc) * L + list(s.values()) + bufs + sems
    resid2, kept = kept[-1], kept[:-1]
    made = pl.pallas_call(
        functools.partial(backward_kernel, pl_, tuple(s), len(bufs)),
        out_shape=out,
        in_specs=[SM, ANY, ANY, VM, VM] + [ANY] * (2 * L + len(kept)),
        out_specs=[ANY] + [VM] * (len(out) - 1),
        scratch_shapes=scratch,
        compiler_params=pltpu.CompilerParams(
            collective_id=2, has_side_effects=True, vmem_limit_bytes=ROOM
        ),
    )(spans, resid_in, grad_out, resid2, table, *weights, *kept)
    return hand_out(made)


def hand_out_kernel(count, *refs):
    sems = refs[-1]
    copies = [
        pltpu.make_async_copy(refs[n], refs[count + n], sems.at[n]) for n in range(count)
    ]
    for copy in copies:
        copy.start()
    for copy in copies:
        copy.wait()


def hand_out(made):
    return pl.pallas_call(
        functools.partial(hand_out_kernel, len(made)),
        out_shape=[jax.ShapeDtypeStruct(v.shape, v.dtype) for v in made],
        in_specs=[ANY] * len(made),
        out_specs=[VM] * len(made),
        scratch_shapes=[pltpu.SemaphoreType.DMA((len(made),))],
    )(*made)


def pad_lanes(v, width=LANES):
    return jnp.pad(v, [(0, 0)] * (v.ndim - 1) + [(0, width - v.shape[-1])])


def plain_gather(pl_, w_gate, w_conv, w_step, in_gain, conv_weight, conv_bias, out_gain, w_out,
                 step_bias, decay_log, skip_gain):
    sz = pl_.sz
    fetch = lambda v, axis=0: lax.all_gather(v, "dp", axis=axis, tiled=True)
    shard = jnp.concatenate([w_gate, w_conv, pad_lanes(w_step)], axis=2)
    full = []
    for l in range(pl_.L):
        full += [fetch(shard[l]), fetch(w_out[l])]
    wide = lambda v: pad_lanes(v.astype(F32), sz.CW)[:, None]
    decay = jnp.exp(decay_log)
    table = jnp.concatenate(
        [wide(fetch(in_gain, 1)), fetch(conv_weight, 2).astype(F32), wide(fetch(conv_bias, 1)),
         wide(fetch(out_gain, 1)), wide(step_bias), wide(jnp.concatenate([decay, decay], 1)),
         wide(jnp.repeat(skip_gain, HD, axis=1))], axis=1)
    return full + [jnp.pad(table, ((0, 0), (0, TABLE_ROWS - table.shape[1]), (0, 0)))]


def plain_scatter(pl_, u, g, grads, smalls, heads):
    sz, K = pl_.sz, pl_.K
    me = lax.axis_index("dp")
    summed = [
        lax.psum(lax.psum_scatter(v, "dp", scatter_dimension=0, tiled=True).astype(F32), "dir")
        for v in grads
    ]
    small, head = lax.psum((jnp.stack(smalls), jnp.stack(heads)), ("dir", "dp"))
    own = lambda v, n: lax.dynamic_slice_in_dim(v, me * n, n, axis=v.ndim - 1)
    win = jnp.stack(summed[0::2])
    return (
        lax.all_gather(u.astype(BF16), "dir"),
        lax.all_gather(g, "dir"),
        own(small[:, 0], pl_.n_in),
        win[:, :, : sz.E],
        win[:, :, sz.E : sz.STEP],
        win[:, :, sz.STEP : sz.STEP + 2 * sz.H],
        own(small[:, 1 : 1 + K], pl_.n_conv),
        own(small[:, 5], pl_.n_conv),
        head[:, 0, : 2 * sz.H],
        head[:, 1, : sz.H] + head[:, 1, sz.H : 2 * sz.H],
        head[:, 2, : sz.H],
        own(small[:, 6], pl_.n_out),
        jnp.stack(summed[1::2]),
    )


def shards(resid_in, grad_out, seq_spans, in_gain, w_gate_in, w_conv_in, w_step, conv_weight,
           conv_bias, step_bias, decay_log, skip_gain, out_gain, w_out):
    layers, taps = conv_weight.shape[:2]
    ndp = lax.axis_size("dp")
    sz = Sizes(resid_in.shape[2], w_gate_in.shape[2], w_conv_in.shape[2], skip_gain.shape[1])
    pl_ = Plan(layers, taps, ndp, sz, in_gain.shape[1], conv_weight.shape[2], out_gain.shape[1])
    whole_tiles = w_gate_in.shape[1] % 16 == 0 and w_out.shape[1] % 16 == 0
    weights = (w_gate_in, w_conv_in, w_step, in_gain, conv_weight, conv_bias, out_gain, w_out,
               step_bias, decay_log, skip_gain)
    u, saved = resid_in, []
    if whole_tiles:
        got = forward_call(pl_, seq_spans, resid_in, *weights)
        out = backward_call(pl_, seq_spans, resid_in, grad_out, got[: 2 * layers],
                            got[2 * layers : -1], got[-1])
        return tuple(out)
    got = plain_gather(pl_, *weights)
    win, wout, table = got[0:-1:2], got[1:-1:2], got[-1]
    for l in range(layers):
        proj, y, unext = fwd_call(sz, l, seq_spans, u, win[l], wout[l], table)
        saved.append((u, proj, y))
        u = unext
    g = grad_out
    grads, smalls, heads = [None] * (2 * layers), [None] * layers, [None] * layers
    for l in reversed(range(layers)):
        u_in, proj, y = saved[l]
        g, grads[2 * l], grads[2 * l + 1], smalls[l], heads[l] = bwd_call(
            sz, l, l == layers - 1, seq_spans, g, u_in, win[l], wout[l], proj, y, table)
    return tuple(plain_scatter(pl_, u, g, grads, smalls, heads))


def solution(mesh):
    rows, cols_, last = P(None, "dp", None), P(None, "dp"), P(None, None, "dp")
    placed = (rows, rows, cols_, cols_, rows, rows, rows, last, cols_, P(), P(), P(), cols_, rows)
    out = (rows, rows, cols_, rows, rows, rows, last, cols_, P(), P(), P(), cols_, rows)
    return jax.shard_map(shards, mesh=mesh, in_specs=placed, out_specs=out, check_vma=False)
```

```python
import functools
import jax
import jax.numpy as jnp
from jax import lax
from jax.experimental import pallas as pl
from jax.experimental.pallas import tpu as pltpu
from jax.sharding import PartitionSpec as P

BLK = 128
HD = 64
F32 = jnp.float32
BF16 = jnp.bfloat16
HIGH = lax.Precision.HIGHEST
LANES = 128


def mm(a, b):
    return lax.dot_general(a, b, (((1,), (0,)), ((), ())), preferred_element_type=F32)


def mm_nt(a, b):
    return lax.dot_general(a, b, (((1,), (1,)), ((), ())), preferred_element_type=F32)


def mm_tn(a, b):
    return lax.dot_general(a, b, (((0,), (0,)), ((), ())), preferred_element_type=F32)


def mm_exact(a, b):
    return lax.dot_general(
        a, b, (((1,), (0,)), ((), ())), precision=HIGH, preferred_element_type=F32
    )


def iota(shape, dim):
    return lax.broadcasted_iota(jnp.int32, shape, dim)


def square_masks():
    row, col = iota((BLK, BLK), 0), iota((BLK, BLK), 1)
    return row, col


def lag_keep(keep1, lag, rows=2 * BLK):
    at = iota((rows, 1), 0)
    first = (at >= lag).astype(F32)
    edge = ((at >= BLK) & (at < BLK + lag)).astype(F32)
    return first - edge * (1.0 - keep1)


def silu(v):
    return v * jax.nn.sigmoid(v)


class Sizes:
    def __init__(self, width, inner, convw, heads):
        self.D, self.E, self.CW, self.H = width, inner, convw, heads
        self.NP = inner + convw + LANES
        self.STEP = inner + convw
        self.T = 2 * BLK


CHUNK = 1536


def spread_matrix(head0, base, width):
    row = iota((LANES, width), 0)
    col = iota((LANES, width), 1)
    return (row % 64 == col // HD + (base + head0)).astype(BF16)


def halves(values):
    high = values.astype(BF16).astype(F32)
    low = values - high
    lane = iota(values.shape, 1)
    return jnp.where(lane < 64, high, pltpu.roll(low, 64, 1)).astype(BF16)


def conv_phase(sz, cin_of, taps, bias, keep1, out_ref, slope_ref):
    keeps = [None] + [lag_keep(keep1, k) for k in range(1, 4)]

    def chunk(n, _):
        at = pl.ds(pl.multiple_of(n * LANES, LANES), LANES)
        cin = cin_of(n)
        z = bias[:, at] + taps[0:1, at] * cin
        for k in range(1, 4):
            z = z + taps[k : k + 1, at] * (pltpu.roll(cin, k, 0) * keeps[k])
        sig = jax.nn.sigmoid(z)
        act = z * sig
        out_ref[:, at] = act
        if slope_ref is not None:
            slope_ref[:, at] = (sig + act * (1.0 - sig)).astype(slope_ref.dtype)
        return 0

    lax.fori_loop(0, sz.CW // LANES, chunk, 0)


def step_phase(sz, raw, sbias, decay):
    z = raw + sbias
    dt = jnp.maximum(z, 0.0) + jnp.log1p(jnp.exp(-jnp.abs(z)))
    a = -dt * decay
    row, col = square_masks()
    lower = (row >= col).astype(F32)
    upper = (row <= col).astype(F32)
    lane = iota((BLK, LANES), 1)
    sums = []
    for b in range(2):
        part = a[b * BLK : (b + 1) * BLK]
        down, up = mm_exact(lower, part), mm_exact(upper, part)
        sums.append(jnp.where(lane < sz.H, down, up))
    return z, dt, a, sums


def b_and_c(sz, conv_ref):
    lane = iota((sz.T, LANES), 1)
    out = []
    for way in range(2):
        pair = conv_ref[:, sz.E + way * LANES : sz.E + (way + 1) * LANES]
        bp = jnp.where(lane < 64, pair, 0.0)
        cp = jnp.where(lane < 64, pltpu.roll(pair, 64, 1), 0.0)
        cp = pltpu.roll(cp, 1 if way == 0 else sz.T - 1, 0)
        out.append((bp.astype(BF16), cp.astype(BF16)))
    return out


def blk(v, b):
    return v[b * BLK : (b + 1) * BLK]


def carry_weights(sz, dt, sums):
    end0 = jnp.exp(sums[0][BLK - 1 : BLK, :] - sums[0])
    end1 = jnp.exp(sums[1][0:1, :] - sums[1])
    lane = iota((BLK, LANES), 1)
    fwd = jnp.where(lane < sz.H, end0, 0.0)
    rev = jnp.where((lane >= sz.H) & (lane < 2 * sz.H), end1, 0.0)
    return fwd, rev


def forward_scan(sz, conv_ref, y_ref, colb, rowt, bc, dt, a, sums, keep1):
    row, col = square_masks()
    low = row > col
    (bf, cf), (bb, cb) = bc
    excl = [sums[b] - blk(a, b) for b in range(2)]
    scores = []
    for b in range(2):
        sf = mm_nt(blk(cf, b), blk(bf, b))
        sb = mm_nt(blk(cb, b), blk(bb, b))
        scores.append(jnp.where(low, sf, jnp.where(row < col, sb, 0.0)))
        rowt[0, b] = sums[b].T
        rowt[1, b] = blk(dt, b).T
        for h in range(sz.H):
            ef = jnp.broadcast_to(excl[b][:, h : h + 1], (BLK, BLK))
            eb = jnp.broadcast_to(excl[b][:, sz.H + h : sz.H + h + 1], (BLK, BLK))
            colb[0, h, b * BLK : (b + 1) * BLK] = jnp.where(low, ef, eb)
    left = iota((BLK, LANES), 1) < HD

    def pair(p, _):
        at = pl.ds(pl.multiple_of(p * LANES, LANES), LANES)
        for b in range(2):
            rows = slice(b * BLK, (b + 1) * BLK)
            x = conv_ref[rows, at].astype(BF16)
            ys = []
            for hh in range(2):
                h = 2 * p + hh
                sum_row = jnp.where(low, rowt[0, b, pl.ds(h, 1)], rowt[0, b, pl.ds(sz.H + h, 1)])
                dt_row = jnp.where(low, rowt[1, b, pl.ds(h, 1)], rowt[1, b, pl.ds(sz.H + h, 1)])
                decay = jnp.exp(jnp.minimum(colb[0, h, rows] - sum_row, 0.0))
                mix = decay * scores[b] * dt_row
                ys.append(mm(mix.astype(BF16), x))
            y_ref[rows, at] = jnp.where(left, ys[0], ys[1])
        return 0

    lax.fori_loop(0, sz.H // 2, pair, 0, unroll=2)
    ends = carry_weights(sz, dt, sums)
    for way, (src, dst) in enumerate(((0, 1), (1, 0))):
        bw, cw = bc[way]
        weight = halves(ends[way] * blk(dt, src))
        enter = halves(jnp.exp(excl[dst]))
        rows_s, rows_d = slice(src * BLK, (src + 1) * BLK), slice(dst * BLK, (dst + 1) * BLK)
        for c0 in range(0, sz.E, CHUNK):
            at = slice(c0, c0 + CHUNK)
            matrix = spread_matrix(c0 // HD, sz.H * way, CHUNK)
            xw = (conv_ref[rows_s, at] * mm(weight, matrix)).astype(BF16)
            state = (mm_tn(blk(bw, src), xw) * keep1).astype(BF16)
            y_ref[rows_d, at] += mm(blk(cw, dst), state) * mm(enter, matrix)


ROWS = 64
SEGMENTS = 4


def row_loop(sz, body, init):
    def step(n, carry):
        return body(pl.ds(pl.multiple_of(n * ROWS, ROWS), ROWS), n, carry)

    return lax.fori_loop(0, sz.T // ROWS, step, init)


def live_rows(n, live1):
    later = (n >= BLK // ROWS).astype(F32)
    return 1.0 + later * (live1 - 1.0)


def norm_in(sz, u_ref, gain, normed_ref):
    def body(at, n, _):
        u = u_ref[at, :].astype(F32)
        r = lax.rsqrt(jnp.mean(u * u, axis=-1, keepdims=True) + 1e-05)
        normed_ref[at, :] = (u * r * gain[...]).astype(BF16)
        return 0

    row_loop(sz, body, 0)


def project(sz, normed_ref, win_ref, proj_ref, cols=None):
    width = sz.NP // 9
    normed = normed_ref[...]
    for n in range(9):
        proj_ref[:, n * width : (n + 1) * width] = mm(normed, win_ref[:, n * width : (n + 1) * width])


def gate_mix(sz, at, y_ref, conv_ref, proj_ref, skipw):
    x = conv_ref[at, : sz.E]
    gate = proj_ref[at, : sz.E]
    mixed = y_ref[at, :] + x * skipw[...]
    sig = jax.nn.sigmoid(gate)
    act = gate * sig
    gated = mixed * act
    scale = lax.rsqrt(jnp.mean(gated * gated, axis=-1, keepdims=True) + 1e-05)
    return x, gate, mixed, sig, act, gated, scale


def post_mix(sz, y_ref, conv_ref, proj_ref, skipw, gain, nout_ref):
    def body(at, n, _):
        _, _, _, _, _, gated, scale = gate_mix(sz, at, y_ref, conv_ref, proj_ref, skipw)
        nout_ref[at, :] = (gated * scale * gain[...]).astype(BF16)
        return 0

    row_loop(sz, body, 0)


def forward_layer(sz, p, flags, u_ref, win_ref, wout_ref, proj_ref, y_ref, unext_ref, conv_ref,
                  normed_ref, nout_ref, colb, rowt, slope_ref=None, hook=lambda n: None):
    keep1, live1 = flags[0], flags[1]
    norm_in(sz, u_ref, p["gain_in"], normed_ref)
    hook(0)
    project(sz, normed_ref, win_ref, proj_ref)
    hook(1)
    cin_of = lambda n: proj_ref[:, pl.ds(pl.multiple_of(sz.E + n * LANES, LANES), LANES)]
    conv_phase(sz, cin_of, p["taps"], p["cbias"], keep1, conv_ref, slope_ref)
    hook(2)
    _, dt, a, sums = step_phase(sz, proj_ref[:, sz.STEP :], p["sbias"][...], p["decay"][...])
    bc = b_and_c(sz, conv_ref)
    forward_scan(sz, conv_ref, y_ref, colb, rowt, bc, dt, a, sums, keep1)
    hook(3)
    post_mix(sz, y_ref, conv_ref, proj_ref, p["skipw"], p["gain_out"], nout_ref)
    hook(4)
    branch = mm(nout_ref[...], wout_ref[...])
    first = u_ref[:BLK, :].astype(F32) + branch[:BLK]
    second = u_ref[BLK:, :].astype(F32) + live1 * branch[BLK:]
    unext_ref[:BLK, :] = first.astype(unext_ref.dtype)
    unext_ref[BLK:, :] = second.astype(unext_ref.dtype)


def fold8(v):
    out = v[0:8]
    for n in range(1, v.shape[0] // 8):
        out = out + v[n * 8 : (n + 1) * 8]
    return out


def colsum(v):
    return jnp.sum(v, axis=0, keepdims=True)


def backward_scan(sz, conv_ref, gy_ref, gx_ref, gbc_ref, colb, rowt, accs, z, dt, a, sums, keep1,
                  decay, hook):
    row, col = square_masks()
    low = row < col
    bc = b_and_c(sz, conv_ref)
    (bf, cf), (bb, cb) = bc
    excl = [sums[b] - blk(a, b) for b in range(2)]
    scores = []
    for b in range(2):
        sf = mm_nt(blk(bf, b), blk(cf, b))
        sb = mm_nt(blk(bb, b), blk(cb, b))
        scores.append(jnp.where(low, sf, jnp.where(row > col, sb, 0.0)))
        rowt[0, b] = excl[b].T
    gscore, rho_ref, kappa_ref = accs
    gscore[...] = jnp.zeros_like(gscore)
    kappa_ref[...] = jnp.zeros_like(kappa_ref)
    rho_ref[...] = jnp.zeros_like(rho_ref)
    lane = iota((BLK, LANES), 1)
    left = lane < HD

    def pair(first, p, _):
        at = pl.ds(pl.multiple_of(p * LANES, LANES), LANES)
        for b in range(2):
            rows = slice(b * BLK, (b + 1) * BLK)
            x = conv_ref[rows, at]
            gy = gy_ref[rows, at]
            x_two = jnp.concatenate([jnp.where(left, x, 0.0), jnp.where(left, 0.0, x)], axis=0)
            w_two = mm_nt(x_two.astype(BF16), gy)
            gxs = []
            gs = gscore[rows]
            kap = kappa_ref[rows]
            for hh in range(2):
                h = 2 * p + hh
                ex_row = jnp.where(low, rowt[0, b, pl.ds(h, 1)], rowt[0, b, pl.ds(sz.H + h, 1)])
                decay_m = jnp.exp(jnp.minimum(ex_row - colb[0, h - first, rows], 0.0))
                dtc = colb[1, h - first, rows]
                w = w_two[hh * BLK : (hh + 1) * BLK]
                es = decay_m * scores[b]
                gxs.append(mm((es * dtc).astype(BF16), gy))
                gs = gs + decay_m * w * dtc
                r = es * w
                q = r * dtc
                rl = jnp.where(low, r, 0.0)
                kap = jnp.where(lane == h, jnp.sum(rl, axis=1, keepdims=True), kap)
                kap = jnp.where(lane == sz.H + h, jnp.sum(r - rl, axis=1, keepdims=True), kap)
                ql = jnp.where(low, q, 0.0)
                rho_ref[b, pl.ds(h, 1)] = colsum(ql)
                rho_ref[b, pl.ds(sz.H + h, 1)] = colsum(q - ql)
            gscore[rows] = gs
            kappa_ref[rows] = kap
            gx_ref[rows, at] += jnp.where(left, gxs[0], gxs[1])
        return 0

    count = sz.H // SEGMENTS
    for seg in range(SEGMENTS):
        first = seg * count
        for h in range(first, first + count):
            for b in range(2):
                for n, v in ((0, sums[b]), (1, blk(dt, b))):
                    vf = jnp.broadcast_to(v[:, h : h + 1], (BLK, BLK))
                    vb = jnp.broadcast_to(v[:, sz.H + h : sz.H + h + 1], (BLK, BLK))
                    colb[n, h - first, b * BLK : (b + 1) * BLK] = jnp.where(low, vf, vb)
        lax.fori_loop(first // 2, (first + count) // 2, functools.partial(pair, first), 0, unroll=3)
        hook("scan")

    ends = carry_weights(sz, dt, sums)
    values, enters = [], []
    for way, (src, dst) in enumerate(((0, 1), (1, 0))):
        bw, cw = bc[way]
        rows_s, rows_d = slice(src * BLK, (src + 1) * BLK), slice(dst * BLK, (dst + 1) * BLK)
        weight_of = halves(ends[way] * blk(dt, src))
        enter_of = halves(jnp.exp(excl[dst]))
        value = enter = gb_s = gc_d = jnp.zeros((BLK, LANES), F32)
        for c0 in range(0, sz.E, CHUNK):
            at = slice(c0, c0 + CHUNK)
            matrix = spread_matrix(c0 // HD, sz.H * way, CHUNK)
            weight = mm(weight_of, matrix)
            x = conv_ref[rows_s, at]
            xw = (x * weight).astype(BF16)
            state = (mm_tn(blk(bw, src), xw) * keep1).astype(BF16)
            gcar = gy_ref[rows_d, at].astype(F32) * mm(enter_of, matrix)
            gcar_low = gcar.astype(BF16)
            enter = enter + mm_nt((gcar * mm(blk(cw, dst), state)).astype(BF16), matrix)
            gstate = (mm_tn(blk(cw, dst), gcar_low) * keep1).astype(BF16)
            gc_d = gc_d + mm_nt(gcar_low, state)
            gb_s = gb_s + mm_nt(xw, gstate)
            bg = mm(blk(bw, src), gstate)
            gx_ref[rows_s, at] += weight * bg
            value = value + mm_nt((x * bg).astype(BF16), matrix)
        values.append(value)
        enters.append(enter)
        gb, gc = [None, None], [None, None]
        for b in range(2):
            g = gscore[b * BLK : (b + 1) * BLK]
            g = jnp.where(low if way == 0 else row > col, g, 0.0).astype(BF16)
            gb[b] = mm(g, blk(cw, b))
            gc[b] = mm_tn(g, blk(bw, b))
        gb[src] = gb[src] + gb_s
        gc[dst] = gc[dst] + gc_d
        gc_all = jnp.concatenate(gc, axis=0)
        at = iota((sz.T, 1), 0)
        if way == 0:
            gc_all = jnp.where(at == sz.T - 1, 0.0, pltpu.roll(gc_all, sz.T - 1, 0))
        else:
            gc_all = jnp.where(at == 0, 0.0, pltpu.roll(gc_all, 1, 0))
        gb_all = jnp.concatenate(gb, axis=0)
        wide_lane = iota((sz.T, LANES), 1)
        gbc_ref[:, way * LANES : (way + 1) * LANES] = jnp.where(
            wide_lane < 64, gb_all, pltpu.roll(gc_all, 64, 1)
        )

    strict_low = (row > col).astype(F32)
    strict_up = (row < col).astype(F32)
    is_f = lane < sz.H
    is_b = (lane >= sz.H) & (lane < 2 * sz.H)
    gsteps, gdecay = [], None
    for b in range(2):
        kr = kappa_ref[b * BLK : (b + 1) * BLK]
        kap = kr * blk(dt, b)
        rho = rho_ref[b].T
        if b == 1:
            rho = rho + jnp.where(is_f, enters[0], 0.0)
            zr = jnp.where(is_b, values[1], 0.0) * ends[1]
        else:
            rho = rho + jnp.where(is_b, enters[1], 0.0)
            zr = jnp.where(is_f, values[0], 0.0) * ends[0]
        zed = zr * blk(dt, b)
        diff = rho - kap
        both = jnp.concatenate([diff, zed], axis=1)
        up, down = mm_exact(strict_up, both), mm_exact(strict_low, both)
        ga = jnp.where(
            is_f, up[:, :LANES] + down[:, LANES:], down[:, :LANES] + up[:, LANES:]
        ) - kap
        ga = jnp.where(is_f | is_b, ga, 0.0)
        gdt = jnp.where(is_f | is_b, kr + zr, 0.0) - ga * decay
        gsteps.append(gdt * jax.nn.sigmoid(blk(z, b)))
        part = colsum(ga * blk(a, b))
        gdecay = part if gdecay is None else gdecay + part
    return jnp.concatenate(gsteps, axis=0), gdecay


def backward_layer(sz, p, flags, g_ref, u_ref, win_ref, wout_ref, proj_ref, y_ref, gu_ref,
                   gwin_ref, gwout_ref, small_ref, head_ref, s, hook=lambda name: None):
    keep1, live1 = flags[0], flags[1]
    conv_ref, slope_ref, gx_ref, gproj_ref = s["conv"], s["slope"], s["gx"], s["gproj"]
    D, E, CW = sz.D, sz.E, sz.CW
    hook("start")

    def mask_g(at, n, _):
        s["gb"][at, :] = (g_ref[at, :].astype(F32) * live_rows(n, live1)).astype(BF16)
        return 0

    row_loop(sz, mask_g, 0)
    hook("w_out")
    gx_ref[...] = mm_nt(s["gb"][...], wout_ref[...])
    hook("proj")
    cin_of = lambda n: proj_ref[:, pl.ds(pl.multiple_of(E + n * LANES, LANES), LANES)]
    conv_phase(sz, cin_of, p["taps"], p["cbias"], keep1, conv_ref, slope_ref)
    s["acc"][...] = jnp.zeros_like(s["acc"])
    hook("y")

    def post_back(at, n, _):
        x, gate, mixed, sig, act, gated, scale = gate_mix(sz, at, y_ref, conv_ref, proj_ref, p["skipw"])
        hat = gated * scale
        gn = gx_ref[at, :]
        s["acc"][0] += fold8(gn * hat)
        gproj_ref[at, E : 2 * E] = (hat * p["gain_out"][...]).astype(BF16)
        gh = gn * p["gain_out"][...]
        gg = scale * (gh - hat * jnp.mean(gh * hat, axis=-1, keepdims=True))
        gm = gg * act
        gproj_ref[at, :E] = (gg * mixed * (sig + act * (1.0 - sig))).astype(BF16)
        s["gy"][at, :] = gm.astype(BF16)
        gx_ref[at, :] = gm * p["skipw"][...]
        s["acc"][1] += fold8(gm * x)
        return 0

    row_loop(sz, post_back, 0)
    hook("post")
    small_ref[6:7, :E] = colsum(s["acc"][0])
    for c0 in range(0, E, 2 * LANES):
        part = mm_tn(gproj_ref[:, E + c0 : E + c0 + 2 * LANES], s["gb"][...])
        gwout_ref[c0 : c0 + 2 * LANES, :] = part.astype(BF16)
    hook("g_out")
    norm_in(sz, u_ref, p["gain_in"], s["normed"])
    width = sz.NP // 9
    normed = s["normed"][...]

    def grad_win(columns):
        for n in columns:
            at = slice(n * width, (n + 1) * width)
            gwin_ref[:, at] = mm_tn(normed, gproj_ref[:, at]).astype(BF16)

    grad_win(range(E // width))
    hook("g_gate")
    z, dt, a, sums = step_phase(sz, proj_ref[:, sz.STEP :], p["sbias"][...], p["decay"][...])
    gsteps, gdecay = backward_scan(
        sz, conv_ref, s["gy"], gx_ref, s["gbc"], s["colb"], s["rowt"],
        (s["gscore"], s["rho"], s["kappa"]), z, dt, a, sums, keep1, p["decay"][...], hook,
    )
    hook("scan")
    gproj_ref[:, sz.STEP :] = gsteps.astype(BF16)
    skip_sum = s["acc"][1]
    first = skip_sum.astype(BF16)
    rest = (skip_sum - first.astype(F32)).astype(BF16)
    matrix = spread_matrix(0, 0, E)
    gskip = colsum(mm_nt(first, matrix) + mm_nt(rest, matrix))
    head_ref[...] = jnp.zeros_like(head_ref)
    head_ref[0:1, :] = colsum(gsteps)
    head_ref[1:2, :] = gdecay
    head_ref[2:3, :] = gskip

    keeps = [None] + [lag_keep(keep1, k) for k in range(1, 4)]

    def conv_chunk(n, gout):
        at = pl.ds(pl.multiple_of(n * LANES, LANES), LANES)
        wide = pl.ds(pl.multiple_of(E + n * LANES, LANES), LANES)
        cin = proj_ref[:, wide]
        gz = gout * slope_ref[:, at].astype(F32)
        taps = p["taps"]
        gc = taps[0:1, at] * gz
        small_ref[1:2, at] = colsum(gz * cin)
        for k in range(1, 4):
            gk = gz * keeps[k]
            small_ref[1 + k : 2 + k, at] = colsum(gk * pltpu.roll(cin, k, 0))
            gc = gc + taps[k : k + 1, at] * pltpu.roll(gk, sz.T - k, 0)
        small_ref[5:6, at] = colsum(gz)
        gproj_ref[:, wide] = gc.astype(BF16)

    def x_chunk(n, _):
        conv_chunk(n, gx_ref[:, pl.ds(pl.multiple_of(n * LANES, LANES), LANES)])
        return 0

    lax.fori_loop(0, E // LANES, x_chunk, 0)
    for n in range((CW - E) // LANES):
        conv_chunk(E // LANES + n, s["gbc"][:, n * LANES : (n + 1) * LANES])
    hook("conv")
    grad_win(range(E // width, 9))
    hook("g_conv")
    hook("w_in")
    for n in range(9):
        at = slice(n * width, (n + 1) * width)
        part = mm_nt(gproj_ref[:, at], win_ref[:, at])
        gx_ref[:, :D] = part if n == 0 else gx_ref[:, :D] + part
    s["acc"][0] = jnp.zeros_like(s["acc"][0])
    hook("normed")

    def in_back(at, n, _):
        u = u_ref[at, :].astype(F32)
        r = lax.rsqrt(jnp.mean(u * u, axis=-1, keepdims=True) + 1e-05)
        hat = u * r
        gn = gx_ref[at, :D]
        s["acc"][0, :, :D] += fold8(gn * hat)
        gh = gn * p["gain_in"][...]
        gu = r * (gh - hat * jnp.mean(gh * hat, axis=-1, keepdims=True))
        gu_ref[at, :] = (g_ref[at, :].astype(F32) + gu).astype(gu_ref.dtype)
        return 0

    row_loop(sz, in_back, 0)
    small_ref[0:1, :D] = colsum(s["acc"][0, :, :D])
    hook("end")


def backward_scratch(sz):
    T, E, CW, D, H = sz.T, sz.E, sz.CW, sz.D, sz.H
    return dict(
        conv=pltpu.VMEM((T, CW), F32),
        slope=pltpu.VMEM((T, CW), BF16),
        normed=pltpu.VMEM((T, D), BF16),
        gb=pltpu.VMEM((T, D), BF16),
        gx=pltpu.VMEM((T, E), F32),
        gy=pltpu.VMEM((T, E), BF16),
        gproj=pltpu.VMEM((T, sz.NP), BF16),
        gbc=pltpu.VMEM((T, 2 * LANES), F32),
        acc=pltpu.VMEM((2, 8, E), F32),
        colb=pltpu.VMEM((2, H // SEGMENTS, T, BLK), F32),
        rowt=pltpu.VMEM((2, 2, LANES, BLK), F32),
        gscore=pltpu.VMEM((T, BLK), F32),
        rho=pltpu.VMEM((2, LANES, BLK), F32),
        kappa=pltpu.VMEM((T, LANES), F32),
    )


PARAMS = ("gain_in", "taps", "cbias", "sbias", "decay", "skipw", "gain_out")


MESH = pl.DeviceIdType.MESH


def remote(src, dst, ssem, rsem, device):
    return pltpu.make_async_remote_copy(
        src, dst, ssem, rsem, device_id=device, device_id_type=MESH
    )


class Ring:
    def __init__(self, ndp, both_ways=True):
        nc = ndp // 2
        self.nc, self.ndp = nc, ndp
        self.plus = nc // 2 if both_ways else nc - 1
        self.minus = nc - 1 - self.plus
        self.d, self.me = lax.axis_index("dir"), lax.axis_index("dp")
        p, self.c = self.me // 2, self.me % 2
        odd = p % 2
        self.pos = (1 - odd) * (p // 2) + odd * (nc - 1 - p // 2)
        self.turn = 1 - 2 * self.c
        self.nxt = (self.d, 2 * self.chip(1) + self.c)
        self.prv = (self.d, 2 * self.chip(-1) + self.c)
        self.sib = (self.d, 2 * p + 1 - self.c)
        self.mate = (1 - self.d, self.me)

    def chip(self, ahead):
        nc = self.nc
        pos = (self.pos + ahead * self.turn + nc) % nc
        half = pos // (nc // 2)
        return (1 - half) * 2 * pos + half * (2 * (nc - 1 - pos) + 1)

    def flip(self, bit):
        return (self.d, self.me + (1 - 2 * ((self.me // bit) % 2)) * bit)

    def flips(self):
        return [self.flip(1 << n) for n in range(self.ndp.bit_length() - 1)]

    def barrier(self, more=()):
        bar = pltpu.get_barrier_semaphore()
        greeted = (self.nxt, self.prv, self.sib, self.mate) + tuple(more)
        for device in greeted:
            pl.semaphore_signal(bar, inc=1, device_id=device, device_id_type=MESH)
        pl.semaphore_wait(bar, len(greeted))

    def hops(self):
        out = []
        for s in range(1, self.plus + 1):
            out.append((1, s))
            if s <= self.minus:
                out.append((-1, s))
        return out

    def index(self, sign, hop):
        return hop if sign > 0 else self.plus + hop


def cols(start, width):
    if isinstance(start, int):
        return pl.ds(start, width)
    return pl.ds(pl.multiple_of(start, LANES), width)


def rows_at(slot, count):
    return pl.ds(pl.multiple_of(slot * count, 16), count)


class Gather:
    def __init__(self, ring, groups, parts, sems):
        self.r, self.g, self.parts = ring, groups, parts
        self.arrive, self.beside, self.along, self.aside, self.across = sems[:5]
        self.local = sems[5]

    @staticmethod
    def scratch(ndp, groups):
        return [pltpu.SemaphoreType.DMA((3 * groups, ndp // 2))] * 5 + [
            pltpu.SemaphoreType.DMA((groups,))
        ]

    def view(self, g, ref, slot, k):
        rows = self.g[g][0].shape[0]
        w, w2 = self.parts[g]
        at = cols(2 * w, w2) if k == 1 else cols((self.r.d if k == 0 else 1 - self.r.d) * w, w)
        return ref.at[:, at] if slot is None else ref.at[rows_at(slot, rows), at]

    def copies(self, g, k, sign, hop):
        r, (src, dst) = self.r, self.g[g]
        m, n = 3 * g + k, (0 if hop == 0 else r.index(sign, hop))
        here = self.view(g, dst, 2 * r.chip(-sign * hop) + r.c, k)
        frm = self.view(g, src, None, k) if hop == 0 else here
        out = []
        if k < 2:
            for way, limit, device in ((1, r.plus, r.nxt), (-1, r.minus, r.prv)):
                if (hop == 0 or way == sign) and hop < limit:
                    to = r.index(way, hop + 1)
                    out.append(remote(frm, here, self.along.at[m, to], self.arrive.at[m, to], device))
        if k == 0 and hop > 0:
            out.append(
                remote(frm, here, self.across.at[m, n], self.arrive.at[m + 2, n], r.mate)
            )
        out.append(remote(frm, here, self.aside.at[m, n], self.beside.at[m, n], r.sib))
        return here, out

    def own(self, g):
        src, dst = self.g[g]
        return pltpu.make_async_copy(
            src, dst.at[rows_at(self.r.me, src.shape[0])], self.local.at[g]
        )

    def event(self, g, k, sign, hop):
        here, out = self.copies(g, k, sign, hop)
        if hop > 0:
            m, n = 3 * g + k, self.r.index(sign, hop)
            remote(here, here, self.along.at[m, n], self.arrive.at[m, n], self.r.nxt).wait_recv()
        for copy in out:
            copy.start()

    def kinds(self, g):
        return (0, 1, 2) if self.parts[g][0] else (1,)

    def begin(self, groups):
        for g in groups:
            for k in self.kinds(g):
                self.event(g, k, 1, 0)
            self.own(g).start()

    def rounds(self, g):
        near = {}
        for sign, hop in self.r.hops():
            near.setdefault(hop, []).append(sign)
        out, late = [[(self.begin, ([g],))]], []
        for hop, signs in near.items():
            now = [
                (self.event, (g, k, sign, hop))
                for k in self.kinds(g) if k < 2 for sign in signs
            ]
            out.append(now + late)
            late = [(self.event, (g, 2, sign, hop)) for sign in signs if 2 in self.kinds(g)]
        return out + ([late] if late else [])

    def finish(self, groups):
        r = self.r
        for g in groups:
            src, dst = self.g[g]
            for k in self.kinds(g):
                for sign, hop in [(1, 0)] + r.hops():
                    m, n = 3 * g + k, (0 if hop == 0 else r.index(sign, hop))
                    there = self.view(g, dst, 2 * r.chip(sign * hop) + 1 - r.c, k)
                    remote(
                        there, there, self.aside.at[m, n], self.beside.at[m, n], r.sib
                    ).wait_recv()
            self.own(g).wait()

    def drain(self, groups):
        for g in groups:
            for k in self.kinds(g):
                for sign, hop in [(1, 0)] + self.r.hops():
                    for copy in self.copies(g, k, sign, hop)[1]:
                        copy.wait_send()


class Scatter:
    def __init__(self, ring, groups, parts, bufs, sems):
        self.r, self.g, self.parts, self.bufs = ring, groups, parts, bufs
        (self.s_sib, self.r_sib, self.s_mate, self.r_mate, self.s_ring, self.r_ring,
         self.s_end, self.r_end) = sems

    @staticmethod
    def scratch(ndp, shapes, parts):
        nc = ndp // 2
        bufs = []
        for (rows, width), (w, w2) in zip(shapes, parts):
            bufs += [
                pltpu.VMEM((nc, rows, width), BF16),
                pltpu.VMEM((nc, rows, w) if w else (1, 16, LANES), BF16),
                pltpu.VMEM((nc + 1, rows, w + w2), BF16),
                pltpu.VMEM((2, rows, w + w2), BF16),
            ]
        n = len(shapes)
        sems = [pltpu.SemaphoreType.DMA((n, nc))] * 4 + [
            pltpu.SemaphoreType.DMA((2 * n, nc + 1))
        ] * 2 + [pltpu.SemaphoreType.DMA((n,))] * 2
        return bufs, sems

    def buf(self, g):
        return self.bufs[4 * g : 4 * g + 4]

    def span(self, g, k):
        w, w2 = self.parts[g]
        if k == 1:
            return cols(2 * w, w2)
        return cols((self.r.d if k == 0 else 1 - self.r.d) * w, w)

    def packed(self, g, k):
        w, w2 = self.parts[g]
        return pl.ds(0, w) if k == 0 else pl.ds(w, w2)

    def order(self):
        r, out = self.r, []
        for s in range(r.plus):
            out.append(r.plus - s)
            if s < r.minus:
                out.append(-(r.minus - s))
        return out + [0]

    def number(self, ahead):
        return ahead % self.r.nc

    def sib_copy(self, g, ahead):
        r, own, n = self.r, self.g[g], self.number(ahead)
        sib = self.buf(g)[0]
        rows = sib.shape[1]
        src = own.at[rows_at(2 * r.chip(-ahead) + 1 - r.c, rows)]
        return remote(src, sib.at[n], self.s_sib.at[g, n], self.r_sib.at[g, n], r.sib)

    def mate_copy(self, g, ahead):
        r, n = self.r, self.number(ahead)
        sib, mate = self.buf(g)[:2]
        src = sib.at[n, :, self.span(g, 2)]
        return remote(src, mate.at[n], self.s_mate.at[g, n], self.r_mate.at[g, n], r.mate)

    def ring_copy(self, g, k, sign, step):
        r = self.r
        run = self.buf(g)[2]
        frm = run.at[self.slot(sign, step), :, self.packed(g, k)]
        to = run.at[self.slot(sign, step + 1), :, self.packed(g, k)]
        n = self.slot(sign, step + 1)
        device = r.nxt if sign > 0 else r.prv
        return remote(
            frm, to, self.s_ring.at[2 * g + k, n], self.r_ring.at[2 * g + k, n], device
        )

    def slot(self, sign, step):
        return step if sign > 0 else self.r.plus + 1 + step

    def kinds(self, g):
        return (0, 1) if self.parts[g][0] else (1,)

    def begin(self, groups):
        for g in groups:
            for ahead in self.order():
                self.sib_copy(g, ahead).start()

    def hand_over(self, g, ahead):
        r, own, n = self.r, self.g[g], self.number(ahead)
        sib = self.buf(g)[0]
        rows = sib.shape[1]
        self.sib_copy(g, ahead).wait_recv()
        if not self.parts[g][0]:
            return
        first = (2 * r.chip(ahead) + r.c) * rows
        at = self.span(g, 2)

        def part(n16, _):
            inner = pl.ds(pl.multiple_of(n16 * 16, 16), 16)
            outer = pl.ds(pl.multiple_of(first + n16 * 16, 16), 16)
            sib[n, inner, at] = (own[outer, at].astype(F32) + sib[n, inner, at].astype(F32)).astype(BF16)
            return 0

        lax.fori_loop(0, rows // 16, part, 0)
        self.mate_copy(g, ahead).start()

    def step(self, g, k, sign, step):
        r, own = self.r, self.g[g]
        sib, mate, run, end = self.buf(g)
        rows = sib.shape[1]
        last = r.plus if sign > 0 else r.minus
        ahead = sign * (last - step)
        n = self.number(ahead)
        if k == 0:
            self.mate_copy(g, ahead).wait_recv()
        if step > 0:
            self.ring_copy(g, k, sign, step - 1).wait_recv()
        first = (2 * r.chip(ahead) + r.c) * rows
        at, mine = self.span(g, k), self.packed(g, k)
        here = self.slot(sign, step)

        def part(n16, _):
            inner = pl.ds(pl.multiple_of(n16 * 16, 16), 16)
            outer = pl.ds(pl.multiple_of(first + n16 * 16, 16), 16)
            total = own[outer, at].astype(F32) + sib[n, inner, at].astype(F32)
            if k == 0:
                total = total + mate[n, inner, :].astype(F32)
            if step > 0:
                total = total + run[here, inner, mine].astype(F32)
            run[here, inner, mine] = total.astype(BF16)
            return 0

        lax.fori_loop(0, rows // 16, part, 0)
        self.ring_copy(g, k, sign, step).start()

    def own_sum(self, g):
        r, own = self.r, self.g[g]
        sib, mate, run, end = self.buf(g)
        rows = sib.shape[1]
        if 0 in self.kinds(g):
            self.mate_copy(g, 0).wait_recv()
        for k in self.kinds(g):
            self.ring_copy(g, k, 1, r.plus - 1).wait_recv()
            self.ring_copy(g, k, -1, r.minus - 1).wait_recv()
        first = (2 * r.chip(0) + r.c) * rows

        def part(n16, _):
            inner = pl.ds(pl.multiple_of(n16 * 16, 16), 16)
            outer = pl.ds(pl.multiple_of(first + n16 * 16, 16), 16)
            for k in self.kinds(g):
                at, mine = self.span(g, k), self.packed(g, k)
                total = own[outer, at].astype(F32) + sib[0, inner, at].astype(F32)
                if k == 0:
                    total = total + mate[0, inner, :].astype(F32)
                total = total + run[self.slot(1, r.plus), inner, mine].astype(F32)
                total = total + run[self.slot(-1, r.minus), inner, mine].astype(F32)
                end[0, inner, mine] = total.astype(BF16)
            return 0

        lax.fori_loop(0, rows // 16, part, 0)
        self.end_copy(g).start()

    def end_copy(self, g):
        end = self.buf(g)[3]
        return remote(end.at[0], end.at[1], self.s_end.at[g], self.r_end.at[g], self.r.mate)

    def result(self, g, out):
        end = self.buf(g)[3]
        rows = end.shape[1]
        self.end_copy(g).wait_recv()

        def part(n16, _):
            inner = pl.ds(pl.multiple_of(n16 * 16, 16), 16)
            mine0, mine1 = self.packed(g, 0), self.packed(g, 1)
            if 0 in self.kinds(g):
                out[inner, self.span(g, 0)] = end[0, inner, mine0].astype(F32)
                out[inner, self.span(g, 2)] = end[1, inner, mine0].astype(F32)
            out[inner, self.span(g, 1)] = end[0, inner, mine1].astype(F32) + end[1, inner, mine1].astype(F32)
            return 0

        lax.fori_loop(0, rows // 16, part, 0)

    def rounds(self, g):
        r = self.r
        over = [(self.hand_over, (g, ahead)) for ahead in self.order()]
        out, waiting = [], []
        for s in range(r.plus):
            signs = (1, -1) if s < r.minus else (1,)
            hand, over = over[: 4 if s == 0 else 2], over[4 if s == 0 else 2 :]
            steps = [(self.step, (g, 1, sign, s)) for sign in signs]
            out.append((hand if s == 0 else []) + steps + waiting + (hand if s > 0 else []))
            waiting = [(self.step, (g, 0, sign, s)) for sign in signs if 0 in self.kinds(g)]
        last = [waiting + over] if waiting + over else []
        return out + last + [[(self.own_sum, (g,))]]

    def drain(self, groups):
        r = self.r
        for g in groups:
            for ahead in self.order():
                self.sib_copy(g, ahead).wait_send()
                if 0 in self.kinds(g):
                    self.mate_copy(g, ahead).wait_send()
            for k in self.kinds(g):
                for s in range(r.plus):
                    self.ring_copy(g, k, 1, s).wait_send()
                for s in range(r.minus):
                    self.ring_copy(g, k, -1, s).wait_send()
            self.end_copy(g).wait_send()


class AllSum:
    @staticmethod
    def scratch(ndp, shape):
        n = ndp.bit_length()
        return [pltpu.VMEM((n,) + shape, F32), pltpu.SemaphoreType.DMA((n,)), pltpu.SemaphoreType.DMA((n,))]

    def __init__(self, ring, acc, bufs):
        self.acc, (self.buf, self.s, self.r) = acc, bufs
        self.partners = [ring.mate] + ring.flips()

    def copy(self, n):
        return remote(self.acc, self.buf.at[n], self.s.at[n], self.r.at[n], self.partners[n])

    def start(self, n):
        self.copy(n).start()

    def end(self, n):
        self.copy(n).wait()
        self.acc[...] += self.buf[n]

    def rounds(self):
        out = [[(self.start, (0,))]]
        for n in range(len(self.partners)):
            out.append([(self.end, (n,))])
            if n + 1 < len(self.partners):
                out[-1].append((self.start, (n + 1,)))
        return out


class Pump:
    def __init__(self):
        self.active = {}

    def add(self, kind, number, rounds, delay=0):
        self.active[kind, number] = [[]] * delay + list(rounds)

    def tick(self):
        queues = [self.active[key].pop(0) for key in list(self.active) if key[0] == "t"]
        sums = [self.active[key].pop(0) for key in list(self.active) if key[0] == "s"]
        for n in range(max([len(q) for q in queues], default=0)):
            for queue in queues:
                if n < len(queue):
                    call, args = queue[n]
                    call(*args)
        for queue in sums:
            for call, args in queue:
                call(*args)
        self.active = {key: rounds for key, rounds in self.active.items() if rounds}

    def until(self, *numbers):
        while any(("t", number) in self.active for number in numbers):
            self.tick()

    def rest(self):
        while self.active:
            self.tick()


VM = pl.BlockSpec(memory_space=pltpu.VMEM)
SM = pl.BlockSpec(memory_space=pltpu.SMEM)
ANY = pl.BlockSpec(memory_space=pl.ANY)
ROOM = 127 << 19
TABLE_ROWS = 16


def table_params(sz, tab):
    return dict(
        gain_in=tab.at[0:1, : sz.D],
        taps=tab.at[1:5],
        cbias=tab.at[5:6],
        gain_out=tab.at[6:7, : sz.E],
        sbias=tab.at[7:8, :LANES],
        decay=tab.at[8:9, :LANES],
        skipw=tab.at[9:10, : sz.E],
    )


def run_flags(spans, d):
    begin, opens = jnp.int32(0), jnp.int32(0)
    for s in range(spans.shape[1]):
        length = spans[d, s]
        starts = jnp.where(begin == 1, 1, 0) * jnp.where(length > 0, 1, 0)
        opens = jnp.maximum(opens, starts)
        begin = begin + length
    live = jnp.where(begin > 1, 1.0, 0.0).astype(F32)
    opened = jnp.maximum(opens.astype(F32), 1.0 - live)
    return 1.0 - opened, live


AG_IN, AG_OUT = 9, 2


class Plan:
    def __init__(self, layers, taps, ndp, sz, n_in, n_conv, n_out):
        self.L, self.K, self.ndp, self.sz = layers, taps, ndp, sz
        self.n_in, self.n_conv, self.n_out = n_in, n_conv, n_out
        self.ag_in = (AG_IN * LANES, sz.NP - 2 * AG_IN * LANES)
        self.ag_out = (AG_OUT * LANES, sz.D - 2 * AG_OUT * LANES)
        tiles = lambda width: width // LANES
        gate, rest, out = tiles(sz.E), tiles(sz.NP - sz.E), tiles(sz.D)
        cut = lambda width, part: (part * LANES, (width - 2 * part) * LANES)
        self.rs_parts = [
            [cut(out, OUT_PARTS[l]), cut(gate, GATE_PARTS[l]), cut(rest, REST_PARTS[l])]
            for l in range(layers)
        ]
        self.rs_widths = [sz.D, sz.E, sz.NP - sz.E]
        self.rs_rows = [sz.E // ndp] + [sz.D // ndp] * 2


OUT_PARTS, GATE_PARTS, REST_PARTS = (1, 1), (3, 3), (0, 3)


def stage_own(pl_, ins, stage, smallf, small, sems):
    sz = pl_.sz
    w_gate, w_conv, w_step, in_gain, conv_weight, conv_bias, out_gain = ins
    copies = []
    for l in range(pl_.L):
        copies.append(
            pltpu.make_async_copy(w_gate.at[l], stage.at[l, :, pl.ds(0, sz.E)], sems.at[2 * l])
        )
        copies.append(
            pltpu.make_async_copy(
                w_conv.at[l], stage.at[l, :, pl.ds(sz.E, sz.CW)], sems.at[2 * l + 1]
            )
        )
    for copy in copies:
        copy.start()
    smallf[...] = jnp.zeros_like(smallf)
    L, K = pl_.L, pl_.K
    smallf[0:L, : pl_.n_in] = in_gain[...].astype(F32)
    for l in range(L):
        smallf[L + l * K : L + (l + 1) * K, : pl_.n_conv] = conv_weight[l].astype(F32)
    smallf[L + L * K : 2 * L + L * K, : pl_.n_conv] = conv_bias[...].astype(F32)
    smallf[2 * L + L * K : 3 * L + L * K, : pl_.n_out] = out_gain[...].astype(F32)
    small[...] = smallf[...].astype(BF16)
    for l in range(L):
        stage[l, :, sz.STEP :] = jnp.zeros((stage.shape[1], LANES), BF16)
        stage[l, :, sz.STEP : sz.STEP + 2 * sz.H] = w_step[l]
    for copy in copies:
        copy.wait()


def fill_table(pl_, table, gathered, step_bias, decay_log, skip_gain):
    sz, L, K = pl_.sz, pl_.L, pl_.K
    table[...] = jnp.zeros_like(table)
    rows = gathered.shape[0] // pl_.ndp
    for q in range(pl_.ndp):
        part = gathered[q * rows : (q + 1) * rows, :].astype(F32)
        for l in range(L):
            table[l, 0:1, q * pl_.n_in : (q + 1) * pl_.n_in] = part[l : l + 1, : pl_.n_in]
            conv = slice(q * pl_.n_conv, (q + 1) * pl_.n_conv)
            table[l, 1 : 1 + K, conv] = part[L + l * K : L + (l + 1) * K, : pl_.n_conv]
            at = L + L * K + l
            table[l, 5:6, conv] = part[at : at + 1, : pl_.n_conv]
            out = slice(q * pl_.n_out, (q + 1) * pl_.n_out)
            table[l, 6:7, out] = part[at + L : at + L + 1, : pl_.n_out]
    head_of = iota((sz.H, sz.E), 1) // HD
    one_hot = (iota((sz.H, sz.E), 0) == head_of).astype(F32)
    wide = mm_exact(skip_gain[...], one_hot)
    decay = jnp.exp(decay_log[...])
    for l in range(L):
        table[l, 7:8, : 2 * sz.H] = step_bias[l : l + 1, :]
        table[l, 8:9, : sz.H] = decay[l : l + 1]
        table[l, 8:9, sz.H : 2 * sz.H] = decay[l : l + 1]
        table[l, 9:10, : sz.E] = wide[l : l + 1]


def forward_kernel(pl_, *refs):
    sz, L = pl_.sz, pl_.L
    (spans, u0, w_gate, w_conv, w_step, in_gain, conv_weight, conv_bias, out_gain, w_out,
     step_bias, decay_log, skip_gain) = refs[:13]
    out_w = refs[13 : 13 + 2 * L]
    out_s = refs[13 + 2 * L : 13 + 5 * L]
    table = refs[13 + 5 * L]
    rest = refs[14 + 5 * L :]
    full, rest = rest[: 2 * L], rest[2 * L :]
    saved, rest = rest[: 3 * L], rest[3 * L :]
    conv, normed, nout, colb, rowt, stage, smallf, small, gathered, own_sems, out_sems = rest[:11]
    sems = rest[11:]
    ring = Ring(pl_.ndp)
    ring.barrier()
    flags = run_flags(spans, ring.d)
    stage_own(pl_, (w_gate, w_conv, w_step, in_gain, conv_weight, conv_bias, out_gain),
              stage, smallf, small, own_sems)
    groups, parts = [(small, gathered)], [(0, LANES)]
    for l in range(L):
        groups += [(stage.at[l], full[2 * l]), (w_out.at[l], full[2 * l + 1])]
        parts += [pl_.ag_in, pl_.ag_out]
    gather = Gather(ring, groups, parts, sems)
    pump = Pump()
    for g, start in enumerate(STARTS):
        pump.add("t", g, gather.rounds(g), start)
    pump.until(0, 1)
    gather.finish([0])
    fill_table(pl_, table, gathered, step_bias, decay_log, skip_gain)
    outward = []

    def send_out(src, dst):
        copy = pltpu.make_async_copy(src, dst, out_sems.at[len(outward)])
        copy.start()
        outward.append(copy)

    u = u0.at[ring.d]
    for l in range(L):
        g_in, g_out = 1 + 2 * l, 2 + 2 * l
        pump.until(g_in)
        gather.finish([g_in])
        send_out(full[2 * l], out_w[2 * l])
        proj, y, unext = saved[3 * l : 3 * l + 3]

        def hook(n):
            if n == 1:
                send_out(proj, out_s[3 * l])
            if n == 4:
                send_out(y, out_s[3 * l + 1])
                pump.until(g_out)
                gather.finish([g_out])
                send_out(full[2 * l + 1], out_w[2 * l + 1])
            elif n in TICKS_F:
                pump.tick()

        forward_layer(sz, table_params(sz, table.at[l]), flags, u, full[2 * l], full[2 * l + 1],
                      proj, y, unext, conv, normed, nout, colb, rowt, hook=hook)
        send_out(unext, out_s[3 * l + 2])
        u = unext
    gather.drain(range(len(groups)))
    for copy in outward:
        copy.wait()


STARTS = (0, 0, 2, 3, 6)
TICKS_F = (0, 2, 3)


def forward_call(pl_, spans, u0, w_gate, w_conv, w_step, in_gain, conv_weight, conv_bias, out_gain,
                 w_out, step_bias, decay_log, skip_gain):
    sz, L = pl_.sz, pl_.L
    full = [((sz.D, sz.NP), BF16), ((sz.E, sz.D), BF16)] * L
    kept = []
    for l in range(L):
        kept += [((sz.T, sz.NP), F32), ((sz.T, sz.E), F32), ((sz.T, sz.D), BF16 if l == L - 1 else F32)]
    shapes = [jax.ShapeDtypeStruct(*s) for s in full + kept]
    return pl.pallas_call(
        functools.partial(forward_kernel, pl_),
        out_shape=shapes + [jax.ShapeDtypeStruct((L, TABLE_ROWS, sz.CW), F32)],
        in_specs=[SM, VM, ANY, ANY] + [VM] * 5 + [ANY] + [VM] * 3,
        out_specs=[ANY] * len(shapes) + [VM],
        scratch_shapes=[pltpu.VMEM(*s) for s in full + kept] + forward_scratch(sz) + [
            pltpu.VMEM((L, w_gate.shape[1], sz.NP), BF16),
            pltpu.VMEM((16, LANES), F32),
            pltpu.VMEM((16, LANES), BF16),
            pltpu.VMEM((16 * pl_.ndp, LANES), BF16),
            pltpu.SemaphoreType.DMA((2 * L,)),
            pltpu.SemaphoreType.DMA((len(shapes),)),
        ] + Gather.scratch(pl_.ndp, 1 + 2 * L),
        compiler_params=pltpu.CompilerParams(
            collective_id=1, has_side_effects=True, vmem_limit_bytes=ROOM
        ),
    )(spans, u0, w_gate, w_conv, w_step, in_gain, conv_weight, conv_bias, out_gain, w_out,
      step_bias, decay_log, skip_gain)


def fwd_kernel(sz, layer, spans, u, win, wout, table, proj, y, unext, conv, normed, nout, colb, rowt):
    d = lax.axis_index("dir")
    flags = run_flags(spans, d)
    forward_layer(sz, table_params(sz, table.at[layer]), flags, u.at[d] if layer == 0 else u,
                  win, wout, proj, y, unext, conv, normed, nout, colb, rowt)


def forward_scratch(sz):
    return [
        pltpu.VMEM((sz.T, sz.CW), F32),
        pltpu.VMEM((sz.T, sz.D), BF16),
        pltpu.VMEM((sz.T, sz.E), BF16),
        pltpu.VMEM((1, sz.H, sz.T, BLK), F32),
        pltpu.VMEM((2, 2, LANES, BLK), F32),
    ]


def saved_shapes(sz):
    return [
        jax.ShapeDtypeStruct((sz.T, sz.NP), F32),
        jax.ShapeDtypeStruct((sz.T, sz.E), F32),
        jax.ShapeDtypeStruct((sz.T, sz.D), F32),
    ]


def fwd_call(sz, layer, spans, u, win, wout, table):
    return pl.pallas_call(
        functools.partial(fwd_kernel, sz, layer),
        out_shape=saved_shapes(sz),
        in_specs=[SM] + [VM] * 4,
        out_specs=[VM] * 3,
        scratch_shapes=forward_scratch(sz),
        compiler_params=pltpu.CompilerParams(vmem_limit_bytes=ROOM),
    )(spans, u, win, wout, table)


def bwd_kernel(sz, layer, last, names, spans, g, u, win, wout, proj, y, table, gu, gwin, gwout,
               small, head, *rest):
    d = lax.axis_index("dir")
    flags = run_flags(spans, d)
    backward_layer(sz, table_params(sz, table.at[layer]), flags, g.at[d] if last else g,
                   u.at[d] if layer == 0 else u, win, wout, proj, y, gu, gwin, gwout, small, head,
                   dict(zip(names, rest)))


def grad_shapes(sz):
    return [
        jax.ShapeDtypeStruct((sz.T, sz.D), F32),
        jax.ShapeDtypeStruct((sz.D, sz.NP), BF16),
        jax.ShapeDtypeStruct((sz.E, sz.D), BF16),
        jax.ShapeDtypeStruct((8, sz.CW), F32),
        jax.ShapeDtypeStruct((8, LANES), F32),
    ]


def bwd_call(sz, layer, last, spans, g, u, win, wout, proj, y, table):
    s = backward_scratch(sz)
    return pl.pallas_call(
        functools.partial(bwd_kernel, sz, layer, last, tuple(s)),
        out_shape=grad_shapes(sz),
        in_specs=[SM] + [VM] * 7,
        out_specs=[VM] * 5,
        scratch_shapes=list(s.values()),
        compiler_params=pltpu.CompilerParams(vmem_limit_bytes=ROOM),
    )(spans, g, u, win, wout, proj, y, table)


def own_small(pl_, acc, picks, outs, me):
    L, K = pl_.L, pl_.K
    for q in range(pl_.ndp):
        for n, count in enumerate((pl_.n_in, pl_.n_conv, pl_.n_out)):
            for l in range(L):
                at = 8 * (L * q + l)
                picks[0, n, at : at + 8, :count] = acc[l, :, q * count : (q + 1) * count]
    mine = rows_at(me, 8 * L)
    p_in, p_conv, p_out = picks[0, 0, mine, :], picks[0, 1, mine, :], picks[0, 2, mine, :]
    g_in, g_taps, g_bias, g_out = outs
    for l in range(L):
        r = 8 * l
        g_in[l : l + 1, :] = p_in[r : r + 1, : pl_.n_in]
        g_taps[l] = p_conv[r + 1 : r + 1 + K, : pl_.n_conv]
        g_bias[l : l + 1, :] = p_conv[r + 5 : r + 6, : pl_.n_conv]
        g_out[l : l + 1, :] = p_out[r + 6 : r + 7, : pl_.n_out]


def head_grads(pl_, acc, g_bias, g_decay, g_skip):
    sz = pl_.sz
    for l in range(pl_.L):
        part = acc[l, :, sz.CW :]
        g_bias[l : l + 1, :] = part[0:1, : 2 * sz.H]
        g_decay[l : l + 1, :] = part[1:2, : sz.H] + part[1:2, sz.H : 2 * sz.H]
        g_skip[l : l + 1, :] = part[2:3, : sz.H]


TICKS = ("proj", "post", "scan1", "scan3", "conv", "normed")


def backward_kernel(pl_, names, nbuf, *refs):
    sz, L = pl_.sz, pl_.L
    E = sz.E
    spans, resid_in, grad_out, resid2, table = refs[:5]
    weights = refs[5 : 5 + 2 * L]
    kept = refs[5 + 2 * L : 5 + 5 * L - 1]
    rest = refs[4 + 5 * L :]
    (resid, grad_in, g_in, g_gate, g_conv, g_step, g_taps, g_cbias, g_sbias, g_decay, g_skip,
     g_gout, g_out) = rest[:13]
    wi1, wo0, wo1, gi1, go1, proj, y, u1, u0, g1, gbuf, accs, load_sems, xsems = rest[13:27]
    sum_bufs, rest = rest[27 : 27 + 3 * L], rest[27 + 3 * L :]
    s = dict(zip(names, rest[: len(names)]))
    rest = rest[len(names) :]
    picks, whole = s["colb"], proj.at[0 : g_conv.shape[1], 0 : sz.NP - E]
    bufs, sems = rest[:nbuf], rest[nbuf:]
    ring = Ring(pl_.ndp)
    flags = run_flags(spans, ring.d)
    proj0, y0, u1_hbm, proj1, y1 = kept
    loads = {}
    for n, (name, src, dst) in enumerate((
        ("wo1", weights[3], wo1), ("proj1", proj1, proj), ("y1", y1, y), ("u1", u1_hbm, u1),
        ("wi1", weights[2], wi1), ("wo0", weights[1], wo0), ("proj0", proj0, proj), ("y0", y0, y),
        ("wi0", weights[0], gi1), ("g1", grad_out.at[ring.d], g1), ("u0", resid_in.at[ring.d], u0),
    )):
        loads[name] = pltpu.make_async_copy(src, dst, load_sems.at[n])
    for name in ("g1", "wo1", "proj1", "y1", "u1", "wi1", "wo0", "u0"):
        loads[name].start()
    ring.barrier(ring.flips())
    give_u = remote(resid2, resid.at[ring.d], xsems.at[0], xsems.at[1], ring.mate)
    keep_u = pltpu.make_async_copy(resid2, resid.at[ring.d], xsems.at[4])
    give_u.start()
    keep_u.start()
    give_g = remote(gbuf.at[0], gbuf.at[1], xsems.at[2], xsems.at[3], ring.mate)

    gwin, gwout = [wi1, gi1], [wo1, go1]
    groups, parts = [], []
    for l in range(L):
        part = lambda start, width: gwin[l].at[:, pl.ds(start, width)]
        groups += [gwout[l], part(0, E), part(E, sz.NP - E)]
        parts += pl_.rs_parts[l]
    scatter = Scatter(ring, groups, parts, bufs, sems)
    pump = Pump()
    seen = []
    sums = [AllSum(ring, accs.at[l], sum_bufs[3 * l : 3 * l + 3]) for l in range(L)]

    def launch(g):
        scatter.begin([g])
        pump.add("t", g, scatter.rounds(g))

    def tick(name):
        if name == "scan":
            name = "scan%d" % len(seen)
            seen.append(name)
        else:
            seen.clear()
        if name in TICKS:
            pump.tick()

    def results(l):
        scatter.result(3 * l, g_out.at[l])
        scatter.result(3 * l + 1, g_gate.at[l])
        scatter.result(3 * l + 2, whole)
        g_conv[l] = whole[:, : sz.CW]
        g_step[l] = whole[:, sz.CW : sz.CW + 2 * sz.H]

    def hook1(name):
        if name == "start":
            loads["g1"].wait()
        elif name == "w_out":
            loads["wo1"].wait()
        elif name == "proj":
            loads["proj1"].wait()
        elif name == "y":
            loads["y1"].wait()
        elif name == "post":
            loads["y0"].start()
        elif name == "g_out":
            launch(3)
            loads["u1"].wait()
        elif name == "g_gate":
            launch(4)
        elif name == "conv":
            loads["proj0"].start()
        elif name == "g_conv":
            launch(5)
        elif name == "w_in":
            loads["wi1"].wait()
        tick(name)

    def hook0(name):
        if name == "w_out":
            loads["wo0"].wait()
        elif name == "proj":
            loads["proj0"].wait()
        elif name == "y":
            loads["y0"].wait()
            pump.add("s", 1, sums[1].rounds())
        elif name == "g_out":
            launch(0)
            loads["u0"].wait()
        elif name == "g_gate":
            launch(1)
        elif name == "conv":
            pump.until(4, 5)
            scatter.drain([4, 5])
            loads["wi0"].start()
        elif name == "g_conv":
            launch(2)
        elif name == "w_in":
            loads["wi0"].wait()
        tick(name)

    for l, hook in ((1, hook1), (0, hook0)):
        small, head = accs.at[l, :, pl.ds(0, sz.CW)], accs.at[l, :, pl.ds(sz.CW, LANES)]
        if l == 1:
            backward_layer(sz, table_params(sz, table.at[l]), flags, g1, u1, wi1, wo1,
                           proj, y, u1, gi1, go1, small, head, s, hook)
        else:
            backward_layer(sz, table_params(sz, table.at[l]), flags, u1, u0, gi1, wo0,
                           proj, y, gbuf.at[0], wi1, wo1, small, head, s, hook)
    give_g.start()
    pump.add("s", 0, sums[0].rounds())
    pump.tick()
    results(1)
    give_u.wait()
    keep_u.wait()
    pump.rest()
    own_small(pl_, accs, picks, (g_in, g_taps, g_cbias, g_gout), ring.me)
    head_grads(pl_, accs, g_sbias, g_decay, g_skip)
    give_g.wait()
    grad_in[ring.d] = gbuf[0].astype(F32)
    grad_in[1 - ring.d] = gbuf[1].astype(F32)
    results(0)
    scatter.drain(range(4))


def backward_call(pl_, spans, resid_in, grad_out, weights, kept, table):
    sz, L, ndp = pl_.sz, pl_.L, pl_.ndp
    shape = lambda *s: jax.ShapeDtypeStruct(s, F32)
    r_in, r_out = sz.D // ndp, sz.E // ndp
    out = [
        jax.ShapeDtypeStruct((2, sz.T, sz.D), BF16),
        shape(2, sz.T, sz.D),
        shape(L, pl_.n_in),
        shape(L, r_in, sz.E),
        shape(L, r_in, sz.CW),
        shape(L, r_in, 2 * sz.H),
        shape(L, pl_.K, pl_.n_conv),
        shape(L, pl_.n_conv),
        shape(L, 2 * sz.H),
        shape(L, sz.H),
        shape(L, sz.H),
        shape(L, pl_.n_out),
        shape(L, r_out, sz.D),
    ]
    shapes, parts = [], []
    for l in range(L):
        shapes += list(zip(pl_.rs_rows, pl_.rs_widths))
        parts += pl_.rs_parts[l]
    bufs, sems = Scatter.scratch(ndp, shapes, parts)
    acc = (8, sz.CW + LANES)
    s = backward_scratch(sz)
    scratch = [
        pltpu.VMEM((sz.D, sz.NP), BF16),
        pltpu.VMEM((sz.E, sz.D), BF16),
        pltpu.VMEM((sz.E, sz.D), BF16),
        pltpu.VMEM((sz.D, sz.NP), BF16),
        pltpu.VMEM((sz.E, sz.D), BF16),
        pltpu.VMEM((sz.T, sz.NP), F32),
        pltpu.VMEM((sz.T, sz.E), F32),
        pltpu.VMEM((sz.T, sz.D), F32),
        pltpu.VMEM((sz.T, sz.D), BF16),
        pltpu.VMEM((sz.T, sz.D), BF16),
        pltpu.VMEM((2, sz.T, sz.D), BF16),
        pltpu.VMEM((L,) + acc, F32),
        pltpu.SemaphoreType.DMA((11,)),
        pltpu.SemaphoreType.DMA((5,)),
    ] + AllSum.scratch(ndp, acc) * L + list(s.values()) + bufs + sems
    resid2, kept = kept[-1], kept[:-1]
    made = pl.pallas_call(
        functools.partial(backward_kernel, pl_, tuple(s), len(bufs)),
        out_shape=out,
        in_specs=[SM, ANY, ANY, VM, VM] + [ANY] * (2 * L + len(kept)),
        out_specs=[ANY] + [VM] * (len(out) - 1),
        scratch_shapes=scratch,
        compiler_params=pltpu.CompilerParams(
            collective_id=2, has_side_effects=True, vmem_limit_bytes=ROOM
        ),
    )(spans, resid_in, grad_out, resid2, table, *weights, *kept)
    return hand_out(made)


def hand_out_kernel(count, *refs):
    sems = refs[-1]
    copies = [
        pltpu.make_async_copy(refs[n], refs[count + n], sems.at[n]) for n in range(count)
    ]
    for copy in copies:
        copy.start()
    for copy in copies:
        copy.wait()


def hand_out(made):
    return pl.pallas_call(
        functools.partial(hand_out_kernel, len(made)),
        out_shape=[jax.ShapeDtypeStruct(v.shape, v.dtype) for v in made],
        in_specs=[ANY] * len(made),
        out_specs=[VM] * len(made),
        scratch_shapes=[pltpu.SemaphoreType.DMA((len(made),))],
    )(*made)


def pad_lanes(v, width=LANES):
    return jnp.pad(v, [(0, 0)] * (v.ndim - 1) + [(0, width - v.shape[-1])])


def plain_gather(pl_, w_gate, w_conv, w_step, in_gain, conv_weight, conv_bias, out_gain, w_out,
                 step_bias, decay_log, skip_gain):
    sz = pl_.sz
    fetch = lambda v, axis=0: lax.all_gather(v, "dp", axis=axis, tiled=True)
    shard = jnp.concatenate([w_gate, w_conv, pad_lanes(w_step)], axis=2)
    full = []
    for l in range(pl_.L):
        full += [fetch(shard[l]), fetch(w_out[l])]
    wide = lambda v: pad_lanes(v.astype(F32), sz.CW)[:, None]
    decay = jnp.exp(decay_log)
    table = jnp.concatenate(
        [wide(fetch(in_gain, 1)), fetch(conv_weight, 2).astype(F32), wide(fetch(conv_bias, 1)),
         wide(fetch(out_gain, 1)), wide(step_bias), wide(jnp.concatenate([decay, decay], 1)),
         wide(jnp.repeat(skip_gain, HD, axis=1))], axis=1)
    return full + [jnp.pad(table, ((0, 0), (0, TABLE_ROWS - table.shape[1]), (0, 0)))]


def plain_scatter(pl_, u, g, grads, smalls, heads):
    sz, K = pl_.sz, pl_.K
    me = lax.axis_index("dp")
    summed = [
        lax.psum(lax.psum_scatter(v, "dp", scatter_dimension=0, tiled=True).astype(F32), "dir")
        for v in grads
    ]
    small, head = lax.psum((jnp.stack(smalls), jnp.stack(heads)), ("dir", "dp"))
    own = lambda v, n: lax.dynamic_slice_in_dim(v, me * n, n, axis=v.ndim - 1)
    win = jnp.stack(summed[0::2])
    return (
        lax.all_gather(u.astype(BF16), "dir"),
        lax.all_gather(g, "dir"),
        own(small[:, 0], pl_.n_in),
        win[:, :, : sz.E],
        win[:, :, sz.E : sz.STEP],
        win[:, :, sz.STEP : sz.STEP + 2 * sz.H],
        own(small[:, 1 : 1 + K], pl_.n_conv),
        own(small[:, 5], pl_.n_conv),
        head[:, 0, : 2 * sz.H],
        head[:, 1, : sz.H] + head[:, 1, sz.H : 2 * sz.H],
        head[:, 2, : sz.H],
        own(small[:, 6], pl_.n_out),
        jnp.stack(summed[1::2]),
    )


def shards(resid_in, grad_out, seq_spans, in_gain, w_gate_in, w_conv_in, w_step, conv_weight,
           conv_bias, step_bias, decay_log, skip_gain, out_gain, w_out):
    layers, taps = conv_weight.shape[:2]
    ndp = lax.axis_size("dp")
    sz = Sizes(resid_in.shape[2], w_gate_in.shape[2], w_conv_in.shape[2], skip_gain.shape[1])
    pl_ = Plan(layers, taps, ndp, sz, in_gain.shape[1], conv_weight.shape[2], out_gain.shape[1])
    whole_tiles = w_gate_in.shape[1] % 16 == 0 and w_out.shape[1] % 16 == 0
    weights = (w_gate_in, w_conv_in, w_step, in_gain, conv_weight, conv_bias, out_gain, w_out,
               step_bias, decay_log, skip_gain)
    u, saved = resid_in, []
    if whole_tiles:
        got = forward_call(pl_, seq_spans, resid_in, *weights)
        out = backward_call(pl_, seq_spans, resid_in, grad_out, got[: 2 * layers],
                            got[2 * layers : -1], got[-1])
        return tuple(out)
    got = plain_gather(pl_, *weights)
    win, wout, table = got[0:-1:2], got[1:-1:2], got[-1]
    for l in range(layers):
        proj, y, unext = fwd_call(sz, l, seq_spans, u, win[l], wout[l], table)
        saved.append((u, proj, y))
        u = unext
    g = grad_out
    grads, smalls, heads = [None] * (2 * layers), [None] * layers, [None] * layers
    for l in reversed(range(layers)):
        u_in, proj, y = saved[l]
        g, grads[2 * l], grads[2 * l + 1], smalls[l], heads[l] = bwd_call(
            sz, l, l == layers - 1, seq_spans, g, u_in, win[l], wout[l], proj, y, table)
    return tuple(plain_scatter(pl_, u, g, grads, smalls, heads))


def solution(mesh):
    rows, cols_, last = P(None, "dp", None), P(None, "dp"), P(None, None, "dp")
    placed = (rows, rows, cols_, cols_, rows, rows, rows, last, cols_, P(), P(), P(), cols_, rows)
    out = (rows, rows, cols_, rows, rows, rows, last, cols_, P(), P(), P(), cols_, rows)
    return jax.shard_map(shards, mesh=mesh, in_specs=placed, out_specs=out, check_vma=False)
```
